256 devices in a mesh: pipe: 16 (over y, x), dp: 16 (over z, core).
Axes of the slice: x: 4, y: 4, z: 8, core: 2. Of those that a mesh axis runs over, the one named last changes fastest.
Arguments:
- inputs: bfloat16 [16, 128, 8192], P('pipe', 'dp'), may hold values from -6 to 6
- cotangent: bfloat16 [16, 128, 8192], P('pipe', 'dp'), may hold values from -6 to 6
- norm_gain: float32 [16, 8192], P('pipe'), may hold values from 0.1 to 1.9
- w_value: bfloat16 [16, 64, 8192], P('pipe'), may hold values from -0.0625 to 0.0625
- w_out: bfloat16 [16, 64, 8192], P('pipe'), may hold values from -0.75 to 0.75
- value_down: bfloat16 [16, 16, 16, 8192], P('pipe', 'dp'), may hold values from -0.0625 to 0.0625
- value_up_factor: bfloat16 [16, 16, 16, 64], P('pipe', 'dp'), may hold values from -1.5 to 1.5
- out_down: bfloat16 [16, 16, 16, 64], P('pipe', 'dp'), may hold values from -0.75 to 0.75
- output_up_factor: bfloat16 [16, 16, 16, 8192], P('pipe', 'dp'), may hold values from -1.5 to 1.5
- block_tenant: int32 [16], replicated, may hold values from 0 to 15
- valid_tokens: int32 [16], replicated, may hold values from 1 to 128, 1536 in all
- tenant_slot: int32 [16], replicated, may hold values from 0 to 15, each once
Outputs:
- grad_value_down: bfloat16 [16, 16, 16, 8192], P('pipe', 'dp')
- grad_value_up: bfloat16 [16, 16, 16, 64], P('pipe', 'dp')
- grad_out_down: bfloat16 [16, 16, 16, 64], P('pipe', 'dp')
- grad_out_up: bfloat16 [16, 16, 16, 8192], P('pipe', 'dp')
The draws below stay inside these ranges and needn't reach their ends.
Inputs may be any that keep to these rules, and one draw needn't show every extreme that they name: `block_tenant`: tenant whose adapters serve all 128 tokens of a dp index. The first valid_tokens[i] block positions of dp index i are valid, the rest padding. A permutation: the adapters and gradients of tenant t sit at slot tenant_slot[t], stored on dp index tenant_slot[t].
All inputs are finite; a program needn't handle non-finite values.
Results may differ from the reference program's by a relative error of at most 0.034.
Values may be sent and summed in bfloat16 or wider, within the bound.
No kernel may reach another device: no remote copies, remote signals or barrier semaphores. Data moves between devices by JAX's collectives and lax.ppermute only.
A program may use at most 64 MiB of HBM per device.

```python
import math
import jax
import jax.numpy as jnp
import numpy as np
from jax import lax

D = 8192
HD = 64
RANK = 16
TOK = 8
LAYERS = 16
MICRO = 16
TENANTS = 16
TOKENS = 128
BLOCK = 128
N_DP = 16


def place_ends(drawn, rng, least, top_value):
    index_at = [jax.random.randint(jax.random.fold_in(rng, axis), (), 0, length) for axis, length in enumerate(drawn.shape)]
    main_axis = drawn.shape.index(max(drawn.shape))
    next_to = index_at[:main_axis] + [(index_at[main_axis] + 1) % drawn.shape[main_axis]] + index_at[main_axis + 1:]
    return drawn.at[tuple(index_at)].set(least).at[tuple(next_to)].set(top_value)


def block_scale(rng, shape, shards, least, high):
    gain, own = 1.0, jax.random.fold_in(rng, 6)
    for dim, parts in shards:
        heights = jnp.exp(jax.random.uniform(jax.random.fold_in(own, dim), (parts,), jnp.float32, least / len(shards), high / len(shards)))
        gain = gain * jnp.repeat(heights, shape[dim] // parts).reshape([-1 if axis == dim else 1 for axis in range(len(shape))])
    return gain


def cumulative_ranks(count, lean):
    weights = [(1 << 20) // math.isqrt(grade ** lean) + 1 for grade in range(1, count + 1)]
    width = 1 + sum(weights) // (1 << 30)
    return np.cumsum(np.array([max(1, weight // width) for weight in weights]))


def skewed_ids(key, extent, amount, skew):
    grid = cumulative_ranks(amount, skew)
    ticket = jax.random.randint(jax.random.fold_in(key, 1), extent, 0, int(grid[amount - 1]))
    standing = jnp.searchsorted(jnp.asarray(grid, jnp.int32), ticket, side="right")
    return jax.random.permutation(jax.random.fold_in(key, 2), amount)[standing].astype(jnp.int32)


def length_profile(count, total, bound, slope):
    portions = [(1 << 20) // math.isqrt(grade ** slope) + 1 for grade in range(2, count + 1)]
    rest, holding = total - bound - (count - 1), [1] * (count - 1)
    while rest > 0:
        movable = [i for i in range(count - 1) if holding[i] < bound]
        whole, left = sum([portions[i] for i in movable]), rest
        for i in movable:
            addition = min(bound - holding[i], max(1, left * portions[i] // whole), rest)
            holding[i] = holding[i] + addition
            rest = rest - addition
    return np.array([bound] + holding)


def uneven_parts(own_key, number_of, total, bound, slope):
    if number_of == 2:
        one = jax.random.randint(own_key, (), max(1, total - bound), min(bound, total - 1) + 1)
        return jnp.stack([one, total - one])
    lengths = jnp.asarray(length_profile(number_of, total, bound, slope), jnp.int32)
    couples = (number_of - 1) // 2
    donor, taker = lengths[1:1 + 2 * couples:2], lengths[2:2 + 2 * couples:2]
    slack = jnp.minimum(donor - 1, bound - taker)
    shifted = jax.random.randint(jax.random.fold_in(own_key, 1), (couples,), 0, 1 << 20) % (slack + 1)
    lengths = lengths.at[1:1 + 2 * couples:2].set(donor - shifted).at[2:2 + 2 * couples:2].set(taker + shifted)
    return lengths[jax.random.permutation(jax.random.fold_in(own_key, 2), number_of)]


def gaussian(key, extent, spread, limit, pieces=(), held_as=jnp.bfloat16):
    array = jax.random.normal(key, extent, jnp.float32) * spread
    if len(pieces) > 0:
        array = block_scale(key, extent, pieces, -0.22, 0.18) * array
    return jnp.clip(array, min=-limit, max=limit).astype(held_as)


def setup_inputs(seed: int = 0) -> dict:
    arg_keys = jax.random.split(jax.random.key(seed), 13)
    inputs = gaussian(arg_keys[0], (MICRO, TOKENS, D), 1.0, 6.0, ((0, 16), (1, 16)))
    cotangent = gaussian(arg_keys[1], (MICRO, TOKENS, D), 1.0, 6.0, ((0, 16), (1, 16)))
    norm_gain = jnp.clip(1.0 + 0.18 * jax.random.normal(arg_keys[2], (LAYERS, D), jnp.float32), 0.1, 1.9)
    w_value = gaussian(arg_keys[3], (LAYERS, HD, D), D ** -0.5, 0.0625, ((0, 16),))
    w_out = gaussian(arg_keys[4], (LAYERS, HD, D), HD ** -0.5, 0.75, ((0, 16),))
    value_down = gaussian(arg_keys[5], (LAYERS, TENANTS, RANK, D), D ** -0.5, 0.0625, ((0, 16), (1, 16)))
    value_up_factor = gaussian(arg_keys[6], (LAYERS, TENANTS, RANK, HD), RANK ** -0.5, 1.5, ((0, 16), (1, 16)))
    out_down = gaussian(arg_keys[7], (LAYERS, TENANTS, RANK, HD), HD ** -0.5, 0.75, ((0, 16), (1, 16)))
    output_up_factor = gaussian(arg_keys[8], (LAYERS, TENANTS, RANK, D), RANK ** -0.5, 1.5, ((0, 16), (1, 16)))
    block_tenant = place_ends(skewed_ids(arg_keys[9], (N_DP,), TENANTS, 2), jax.random.fold_in(arg_keys[9], 3), 0, TENANTS - 1).astype(jnp.int32)
    valid_tokens = uneven_parts(arg_keys[10], N_DP, N_DP * BLOCK * 3 // 4, BLOCK, 2).astype(jnp.int32)
    tenant_slot = jax.random.permutation(arg_keys[11], TENANTS).astype(jnp.int32)
    return {"inputs": inputs, "cotangent": cotangent, "norm_gain": norm_gain, "w_value": w_value, "w_out": w_out, "value_down": value_down, "value_up_factor": value_up_factor, "out_down": out_down, "output_up_factor": output_up_factor, "block_tenant": block_tenant, "valid_tokens": valid_tokens, "tenant_slot": tenant_slot}


adapter_scale = 2.0
norm_eps = 1e-05

def normalize(token_rows, gain_row):
    wide_rows = token_rows.astype(jnp.float32)
    inverse = lax.rsqrt(lax.optimization_barrier(jnp.mean(wide_rows * wide_rows, axis=-1, keepdims=True)) + norm_eps)
    return ((wide_rows * inverse * gain_row).astype(jnp.bfloat16), inverse)

def contract_trailing(left, right):
    return lax.dot_general(left, right, (((1,), (1,)), ((), ())), preferred_element_type=jnp.float32)

def contract_leading(left, right):
    return lax.dot_general(left, right, (((0,), (0,)), ((), ())), preferred_element_type=jnp.float32)

def section_parts(token_rows, gain_row, value_weight, tenant_adapters):
    value_down, value_up_factor, out_down, output_up_factor = tenant_adapters
    normalized_rows, inverse = normalize(token_rows, gain_row)
    lowrank_product = contract_trailing(normalized_rows, value_down).astype(jnp.bfloat16)
    value_blend = contract_trailing(normalized_rows, value_weight)
    value_blend = value_blend + adapter_scale * jnp.dot(lowrank_product, value_up_factor, preferred_element_type=jnp.float32)
    value_row_block = value_blend.astype(jnp.bfloat16)
    sidepath_rank = contract_trailing(value_row_block, out_down).astype(jnp.bfloat16)
    return (normalized_rows, inverse, lowrank_product, value_row_block, sidepath_rank)

def section_output(token_rows, layer_pieces, out_weight, tenant_adapters):
    blended_rows = token_rows.astype(jnp.float32) + jnp.dot(layer_pieces[3], out_weight, preferred_element_type=jnp.float32)
    blended_rows = blended_rows + adapter_scale * jnp.dot(layer_pieces[4], tenant_adapters[3], preferred_element_type=jnp.float32)
    return blended_rows.astype(jnp.bfloat16)

def section_backward(token_rows, input_gradient, layer_pieces, gain_row, value_weight, out_weight, tenant_adapters):
    value_down, value_up_factor, out_down, output_up_factor = tenant_adapters
    normalized_rows, inverse, lowrank_product, value_row_block, sidepath_rank = layer_pieces
    sidepath_gradient = (adapter_scale * contract_trailing(input_gradient, output_up_factor)).astype(jnp.bfloat16)
    value_gradient = contract_trailing(input_gradient, out_weight)
    value_gradient = (value_gradient + jnp.dot(sidepath_gradient, out_down, preferred_element_type=jnp.float32)).astype(jnp.bfloat16)
    lowrank_gradient = (adapter_scale * contract_trailing(value_gradient, value_up_factor)).astype(jnp.bfloat16)
    grad_normed = jnp.dot(value_gradient, value_weight, preferred_element_type=jnp.float32) + jnp.dot(lowrank_gradient, value_down, preferred_element_type=jnp.float32)
    scaled = grad_normed * gain_row
    wide_rows = token_rows.astype(jnp.float32)
    correction = lax.optimization_barrier(jnp.mean(scaled * wide_rows, axis=-1, keepdims=True))
    grad_rows = inverse * scaled - wide_rows * (inverse * inverse * inverse) * correction
    grad_out = (input_gradient.astype(jnp.float32) + grad_rows).astype(jnp.bfloat16)
    gradient_pieces = (contract_leading(lowrank_gradient, normalized_rows), adapter_scale * contract_leading(lowrank_product, value_gradient), contract_leading(sidepath_gradient, value_row_block), adapter_scale * contract_leading(sidepath_rank, input_gradient))
    return (grad_out, gradient_pieces)

def reference(inputs, cotangent, norm_gain, w_value, w_out, value_down, value_up_factor, out_down, output_up_factor, block_tenant, valid_tokens, tenant_slot):
    tenant_ids = jnp.arange(TENANTS, dtype=jnp.int32)
    tenant_hot = block_tenant[:, None] == tenant_ids[None, :]
    slot_of = lax.optimization_barrier(jnp.sum(jnp.where(tenant_hot, tenant_slot[None, :], 0), axis=1)).astype(jnp.int32)
    slot_hot = (slot_of[:, None] == tenant_ids[None, :]).astype(jnp.float32)
    same_tenant = block_tenant[:, None] == block_tenant[None, :]
    tenant_tokens = lax.optimization_barrier(jnp.sum(jnp.where(same_tenant, valid_tokens[None, :], 0), axis=1)).astype(jnp.float32)
    adapters_used = tuple((jnp.take(adapter_table, slot_of, axis=1) for adapter_table in (value_down, value_up_factor, out_down, output_up_factor)))
    parts_all = jax.vmap(section_parts, in_axes=(0, None, None, 0))
    output_all = jax.vmap(section_output, in_axes=(0, 0, None, 0))
    backward_all = jax.vmap(section_backward, in_axes=(0, 0, 0, None, None, None, 0))

    def micro_step(carry, micro_index):
        token_rows = lax.dynamic_index_in_dim(inputs, micro_index, 0, keepdims=False).reshape(N_DP, TOK, D)
        stored = []
        for layer_index in range(LAYERS):
            tenant_adapters = tuple((adapter_table[layer_index] for adapter_table in adapters_used))
            layer_pieces = parts_all(token_rows, norm_gain[layer_index], w_value[layer_index], tenant_adapters)
            stored.append((token_rows, layer_pieces))
            token_rows = output_all(token_rows, layer_pieces, w_out[layer_index], tenant_adapters)
        position = micro_index * TOK + jnp.arange(TOK, dtype=jnp.int32)
        weight = jnp.where(position[None, :] < valid_tokens[:, None], 1.0, 0.0).astype(jnp.float32) / tenant_tokens[:, None]
        seed_rows = lax.dynamic_index_in_dim(cotangent, micro_index, 0, keepdims=False).reshape(N_DP, TOK, D)
        grad_rows = (seed_rows.astype(jnp.float32) * weight[:, :, None]).astype(jnp.bfloat16)
        layer_terms = [None] * LAYERS
        for layer_index in reversed(range(LAYERS)):
            tenant_adapters = tuple((adapter_table[layer_index] for adapter_table in adapters_used))
            grad_rows, gradient_pieces = backward_all(stored[layer_index][0], grad_rows, stored[layer_index][1], norm_gain[layer_index], w_value[layer_index], w_out[layer_index], tenant_adapters)
            layer_terms[layer_index] = gradient_pieces
        stacked = tuple((jnp.stack([layer_terms[layer_index][term_index] for layer_index in range(LAYERS)]) for term_index in range(4)))
        return (tuple((running + addend for running, addend in zip(carry, stacked))), None)
    start = tuple((jnp.zeros((LAYERS, N_DP, RANK, column_count), jnp.float32) for column_count in (D, HD, HD, D)))
    totals, _ = lax.scan(micro_step, start, jnp.arange(MICRO, dtype=jnp.int32))

    def owner_sum(per_member):
        return jnp.einsum('ns,nrw->srw', slot_hot, per_member, precision=lax.Precision.HIGHEST).astype(jnp.bfloat16)
    return (lax.map(owner_sum, totals[0]), lax.map(owner_sum, totals[1]), lax.map(owner_sum, totals[2]), lax.map(owner_sum, totals[3]))
```

```python
import functools

import jax
import jax.numpy as jnp
from jax import lax
from jax.experimental import pallas as pl
from jax.experimental.pallas import tpu as pltpu
from jax.sharding import PartitionSpec as P

adapter_scale = 2.0
norm_eps = 1e-05
block = 256
vmem_bytes = 56 * 1024 * 1024


def mm(left, right):
    return lax.dot_general(
        left, right, (((1,), (0,)), ((), ())), preferred_element_type=jnp.float32
    )


def mm_nt(left, right):
    return lax.dot_general(
        left, right, (((1,), (1,)), ((), ())), preferred_element_type=jnp.float32
    )


def mm_tn(left, right):
    return lax.dot_general(
        left, right, (((0,), (0,)), ((), ())), preferred_element_type=jnp.float32
    )


def layer_mask(rows, columns, hd, compare):
    row_layer = lax.broadcasted_iota(jnp.int32, (rows, columns), 0) // hd
    column_layer = lax.broadcasted_iota(jnp.int32, (rows, columns), 1) // hd
    return compare(row_layer, column_layer)


def gram_kernel(sizes, w_ref, x_ref, s_ref, q_ref, u_ref, v_ref, out_ref):
    layers, hd, rank, tokens, cols = sizes
    for l in range(layers):
        small = q_ref[l, :, 2 * cols : 2 * cols + 2 * hd]
        delta_v = mm_tn(small[:, :hd], q_ref[l, :, :cols])
        delta_u = mm_tn(small[:, hd:], q_ref[l, :, cols : 2 * cols])
        at = pl.ds(l * hd, hd)
        v_ref[at, :] = (w_ref[l, :hd, :].astype(jnp.float32) + adapter_scale * delta_v).astype(
            jnp.bfloat16
        )
        u_ref[at, :] = (
            w_ref[l, hd : 2 * hd, :].astype(jnp.float32) + adapter_scale * delta_u
        ).astype(jnp.bfloat16)
    width = layers * hd
    base = 3 * tokens
    below = layer_mask(block, block, hd, lambda r, c: r < c)
    for bj in range(width // block):
        at_col = pl.ds(bj * block, block)
        u_col, v_col = u_ref[at_col, :], v_ref[at_col, :]
        out_ref[:tokens, at_col] = mm_nt(x_ref[...], v_col).astype(jnp.bfloat16)
        out_ref[tokens : 2 * tokens, at_col] = mm_nt(x_ref[...], u_col).astype(jnp.bfloat16)
        out_ref[2 * tokens : 3 * tokens, at_col] = mm_nt(s_ref[...], u_col).astype(jnp.bfloat16)
        for bi in range(width // block):
            rows = u_ref[pl.ds(bi * block, block), :]
            if bi < bj:
                part = mm_nt(rows, v_col)
            elif bi > bj:
                part = mm_nt(rows, u_col)
            else:
                part = jnp.where(below, mm_nt(rows, v_col), mm_nt(rows, u_col))
            out_ref[pl.ds(base + bi * block, block), at_col] = part.astype(jnp.bfloat16)


def half(pair, l):
    hd = pair.shape[1] // 2
    return pair[:, hd:] if l % 2 else pair[:, :hd]


def solve_kernel(
    sizes,
    features,
    k_ref,
    n_ref,
    x_ref,
    s_ref,
    u_ref,
    v_ref,
    q_ref,
    out_ref,
    c_ref,
    d_ref,
    ec_ref,
    a_ref,
    bp_ref,
    inv_ref,
):
    layers, hd, rank, tokens, cols = sizes
    width = layers * hd
    base = 3 * tokens
    c_ref[...] = jnp.zeros_like(c_ref)
    d_ref[...] = jnp.zeros_like(d_ref)
    ec_ref[...] = jnp.zeros_like(ec_ref)

    def pair_of(l):
        return pl.ds(2 * hd * (l // 2), 2 * hd)

    def upto(l):
        return 2 * hd * ((l + 1) // 2)

    square = n_ref[...]
    for l in range(layers):
        pair = pair_of(l)
        rows_l = pl.ds(base + l * hd, hd)
        a = half(k_ref[:tokens, pair], l).astype(jnp.float32)
        b = half(k_ref[tokens : 2 * tokens, pair], l).astype(jnp.float32)
        if l:
            w = upto(l)
            known = c_ref[:, :w]
            a = a + half(mm(known, k_ref[base : base + w, pair]), l)
            b = b + mm_nt(known, k_ref[rows_l, :w])
        inverse = lax.rsqrt(jnp.maximum(square, 0.0) / features + norm_eps)
        c = (inverse * a).astype(jnp.bfloat16)
        wide = c.astype(jnp.float32)
        after = b + half(mm(c, k_ref[rows_l, pair]), l)
        square = square + jnp.sum(wide * (b + after), axis=1, keepdims=True)
        c_ref[:, l * hd : (l + 1) * hd] = c
        a_ref[l] = a
        bp_ref[l] = after
        inv_ref[l] = inverse

    pull = jnp.zeros_like(square)
    for l in range(layers - 1, -1, -1):
        pair = pair_of(l)
        rows_l = pl.ds(base + l * hd, hd)
        p = half(k_ref[2 * tokens : 3 * tokens, pair], l).astype(jnp.float32) - pull * bp_ref[l]
        if l < layers - 1:
            w = upto(l)
            p = p + mm_nt(d_ref[:, w:], k_ref[rows_l, w:])
            p = p - half(mm(ec_ref[:, w:], k_ref[base + w : base + width, pair]), l)
        inverse = inv_ref[l]
        d_ref[:, l * hd : (l + 1) * hd] = (inverse * p).astype(jnp.bfloat16)
        c = c_ref[:, l * hd : (l + 1) * hd].astype(jnp.float32)
        ec_ref[:, l * hd : (l + 1) * hd] = (pull * c).astype(jnp.bfloat16)
        correction = jnp.sum(p * a_ref[l], axis=1, keepdims=True) / features
        pull = pull + inverse * inverse * inverse * correction

    below = layer_mask(block, block, hd, lambda r, c: r > c)
    upto_diag = layer_mask(block, block, hd, lambda r, c: r >= c)
    blocks = width // block
    for bl in range(blocks):
        mine = pl.ds(bl * block, block)
        c_t = c_ref[:, mine].T
        d_t = d_ref[:, mine].T
        ec_t = ec_ref[:, mine].T
        y = mm(d_t, x_ref[...])
        z = mm(c_t, s_ref[...]) - mm(ec_t, x_ref[...])
        for bk in range(blocks):
            other = pl.ds(bk * block, block)
            u_k = u_ref[other, :]
            if bk <= bl:
                m = mm(d_t, c_ref[:, other])
                if bk == bl:
                    m = jnp.where(below, m, 0.0)
                y = y + mm(m.astype(jnp.bfloat16), u_k)
            if bk >= bl:
                m = mm(c_t, d_ref[:, other])
                if bk == bl:
                    m = jnp.where(upto_diag, 0.0, m)
                z = z + mm(m.astype(jnp.bfloat16), v_ref[other, :])
            if bk < bl:
                m = mm(ec_t, c_ref[:, other])
            elif bk > bl:
                m = mm(c_t, ec_ref[:, other])
            else:
                m = jnp.where(upto_diag, mm(ec_t, c_ref[:, other]), mm(c_t, ec_ref[:, other]))
            z = z - mm(m.astype(jnp.bfloat16), u_k)
        y = y.astype(jnp.bfloat16)
        z = z.astype(jnp.bfloat16)
        for j in range(block // hd):
            l = bl * (block // hd) + j
            y_l, z_l = y[j * hd : (j + 1) * hd], z[j * hd : (j + 1) * hd]
            small = q_ref[l, :, 2 * cols : 2 * cols + 2 * hd]
            out_ref[l, :, :cols] = (adapter_scale * mm(small[:, :hd], y_l)).astype(jnp.bfloat16)
            out_ref[l, :, cols : 2 * cols] = (adapter_scale * mm(small[:, hd:], z_l)).astype(
                jnp.bfloat16
            )
            tail = jnp.concatenate(
                [mm_nt(q_ref[l, :, :cols], y_l), mm_nt(q_ref[l, :, cols : 2 * cols], z_l)], axis=1
            )
            out_ref[l, :, 2 * cols :] = (adapter_scale * tail).astype(jnp.bfloat16)


def params():
    return pltpu.CompilerParams(vmem_limit_bytes=vmem_bytes)


def in_vmem(count):
    return [pl.BlockSpec(memory_space=pltpu.VMEM)] * count


def gram(sizes, w, x, s, q):
    layers, hd, rank, tokens, cols = sizes
    width = layers * hd
    return pl.pallas_call(
        functools.partial(gram_kernel, sizes),
        out_shape=(
            jax.ShapeDtypeStruct((width, cols), jnp.bfloat16),
            jax.ShapeDtypeStruct((width, cols), jnp.bfloat16),
            jax.ShapeDtypeStruct((3 * tokens + width, width), jnp.bfloat16),
        ),
        in_specs=in_vmem(4),
        out_specs=tuple(in_vmem(3)),
        compiler_params=params(),
    )(w, x, s, q)


def solve(sizes, features, k, squares, x, s, u, v, q):
    layers, hd, rank, tokens, cols = sizes
    width = layers * hd
    return pl.pallas_call(
        functools.partial(solve_kernel, sizes, features),
        out_shape=jax.ShapeDtypeStruct(q.shape, jnp.bfloat16),
        in_specs=in_vmem(7),
        out_specs=in_vmem(1)[0],
        scratch_shapes=[
            pltpu.VMEM((tokens, width), jnp.bfloat16),
            pltpu.VMEM((tokens, width), jnp.bfloat16),
            pltpu.VMEM((tokens, width), jnp.bfloat16),
            pltpu.VMEM((layers, tokens, hd), jnp.float32),
            pltpu.VMEM((layers, tokens, hd), jnp.float32),
            pltpu.VMEM((layers, tokens, 1), jnp.float32),
        ],
        compiler_params=params(),
    )(k, squares, x, s, u, v, q)


def swap(value, axis):
    return lax.all_to_all(value, axis, split_axis=0, concat_axis=0, tiled=True)


def by_columns(rows, parts):
    return rows.reshape(rows.shape[0], parts, -1).transpose(1, 0, 2)


def pick(chooser, parts):
    flat = parts.reshape(parts.shape[0], -1)
    return mm(chooser, flat).astype(jnp.bfloat16).reshape((chooser.shape[0],) + parts.shape[1:])


def body(
    inputs,
    cotangent,
    norm_gain,
    w_value,
    w_out,
    value_down,
    value_up_factor,
    out_down,
    output_up_factor,
    block_tenant,
    valid_tokens,
    tenant_slot,
):
    section = lax.axis_index("pipe")
    sections = lax.axis_size("pipe")
    member = lax.axis_index("dp")
    members = lax.axis_size("dp")
    rows, features = inputs.shape[1], inputs.shape[2]
    hd, rank = w_value.shape[1], value_down.shape[2]
    cols = features // sections
    tokens = rows * sections
    sizes = (sections, hd, rank, tokens, cols)

    ids = jnp.arange(tenant_slot.shape[0], dtype=jnp.int32)
    tenant_hot = block_tenant[:, None] == ids[None, :]
    slot_of = jnp.sum(jnp.where(tenant_hot, tenant_slot[None, :], 0), axis=1)
    slot_hot = (slot_of[:, None] == ids[None, :]).astype(jnp.bfloat16)
    member_hot = jnp.arange(members, dtype=jnp.int32) == member
    own_tenant = jnp.sum(jnp.where(member_hot, block_tenant, 0))
    own_valid = jnp.sum(jnp.where(member_hot, valid_tokens, 0))
    tenant_tokens = jnp.sum(jnp.where(block_tenant == own_tenant, valid_tokens, 0)).astype(
        jnp.float32
    )

    gain = norm_gain[0]
    value_down_gained = (value_down[0, 0].astype(jnp.float32) * gain).astype(jnp.bfloat16)
    w_value_gained = (w_value[0].astype(jnp.float32) * gain).astype(jnp.bfloat16)
    small = jnp.concatenate([value_up_factor[0, 0], out_down[0, 0]], axis=1)
    stored = jnp.concatenate(
        [
            by_columns(value_down_gained, members),
            by_columns(output_up_factor[0, 0], members),
            jnp.broadcast_to(small[None], (members,) + small.shape),
        ],
        axis=2,
    )
    adapters = swap(pick(slot_hot, swap(stored, "dp")), "dp")

    position = section * rows + jnp.arange(rows, dtype=jnp.int32)
    weight = jnp.where(position < own_valid, 1.0, 0.0).astype(jnp.float32) / tenant_tokens
    seeded = (cotangent[0].astype(jnp.float32) * weight[:, None]).astype(jnp.bfloat16)
    own_rows = inputs[0].astype(jnp.float32)
    squares = lax.all_gather(jnp.sum(own_rows * own_rows, axis=1), "pipe", axis=0, tiled=True)
    packed = jnp.concatenate(
        [
            by_columns(w_value_gained, sections),
            by_columns(w_out[0], sections),
            by_columns(inputs[0], sections),
            by_columns(seeded, sections),
        ],
        axis=1,
    )
    packed = swap(packed, "pipe")
    adapters = swap(adapters, "pipe")
    x = packed[:, 2 * hd : 2 * hd + rows].reshape(tokens, cols)
    s = packed[:, 2 * hd + rows :].reshape(tokens, cols)

    u, v, partial = gram(sizes, packed, x, s, adapters)
    width = partial.shape[1]
    shares = swap(partial.reshape(sections, -1, width), "pipe")
    share = jnp.sum(shares.astype(jnp.float32), axis=0).astype(jnp.bfloat16)
    whole = swap(jnp.broadcast_to(share[None], shares.shape), "pipe").reshape(partial.shape)

    grads = solve(sizes, features, whole, squares[:, None], x, s, u, v, adapters)

    by_layer = swap(grads, "dp")
    summed = pick(slot_hot.T, by_layer)
    owned = swap(swap(summed, "dp"), "pipe")
    grad_value_down = owned[:, :, :cols].transpose(1, 0, 2).reshape(rank, features)
    grad_value_down = (grad_value_down.astype(jnp.float32) * gain).astype(jnp.bfloat16)
    grad_out_up = owned[:, :, cols : 2 * cols].transpose(1, 0, 2).reshape(rank, features)
    tail = jnp.sum(owned[:, :, 2 * cols :].astype(jnp.float32), axis=0).astype(jnp.bfloat16)
    return (
        grad_value_down[None, None],
        tail[None, None, :, :hd],
        tail[None, None, :, hd:],
        grad_out_up[None, None],
    )


def solution(mesh):
    return jax.shard_map(
        body,
        mesh=mesh,
        in_specs=(
            P("pipe", "dp", None),
            P("pipe", "dp", None),
            P("pipe", None),
            P("pipe", None, None),
            P("pipe", None, None),
            P("pipe", "dp", None, None),
            P("pipe", "dp", None, None),
            P("pipe", "dp", None, None),
            P("pipe", "dp", None, None),
            P(),
            P(),
            P(),
        ),
        out_specs=(
            P("pipe", "dp", None, None),
            P("pipe", "dp", None, None),
            P("pipe", "dp", None, None),
            P("pipe", "dp", None, None),
        ),
        check_vma=False,
    )
```

```python
import functools

import jax
import jax.numpy as jnp
from jax import lax
from jax.experimental import pallas as pl
from jax.experimental.pallas import tpu as pltpu
from jax.sharding import PartitionSpec as P

adapter_scale = 2.0
norm_eps = 1e-05
block = 256
vmem_bytes = 56 * 1024 * 1024


def mm(left, right):
    return lax.dot_general(
        left, right, (((1,), (0,)), ((), ())), preferred_element_type=jnp.float32
    )


def mm_nt(left, right):
    return lax.dot_general(
        left, right, (((1,), (1,)), ((), ())), preferred_element_type=jnp.float32
    )


def mm_tn(left, right):
    return lax.dot_general(
        left, right, (((0,), (0,)), ((), ())), preferred_element_type=jnp.float32
    )


def layer_mask(rows, columns, hd, compare):
    row_layer = lax.broadcasted_iota(jnp.int32, (rows, columns), 0) // hd
    column_layer = lax.broadcasted_iota(jnp.int32, (rows, columns), 1) // hd
    return compare(row_layer, column_layer)


def spread_kernel(
    sizes, p_ref, wv_ref, wo_ref, gain_ref, x_ref, cot_ref, weight_ref, *out_refs
):
    layers, hd, rank, tokens, cols = sizes
    rows = tokens // layers
    section = p_ref[0]
    for step, out_ref in enumerate(out_refs):
        at = pl.ds(pl.multiple_of(lax.rem(section + step, layers) * cols, cols), cols)
        out_ref[:hd, :] = (wv_ref[:, at].astype(jnp.float32) * gain_ref[:, at]).astype(jnp.bfloat16)
        out_ref[hd : 2 * hd, :] = wo_ref[:, at]
        seeded = cot_ref[:, at].astype(jnp.float32) * weight_ref[...]
        out_ref[2 * hd :, :] = jnp.concatenate(
            [x_ref[:, at].astype(jnp.float32), seeded], axis=0
        ).astype(jnp.bfloat16)


def store_kernel(sizes, vd_ref, ou_ref, gain_ref, vu_ref, od_ref, out_ref):
    layers, hd, rank, tokens, cols = sizes
    small = jnp.concatenate([vu_ref[...], od_ref[...]], axis=1)
    for k in range(out_ref.shape[0]):
        at = pl.ds(k * cols, cols)
        out_ref[k, :, :cols] = (vd_ref[:, at].astype(jnp.float32) * gain_ref[:, at]).astype(
            jnp.bfloat16
        )
        out_ref[k, :, cols : 2 * cols] = ou_ref[:, at]
        out_ref[k, :, 2 * cols :] = small


def gram_kernel(sizes, p_ref, *refs):
    layers, hd, rank, tokens, cols = sizes
    rows = tokens // layers
    w_refs = refs[:layers]
    q_ref, u_ref, v_ref, x_ref, s_ref, out_ref, x_wide, s_wide = refs[layers:]
    section = p_ref[0]
    for step, w_ref in enumerate(w_refs):
        l = lax.rem(section + layers - step, layers)
        q_l = q_ref[l]
        small = q_l[:, 2 * cols : 2 * cols + 2 * hd]
        delta_v = mm_tn(small[:, :hd], q_l[:, :cols])
        delta_u = mm_tn(small[:, hd:], q_l[:, cols : 2 * cols])
        at = pl.ds(pl.multiple_of(l * hd, hd), hd)
        v_ref[at, :] = (w_ref[:hd, :].astype(jnp.float32) + adapter_scale * delta_v).astype(
            jnp.bfloat16
        )
        u_ref[at, :] = (w_ref[hd : 2 * hd, :].astype(jnp.float32) + adapter_scale * delta_u).astype(
            jnp.bfloat16
        )
        both = w_ref[2 * hd :, :].astype(jnp.float32)
        at = pl.ds(pl.multiple_of(l * rows, rows), rows)
        x_wide[at, :] = both[:rows]
        s_wide[at, :] = both[rows:]
    x_ref[...] = x_wide[...].astype(jnp.bfloat16)
    s_ref[...] = s_wide[...].astype(jnp.bfloat16)
    width = layers * hd
    base = 3 * tokens
    below = layer_mask(block, block, hd, lambda r, c: r < c)
    for bj in range(width // block):
        at_col = pl.ds(bj * block, block)
        u_col, v_col = u_ref[at_col, :], v_ref[at_col, :]
        out_ref[:tokens, at_col] = mm_nt(x_ref[...], v_col).astype(jnp.bfloat16)
        out_ref[tokens : 2 * tokens, at_col] = mm_nt(x_ref[...], u_col).astype(jnp.bfloat16)
        out_ref[2 * tokens : 3 * tokens, at_col] = mm_nt(s_ref[...], u_col).astype(jnp.bfloat16)
        for bi in range(width // block):
            rows = u_ref[pl.ds(bi * block, block), :]
            if bi < bj:
                part = mm_nt(rows, v_col)
            elif bi > bj:
                part = mm_nt(rows, u_col)
            else:
                part = jnp.where(below, mm_nt(rows, v_col), mm_nt(rows, u_col))
            out_ref[pl.ds(base + bi * block, block), at_col] = part.astype(jnp.bfloat16)
    wide = x_wide[...]
    wide = wide * wide
    folded = wide[:, : 2 * hd]
    for at in range(2 * hd, cols, 2 * hd):
        folded = folded + wide[:, at : at + 2 * hd]
    out_ref[tokens : 2 * tokens, width - hd :] = (folded[:, :hd] + folded[:, hd:]).astype(
        jnp.bfloat16
    )


def half(pair, l):
    hd = pair.shape[1] // 2
    return pair[:, hd:] if l % 2 else pair[:, :hd]


def solve_kernel(
    sizes,
    features,
    k_ref,
    x_ref,
    s_ref,
    u_ref,
    v_ref,
    q_ref,
    out_ref,
    c_ref,
    d_ref,
    ec_ref,
    a_ref,
    bp_ref,
    inv_ref,
):
    layers, hd, rank, tokens, cols = sizes
    width = layers * hd
    base = 3 * tokens
    c_ref[...] = jnp.zeros_like(c_ref)
    d_ref[...] = jnp.zeros_like(d_ref)
    ec_ref[...] = jnp.zeros_like(ec_ref)

    def pair_of(l):
        return pl.ds(2 * hd * (l // 2), 2 * hd)

    def upto(l):
        return 2 * hd * ((l + 1) // 2)

    folded = k_ref[tokens : 2 * tokens, width - 2 * hd :].astype(jnp.float32)[:, hd:]
    square = jnp.sum(folded, axis=1, keepdims=True)
    for l in range(layers):
        pair = pair_of(l)
        rows_l = pl.ds(base + l * hd, hd)
        a = half(k_ref[:tokens, pair], l).astype(jnp.float32)
        if l:
            w = upto(l)
            known = c_ref[:, :w]
            a = a + half(mm(known, k_ref[base : base + w, pair]), l)
        inverse = lax.rsqrt(jnp.maximum(square, 0.0) / features + norm_eps)
        c = (inverse * a).astype(jnp.bfloat16)
        c_ref[:, l * hd : (l + 1) * hd] = c
        a_ref[l] = a
        inv_ref[l] = inverse
        if l == layers - 1:
            break
        b = half(k_ref[tokens : 2 * tokens, pair], l).astype(jnp.float32)
        if l:
            b = b + mm_nt(known, k_ref[rows_l, :w])
        wide = c.astype(jnp.float32)
        after = b + half(mm(c, k_ref[rows_l, pair]), l)
        square = square + jnp.sum(wide * (b + after), axis=1, keepdims=True)
        bp_ref[l] = after

    pull = jnp.zeros((tokens, 1), jnp.float32)
    for l in range(layers - 1, -1, -1):
        pair = pair_of(l)
        rows_l = pl.ds(base + l * hd, hd)
        p = half(k_ref[2 * tokens : 3 * tokens, pair], l).astype(jnp.float32)
        if l < layers - 1:
            w = upto(l)
            p = p - pull * bp_ref[l]
            p = p + mm_nt(d_ref[:, w:], k_ref[rows_l, w:])
            p = p - half(mm(ec_ref[:, w:], k_ref[base + w : base + width, pair]), l)
        inverse = inv_ref[l]
        d_ref[:, l * hd : (l + 1) * hd] = (inverse * p).astype(jnp.bfloat16)
        c = c_ref[:, l * hd : (l + 1) * hd].astype(jnp.float32)
        ec_ref[:, l * hd : (l + 1) * hd] = (pull * c).astype(jnp.bfloat16)
        correction = jnp.sum(p * a_ref[l], axis=1, keepdims=True) / features
        pull = pull + inverse * inverse * inverse * correction

    below = layer_mask(block, block, hd, lambda r, c: r > c)
    upto_diag = layer_mask(block, block, hd, lambda r, c: r >= c)
    blocks = width // block
    for bl in range(blocks):
        mine = pl.ds(bl * block, block)
        c_t = c_ref[:, mine].T
        d_t = d_ref[:, mine].T
        ec_t = ec_ref[:, mine].T
        y = mm(d_t, x_ref[...])
        z = mm(c_t, s_ref[...]) - mm(ec_t, x_ref[...])
        for bk in range(blocks):
            other = pl.ds(bk * block, block)
            u_k = u_ref[other, :]
            if bk <= bl:
                m = mm(d_t, c_ref[:, other])
                if bk == bl:
                    m = jnp.where(below, m, 0.0)
                y = y + mm(m.astype(jnp.bfloat16), u_k)
            if bk >= bl:
                m = mm(c_t, d_ref[:, other])
                if bk == bl:
                    m = jnp.where(upto_diag, 0.0, m)
                z = z + mm(m.astype(jnp.bfloat16), v_ref[other, :])
            if bk < bl:
                m = mm(ec_t, c_ref[:, other])
            elif bk > bl:
                m = mm(c_t, ec_ref[:, other])
            else:
                m = jnp.where(upto_diag, mm(ec_t, c_ref[:, other]), mm(c_t, ec_ref[:, other]))
            z = z - mm(m.astype(jnp.bfloat16), u_k)
        y = y.astype(jnp.bfloat16)
        z = z.astype(jnp.bfloat16)
        for j in range(block // hd):
            l = bl * (block // hd) + j
            y_l, z_l = y[j * hd : (j + 1) * hd], z[j * hd : (j + 1) * hd]
            small = q_ref[l, :, 2 * cols : 2 * cols + 2 * hd]
            out_ref[l, :, :cols] = (adapter_scale * mm(small[:, :hd], y_l)).astype(jnp.bfloat16)
            out_ref[l, :, cols : 2 * cols] = (adapter_scale * mm(small[:, hd:], z_l)).astype(
                jnp.bfloat16
            )
            tail = jnp.concatenate(
                [mm_nt(q_ref[l, :, :cols], y_l), mm_nt(q_ref[l, :, cols : 2 * cols], z_l)], axis=1
            )
            out_ref[l, :, 2 * cols :] = (adapter_scale * tail).astype(jnp.bfloat16)


def params():
    return pltpu.CompilerParams(vmem_limit_bytes=vmem_bytes)


def in_vmem(count):
    return [pl.BlockSpec(memory_space=pltpu.VMEM)] * count


def spread(sizes, section, w_value, w_out, gain, x, cotangent, weight):
    layers, hd, rank, tokens, cols = sizes
    shape = jax.ShapeDtypeStruct((2 * hd + 2 * (tokens // layers), cols), jnp.bfloat16)
    return pl.pallas_call(
        functools.partial(spread_kernel, sizes),
        out_shape=(shape,) * layers,
        in_specs=[pl.BlockSpec(memory_space=pltpu.SMEM)] + in_vmem(6),
        out_specs=tuple(in_vmem(layers)),
        compiler_params=params(),
    )(section, w_value, w_out, gain, x, cotangent, weight)


def store(sizes, members, value_down, output_up, gain, value_up, out_down):
    layers, hd, rank, tokens, cols = sizes
    return pl.pallas_call(
        functools.partial(store_kernel, sizes),
        out_shape=jax.ShapeDtypeStruct((members, rank, 2 * cols + 2 * hd), jnp.bfloat16),
        in_specs=in_vmem(5),
        out_specs=in_vmem(1)[0],
        compiler_params=params(),
    )(value_down, output_up, gain, value_up, out_down)


def gram(sizes, section, blocks, q):
    layers, hd, rank, tokens, cols = sizes
    width = layers * hd
    return pl.pallas_call(
        functools.partial(gram_kernel, sizes),
        out_shape=(
            jax.ShapeDtypeStruct((width, cols), jnp.bfloat16),
            jax.ShapeDtypeStruct((width, cols), jnp.bfloat16),
            jax.ShapeDtypeStruct((tokens, cols), jnp.bfloat16),
            jax.ShapeDtypeStruct((tokens, cols), jnp.bfloat16),
            jax.ShapeDtypeStruct((3 * tokens + width, width), jnp.bfloat16),
        ),
        in_specs=[pl.BlockSpec(memory_space=pltpu.SMEM)] + in_vmem(layers + 1),
        out_specs=tuple(in_vmem(5)),
        scratch_shapes=[
            pltpu.VMEM((tokens, cols), jnp.float32),
            pltpu.VMEM((tokens, cols), jnp.float32),
        ],
        compiler_params=params(),
    )(section, *blocks, q)


def solve(sizes, features, k, x, s, u, v, q):
    layers, hd, rank, tokens, cols = sizes
    width = layers * hd
    return pl.pallas_call(
        functools.partial(solve_kernel, sizes, features),
        out_shape=jax.ShapeDtypeStruct(q.shape, jnp.bfloat16),
        in_specs=in_vmem(6),
        out_specs=in_vmem(1)[0],
        scratch_shapes=[
            pltpu.VMEM((tokens, width), jnp.bfloat16),
            pltpu.VMEM((tokens, width), jnp.bfloat16),
            pltpu.VMEM((tokens, width), jnp.bfloat16),
            pltpu.VMEM((layers, tokens, hd), jnp.float32),
            pltpu.VMEM((layers, tokens, hd), jnp.float32),
            pltpu.VMEM((layers, tokens, 1), jnp.float32),
        ],
        compiler_params=params(),
    )(k, x, s, u, v, q)


def swap(value, axis):
    return lax.all_to_all(value, axis, split_axis=0, concat_axis=0, tiled=True)


def pick(chooser, parts):
    flat = parts.reshape(parts.shape[0], -1)
    return mm(chooser, flat).astype(jnp.bfloat16).reshape((chooser.shape[0],) + parts.shape[1:])


def body(
    inputs,
    cotangent,
    norm_gain,
    w_value,
    w_out,
    value_down,
    value_up_factor,
    out_down,
    output_up_factor,
    block_tenant,
    valid_tokens,
    tenant_slot,
):
    section = lax.axis_index("pipe")
    sections = lax.axis_size("pipe")
    member = lax.axis_index("dp")
    members = lax.axis_size("dp")
    rows, features = inputs.shape[1], inputs.shape[2]
    hd, rank = w_value.shape[1], value_down.shape[2]
    cols = features // sections
    tokens = rows * sections
    sizes = (sections, hd, rank, tokens, cols)

    ids = jnp.arange(tenant_slot.shape[0], dtype=jnp.int32)
    tenant_hot = block_tenant[:, None] == ids[None, :]
    slot_of = jnp.sum(jnp.where(tenant_hot, tenant_slot[None, :], 0), axis=1)
    slot_hot = (slot_of[:, None] == ids[None, :]).astype(jnp.bfloat16)
    member_hot = jnp.arange(members, dtype=jnp.int32) == member
    own_tenant = jnp.sum(jnp.where(member_hot, block_tenant, 0))
    own_valid = jnp.sum(jnp.where(member_hot, valid_tokens, 0))
    tenant_tokens = jnp.sum(jnp.where(block_tenant == own_tenant, valid_tokens, 0)).astype(
        jnp.float32
    )

    gain = norm_gain
    stored = store(
        sizes,
        members,
        value_down[0, 0],
        output_up_factor[0, 0],
        gain,
        value_up_factor[0, 0],
        out_down[0, 0],
    )
    position = section * rows + jnp.arange(rows, dtype=jnp.int32)
    weight = jnp.where(position < own_valid, 1.0, 0.0).astype(jnp.float32) / tenant_tokens
    own_section = section.astype(jnp.int32)[None]
    blocks = spread(
        sizes,
        own_section,
        w_value[0],
        w_out[0],
        gain,
        inputs[0],
        cotangent[0],
        weight[:, None],
    )
    blocks = [blocks[0]] + [
        lax.ppermute(blocks[step], "pipe", [(i, (i + step) % sections) for i in range(sections)])
        for step in range(1, sections)
    ]
    adapters = swap(swap(pick(slot_hot, swap(stored, "dp")), "dp"), "pipe")

    u, v, x, s, partial = gram(sizes, own_section, blocks, adapters)
    width = partial.shape[1]
    shares = swap(partial.reshape(sections, -1, width), "pipe")
    share = jnp.sum(shares.astype(jnp.float32), axis=0).astype(jnp.bfloat16)
    whole = swap(jnp.broadcast_to(share[None], shares.shape), "pipe").reshape(partial.shape)

    grads = solve(sizes, features, whole, x, s, u, v, adapters)

    by_layer = swap(grads, "dp")
    summed = pick(slot_hot.T, by_layer)
    owned = swap(swap(summed, "dp"), "pipe")
    grad_value_down = owned[:, :, :cols].transpose(1, 0, 2).reshape(rank, features)
    grad_value_down = (grad_value_down.astype(jnp.float32) * gain).astype(jnp.bfloat16)
    grad_out_up = owned[:, :, cols : 2 * cols].transpose(1, 0, 2).reshape(rank, features)
    tail = jnp.sum(owned[:, :, 2 * cols :].astype(jnp.float32), axis=0).astype(jnp.bfloat16)
    return (
        grad_value_down[None, None],
        tail[None, None, :, :hd],
        tail[None, None, :, hd:],
        grad_out_up[None, None],
    )


def solution(mesh):
    return jax.shard_map(
        body,
        mesh=mesh,
        in_specs=(
            P("pipe", "dp", None),
            P("pipe", "dp", None),
            P("pipe", None),
            P("pipe", None, None),
            P("pipe", None, None),
            P("pipe", "dp", None, None),
            P("pipe", "dp", None, None),
            P("pipe", "dp", None, None),
            P("pipe", "dp", None, None),
            P(),
            P(),
            P(),
        ),
        out_specs=(
            P("pipe", "dp", None, None),
            P("pipe", "dp", None, None),
            P("pipe", "dp", None, None),
            P("pipe", "dp", None, None),
        ),
        check_vma=False,
    )
```

```python
import functools

import jax
import jax.numpy as jnp
from jax import lax
from jax.experimental import pallas as pl
from jax.experimental.pallas import tpu as pltpu
from jax.sharding import PartitionSpec as P

adapter_scale = 2.0
norm_eps = 1e-05
block = 256
vmem_bytes = 56 * 1024 * 1024


def mm(left, right):
    return lax.dot_general(
        left, right, (((1,), (0,)), ((), ())), preferred_element_type=jnp.float32
    )


def mm_nt(left, right):
    return lax.dot_general(
        left, right, (((1,), (1,)), ((), ())), preferred_element_type=jnp.float32
    )


def mm_tn(left, right):
    return lax.dot_general(
        left, right, (((0,), (0,)), ((), ())), preferred_element_type=jnp.float32
    )


def layer_mask(rows, columns, hd, compare):
    row_layer = lax.broadcasted_iota(jnp.int32, (rows, columns), 0) // hd
    column_layer = lax.broadcasted_iota(jnp.int32, (rows, columns), 1) // hd
    return compare(row_layer, column_layer)


def pack_kernel(
    sizes,
    here_ref,
    tenant_ref,
    valid_ref,
    wv_ref,
    wo_ref,
    gain_ref,
    x_ref,
    cot_ref,
    vd_ref,
    ou_ref,
    vu_ref,
    od_ref,
    stored_ref,
    *out_refs
):
    layers, hd, rank, tokens, cols = sizes
    rows = tokens // layers
    part = hd // 2
    section, member = here_ref[0], here_ref[1]
    side = len(out_refs)
    across = layers // side
    mine = pl.ds(pl.multiple_of(lax.rem(member, 2) * part, part), part)
    own = tenant_ref[member]
    total = jnp.int32(0)
    for i in range(tenant_ref.shape[0]):
        total = total + jnp.where(tenant_ref[i] == own, valid_ref[i], 0)
    position = section * rows + lax.broadcasted_iota(jnp.int32, (rows, 1), 0)
    weight = jnp.where(position < valid_ref[member], 1.0, 0.0).astype(jnp.float32)
    weight = weight / jnp.full((rows, 1), total, jnp.int32).astype(jnp.float32)
    small = jnp.concatenate([vu_ref[...], od_ref[...]], axis=1)
    for k in range(stored_ref.shape[0]):
        at = pl.ds(k * cols, cols)
        stored_ref[k, :, :cols] = (vd_ref[:, at].astype(jnp.float32) * gain_ref[:, at]).astype(
            jnp.bfloat16
        )
        stored_ref[k, :, cols : 2 * cols] = ou_ref[:, at]
        stored_ref[k, :, 2 * cols :] = small
    own_line = section // across
    for step, out_ref in enumerate(out_refs):
        line = lax.rem(own_line + step, side)
        for k in range(across):
            at = pl.ds(pl.multiple_of((line * across + k) * cols, cols), cols)
            out_ref[k, :part, :] = (wv_ref[mine, at].astype(jnp.float32) * gain_ref[:, at]).astype(
                jnp.bfloat16
            )
            out_ref[k, part:hd, :] = wo_ref[mine, at]
            seeded = cot_ref[:, at].astype(jnp.float32) * weight
            out_ref[k, hd:, :] = jnp.concatenate(
                [x_ref[:, at].astype(jnp.float32), seeded], axis=0
            ).astype(jnp.bfloat16)


def pick_kernel(side, across, here_ref, tenant_ref, slot_ref, parts_ref, *refs):
    lines, out_ref, turned = refs[:side], refs[side], refs[side + 1 :]
    for j in range(out_ref.shape[0]):
        out_ref[j] = parts_ref[slot_ref[tenant_ref[j]]]
    place = lax.rem(here_ref[0], across)
    for step, turned_ref in enumerate(turned):
        at = lax.rem(place + step, across)
        for k in range(side):
            turned_ref[k] = lines[k][at]


def finish_kernel(sizes, owned_ref, gain_ref, gvd_ref, gvu_ref, god_ref, gou_ref):
    layers, hd, rank, tokens, cols = sizes
    tail = jnp.zeros((rank, 2 * hd), jnp.float32)
    for c in range(layers):
        at = pl.ds(c * cols, cols)
        gvd_ref[:, at] = (owned_ref[c, :, :cols].astype(jnp.float32) * gain_ref[:, at]).astype(
            jnp.bfloat16
        )
        gou_ref[:, at] = owned_ref[c, :, cols : 2 * cols]
        tail = tail + owned_ref[c, :, 2 * cols :].astype(jnp.float32)
    gvu_ref[...] = tail[:, :hd].astype(jnp.bfloat16)
    god_ref[...] = tail[:, hd:].astype(jnp.bfloat16)


def gram_kernel(sizes, side, across, here_ref, *refs):
    layers, hd, rank, tokens, cols = sizes
    own_refs, other_refs, refs = refs[:across], refs[across : 2 * across], refs[2 * across :]
    q_ref, u_ref, v_ref, x_ref, s_ref, out_ref, x_wide, s_wide, w_wide = refs
    rows = tokens // layers
    part = hd // 2
    section, core = here_ref[0], lax.rem(here_ref[1], 2)
    line, place = section // across, lax.rem(section, across)
    mine = pl.ds(pl.multiple_of(core * part, part), part)
    theirs = pl.ds(pl.multiple_of((1 - core) * part, part), part)
    for step in range(layers):
        dx, dy = step // side, step % side
        l = lax.rem(line + side - dy, side) * across + lax.rem(place + across - dx, across)
        slot = step % 2
        for kind in range(2):
            at = pl.ds(kind * part, part)
            w_wide[slot, kind, mine, :] = own_refs[dx][dy, at, :].astype(jnp.float32)
            w_wide[slot, kind, theirs, :] = other_refs[dx][dy, at, :].astype(jnp.float32)
        q_l = q_ref[l]
        small = q_l[:, 2 * cols : 2 * cols + 2 * hd]
        delta_v = mm_tn(small[:, :hd], q_l[:, :cols])
        delta_u = mm_tn(small[:, hd:], q_l[:, cols : 2 * cols])
        at = pl.ds(pl.multiple_of(l * hd, hd), hd)
        v_ref[at, :] = (w_wide[slot, 0] + adapter_scale * delta_v).astype(jnp.bfloat16)
        u_ref[at, :] = (w_wide[slot, 1] + adapter_scale * delta_u).astype(jnp.bfloat16)
        both = own_refs[dx][dy, hd:, :].astype(jnp.float32)
        at = pl.ds(pl.multiple_of(l * rows, rows), rows)
        x_wide[at, :] = both[:rows]
        s_wide[at, :] = both[rows:]
    x_ref[...] = x_wide[...].astype(jnp.bfloat16)
    s_ref[...] = s_wide[...].astype(jnp.bfloat16)
    width = layers * hd
    base = 3 * tokens
    below = layer_mask(block, block, hd, lambda r, c: r < c)
    for bj in range(width // block):
        at_col = pl.ds(bj * block, block)
        u_col, v_col = u_ref[at_col, :], v_ref[at_col, :]
        out_ref[:tokens, at_col] = mm_nt(x_ref[...], v_col).astype(jnp.bfloat16)
        out_ref[tokens : 2 * tokens, at_col] = mm_nt(x_ref[...], u_col).astype(jnp.bfloat16)
        out_ref[2 * tokens : 3 * tokens, at_col] = mm_nt(s_ref[...], u_col).astype(jnp.bfloat16)
        for bi in range(width // block):
            rows = u_ref[pl.ds(bi * block, block), :]
            if bi < bj:
                part = mm_nt(rows, v_col)
            elif bi > bj:
                part = mm_nt(rows, u_col)
            else:
                part = jnp.where(below, mm_nt(rows, v_col), mm_nt(rows, u_col))
            out_ref[pl.ds(base + bi * block, block), at_col] = part.astype(jnp.bfloat16)
    wide = x_wide[...]
    wide = wide * wide
    folded = wide[:, : 2 * hd]
    for at in range(2 * hd, cols, 2 * hd):
        folded = folded + wide[:, at : at + 2 * hd]
    out_ref[tokens : 2 * tokens, width - hd :] = (folded[:, :hd] + folded[:, hd:]).astype(
        jnp.bfloat16
    )


def half(pair, l):
    hd = pair.shape[1] // 2
    return pair[:, hd:] if l % 2 else pair[:, :hd]


def solve_kernel(
    sizes,
    features,
    k_ref,
    x_ref,
    s_ref,
    u_ref,
    v_ref,
    q_ref,
    out_ref,
    c_ref,
    d_ref,
    ec_ref,
    a_ref,
    bp_ref,
    inv_ref,
):
    layers, hd, rank, tokens, cols = sizes
    width = layers * hd
    base = 3 * tokens
    c_ref[...] = jnp.zeros_like(c_ref)
    d_ref[...] = jnp.zeros_like(d_ref)
    ec_ref[...] = jnp.zeros_like(ec_ref)

    def pair_of(l):
        return pl.ds(2 * hd * (l // 2), 2 * hd)

    def upto(l):
        return 2 * hd * ((l + 1) // 2)

    folded = k_ref[tokens : 2 * tokens, width - 2 * hd :].astype(jnp.float32)[:, hd:]
    square = jnp.sum(folded, axis=1, keepdims=True)
    for l in range(layers):
        pair = pair_of(l)
        rows_l = pl.ds(base + l * hd, hd)
        a = half(k_ref[:tokens, pair], l).astype(jnp.float32)
        if l:
            w = upto(l)
            known = c_ref[:, :w]
            a = a + half(mm(known, k_ref[base : base + w, pair]), l)
        inverse = lax.rsqrt(jnp.maximum(square, 0.0) / features + norm_eps)
        c = (inverse * a).astype(jnp.bfloat16)
        c_ref[:, l * hd : (l + 1) * hd] = c
        a_ref[l] = a
        inv_ref[l] = inverse
        if l == layers - 1:
            break
        b = half(k_ref[tokens : 2 * tokens, pair], l).astype(jnp.float32)
        if l:
            b = b + mm_nt(known, k_ref[rows_l, :w])
        wide = c.astype(jnp.float32)
        after = b + half(mm(c, k_ref[rows_l, pair]), l)
        square = square + jnp.sum(wide * (b + after), axis=1, keepdims=True)
        bp_ref[l] = after

    pull = jnp.zeros((tokens, 1), jnp.float32)
    for l in range(layers - 1, -1, -1):
        pair = pair_of(l)
        rows_l = pl.ds(base + l * hd, hd)
        p = half(k_ref[2 * tokens : 3 * tokens, pair], l).astype(jnp.float32)
        if l < layers - 1:
            w = upto(l)
            p = p - pull * bp_ref[l]
            p = p + mm_nt(d_ref[:, w:], k_ref[rows_l, w:])
            p = p - half(mm(ec_ref[:, w:], k_ref[base + w : base + width, pair]), l)
        inverse = inv_ref[l]
        d_ref[:, l * hd : (l + 1) * hd] = (inverse * p).astype(jnp.bfloat16)
        c = c_ref[:, l * hd : (l + 1) * hd].astype(jnp.float32)
        ec_ref[:, l * hd : (l + 1) * hd] = (pull * c).astype(jnp.bfloat16)
        correction = jnp.sum(p * a_ref[l], axis=1, keepdims=True) / features
        pull = pull + inverse * inverse * inverse * correction

    below = layer_mask(block, block, hd, lambda r, c: r > c)
    upto_diag = layer_mask(block, block, hd, lambda r, c: r >= c)
    blocks = width // block
    for bl in range(blocks):
        mine = pl.ds(bl * block, block)
        c_t = c_ref[:, mine].T
        d_t = d_ref[:, mine].T
        ec_t = ec_ref[:, mine].T
        y = mm(d_t, x_ref[...])
        z = mm(c_t, s_ref[...]) - mm(ec_t, x_ref[...])
        for bk in range(blocks):
            other = pl.ds(bk * block, block)
            u_k = u_ref[other, :]
            if bk <= bl:
                m = mm(d_t, c_ref[:, other])
                if bk == bl:
                    m = jnp.where(below, m, 0.0)
                y = y + mm(m.astype(jnp.bfloat16), u_k)
            if bk >= bl:
                m = mm(c_t, d_ref[:, other])
                if bk == bl:
                    m = jnp.where(upto_diag, 0.0, m)
                z = z + mm(m.astype(jnp.bfloat16), v_ref[other, :])
            if bk < bl:
                m = mm(ec_t, c_ref[:, other])
            elif bk > bl:
                m = mm(c_t, ec_ref[:, other])
            else:
                m = jnp.where(upto_diag, mm(ec_t, c_ref[:, other]), mm(c_t, ec_ref[:, other]))
            z = z - mm(m.astype(jnp.bfloat16), u_k)
        y = y.astype(jnp.bfloat16)
        z = z.astype(jnp.bfloat16)
        for j in range(block // hd):
            l = bl * (block // hd) + j
            y_l, z_l = y[j * hd : (j + 1) * hd], z[j * hd : (j + 1) * hd]
            small = q_ref[l, :, 2 * cols : 2 * cols + 2 * hd]
            out_ref[l, :, :cols] = (adapter_scale * mm(small[:, :hd], y_l)).astype(jnp.bfloat16)
            out_ref[l, :, cols : 2 * cols] = (adapter_scale * mm(small[:, hd:], z_l)).astype(
                jnp.bfloat16
            )
            tail = jnp.concatenate(
                [mm_nt(q_ref[l, :, :cols], y_l), mm_nt(q_ref[l, :, cols : 2 * cols], z_l)], axis=1
            )
            out_ref[l, :, 2 * cols :] = (adapter_scale * tail).astype(jnp.bfloat16)


def params():
    return pltpu.CompilerParams(vmem_limit_bytes=vmem_bytes)


def in_vmem(count):
    return [pl.BlockSpec(memory_space=pltpu.VMEM)] * count


def in_smem(count):
    return [pl.BlockSpec(memory_space=pltpu.SMEM)] * count


def pack(sizes, side, members, scalars, arrays):
    layers, hd, rank, tokens, cols = sizes
    line = jax.ShapeDtypeStruct(
        (layers // side, hd + 2 * (tokens // layers), cols), jnp.bfloat16
    )
    stored = jax.ShapeDtypeStruct((members, rank, 2 * cols + 2 * hd), jnp.bfloat16)
    return pl.pallas_call(
        functools.partial(pack_kernel, sizes),
        out_shape=(stored,) + (line,) * side,
        in_specs=in_smem(len(scalars)) + in_vmem(len(arrays)),
        out_specs=tuple(in_vmem(1 + side)),
        compiler_params=params(),
    )(*scalars, *arrays)


def pick_rows(scalars, parts, lines):
    side = len(lines)
    across = lines[0].shape[0]
    turned = jax.ShapeDtypeStruct((side,) + lines[0].shape[1:], jnp.bfloat16)
    return pl.pallas_call(
        functools.partial(pick_kernel, side, across),
        out_shape=(jax.ShapeDtypeStruct(parts.shape, parts.dtype),) + (turned,) * across,
        in_specs=in_smem(len(scalars)) + in_vmem(1 + side),
        out_specs=tuple(in_vmem(1 + across)),
        compiler_params=params(),
    )(*scalars, parts, *lines)


def relay_kernel(*refs):
    pass


def relay(value, after):
    return pl.pallas_call(
        relay_kernel,
        out_shape=jax.ShapeDtypeStruct(value.shape, value.dtype),
        in_specs=[pl.BlockSpec(memory_space=pl.ANY)] * (1 + len(after)),
        out_specs=pl.BlockSpec(memory_space=pl.ANY),
        input_output_aliases={0: 0},
    )(value, *after)


def finish(sizes, owned, gain):
    layers, hd, rank, tokens, cols = sizes
    wide = jax.ShapeDtypeStruct((rank, layers * cols), jnp.bfloat16)
    narrow = jax.ShapeDtypeStruct((rank, hd), jnp.bfloat16)
    return pl.pallas_call(
        functools.partial(finish_kernel, sizes),
        out_shape=(wide, narrow, narrow, wide),
        in_specs=in_vmem(2),
        out_specs=tuple(in_vmem(4)),
        compiler_params=params(),
    )(owned, gain)


def gram(sizes, side, here, own, other, q):
    layers, hd, rank, tokens, cols = sizes
    width = layers * hd
    return pl.pallas_call(
        functools.partial(gram_kernel, sizes, side, len(own)),
        out_shape=(
            jax.ShapeDtypeStruct((width, cols), jnp.bfloat16),
            jax.ShapeDtypeStruct((width, cols), jnp.bfloat16),
            jax.ShapeDtypeStruct((tokens, cols), jnp.bfloat16),
            jax.ShapeDtypeStruct((tokens, cols), jnp.bfloat16),
            jax.ShapeDtypeStruct((3 * tokens + width, width), jnp.bfloat16),
        ),
        in_specs=in_smem(1) + in_vmem(2 * len(own) + 1),
        out_specs=tuple(in_vmem(5)),
        scratch_shapes=[
            pltpu.VMEM((tokens, cols), jnp.float32),
            pltpu.VMEM((tokens, cols), jnp.float32),
            pltpu.VMEM((2, 2, hd, cols), jnp.float32),
        ],
        compiler_params=params(),
    )(here, *own, *other, q)


def solve(sizes, features, k, x, s, u, v, q):
    layers, hd, rank, tokens, cols = sizes
    width = layers * hd
    return pl.pallas_call(
        functools.partial(solve_kernel, sizes, features),
        out_shape=jax.ShapeDtypeStruct(q.shape, jnp.bfloat16),
        in_specs=in_vmem(6),
        out_specs=in_vmem(1)[0],
        scratch_shapes=[
            pltpu.VMEM((tokens, width), jnp.bfloat16),
            pltpu.VMEM((tokens, width), jnp.bfloat16),
            pltpu.VMEM((tokens, width), jnp.bfloat16),
            pltpu.VMEM((layers, tokens, hd), jnp.float32),
            pltpu.VMEM((layers, tokens, hd), jnp.float32),
            pltpu.VMEM((layers, tokens, 1), jnp.float32),
        ],
        compiler_params=params(),
    )(k, x, s, u, v, q)


def swap(value, axis):
    return lax.all_to_all(value, axis, split_axis=0, concat_axis=0, tiled=True)


def pick(chooser, parts):
    flat = parts.reshape(parts.shape[0], -1)
    return mm(chooser, flat).astype(jnp.bfloat16).reshape((chooser.shape[0],) + parts.shape[1:])


def body(
    inputs,
    cotangent,
    norm_gain,
    w_value,
    w_out,
    value_down,
    value_up_factor,
    out_down,
    output_up_factor,
    block_tenant,
    valid_tokens,
    tenant_slot,
):
    section = lax.axis_index("pipe")
    sections = lax.axis_size("pipe")
    member = lax.axis_index("dp")
    members = lax.axis_size("dp")
    rows, features = inputs.shape[1], inputs.shape[2]
    hd, rank = w_value.shape[1], value_down.shape[2]
    cols = features // sections
    tokens = rows * sections
    sizes = (sections, hd, rank, tokens, cols)

    ids = jnp.arange(tenant_slot.shape[0], dtype=jnp.int32)
    tenant_hot = block_tenant[:, None] == ids[None, :]
    slot_of = jnp.sum(jnp.where(tenant_hot, tenant_slot[None, :], 0), axis=1)
    slot_hot = (slot_of[:, None] == ids[None, :]).astype(jnp.bfloat16)
    gain = norm_gain
    here = jnp.stack([section, member]).astype(jnp.int32)
    side = 4 if sections % 4 == 0 else 2
    across = sections // side
    stored, *lines = pack(
        sizes,
        side,
        members,
        (here, block_tenant, valid_tokens),
        (
            w_value[0],
            w_out[0],
            gain,
            inputs[0],
            cotangent[0],
            value_down[0, 0],
            output_up_factor[0, 0],
            value_up_factor[0, 0],
            out_down[0, 0],
        ),
    )
    lines = [lines[0]] + [
        lax.ppermute(
            lines[step], "pipe", [(i, (i + step * across) % sections) for i in range(sections)]
        )
        for step in range(1, side)
    ]
    adapters, *turned = pick_rows((here, block_tenant, tenant_slot), swap(stored, "dp"), lines)
    turned = [turned[0]] + [
        lax.ppermute(
            turned[step],
            "pipe",
            [(i, i // across * across + (i + step) % across) for i in range(sections)],
        )
        for step in range(1, across)
    ]
    adapters = swap(relay(swap(adapters, "dp"), turned[1:]), "pipe")
    other = [lax.ppermute(part, "dp", [(i, i ^ 1) for i in range(members)]) for part in turned]

    u, v, x, s, partial = gram(sizes, side, here, turned, other, adapters)
    width = partial.shape[1]
    shares = swap(partial.reshape(sections, -1, width), "pipe")
    share = jnp.sum(shares.astype(jnp.float32), axis=0).astype(jnp.bfloat16)
    whole = swap(jnp.broadcast_to(share[None], shares.shape), "pipe").reshape(partial.shape)

    grads = solve(sizes, features, whole, x, s, u, v, adapters)

    by_layer = swap(grads, "dp")
    summed = pick(slot_hot.T, by_layer)
    owned = swap(swap(summed, "dp"), "pipe")
    return tuple(part[None, None] for part in finish(sizes, owned, gain))


def solution(mesh):
    return jax.shard_map(
        body,
        mesh=mesh,
        in_specs=(
            P("pipe", "dp", None),
            P("pipe", "dp", None),
            P("pipe", None),
            P("pipe", None, None),
            P("pipe", None, None),
            P("pipe", "dp", None, None),
            P("pipe", "dp", None, None),
            P("pipe", "dp", None, None),
            P("pipe", "dp", None, None),
            P(),
            P(),
            P(),
        ),
        out_specs=(
            P("pipe", "dp", None, None),
            P("pipe", "dp", None, None),
            P("pipe", "dp", None, None),
            P("pipe", "dp", None, None),
        ),
        check_vma=False,
    )
```

```python
import functools

import jax
import jax.numpy as jnp
from jax import lax
from jax.experimental import pallas as pl
from jax.experimental.pallas import tpu as pltpu
from jax.sharding import PartitionSpec as P

adapter_scale = 2.0
norm_eps = 1e-05
block = 256
vmem_bytes = 20 * 1024 * 1024
whole_vmem_bytes = 56 * 1024 * 1024
pipe = ("a", "b", "x")
dp = ("z", "core")


def mm(left, right):
    return lax.dot_general(
        left, right, (((1,), (0,)), ((), ())), preferred_element_type=jnp.float32
    )


def mm_nt(left, right):
    return lax.dot_general(
        left, right, (((1,), (1,)), ((), ())), preferred_element_type=jnp.float32
    )


def mm_tn(left, right):
    return lax.dot_general(
        left, right, (((0,), (0,)), ((), ())), preferred_element_type=jnp.float32
    )


def layer_mask(rows, columns, hd, compare):
    row_layer = lax.broadcasted_iota(jnp.int32, (rows, columns), 0) // hd
    column_layer = lax.broadcasted_iota(jnp.int32, (rows, columns), 1) // hd
    return compare(row_layer, column_layer)


def store_kernel(sizes, vd_ref, ou_ref, gain_ref, vu_ref, od_ref, out_ref):
    layers, hd, rank, tokens, cols = sizes
    small = jnp.concatenate([vu_ref[...], od_ref[...]], axis=1)
    for k in range(out_ref.shape[0]):
        at = pl.ds(k * cols, cols)
        out_ref[k, :, :cols] = (vd_ref[:, at].astype(jnp.float32) * gain_ref[:, at]).astype(
            jnp.bfloat16
        )
        out_ref[k, :, cols : 2 * cols] = ou_ref[:, at]
        out_ref[k, :, 2 * cols :] = small


def lines_kernel(
    sizes,
    here_ref,
    tenant_ref,
    valid_ref,
    wv_ref,
    wo_ref,
    gain_ref,
    x_ref,
    cot_ref,
    other_x_ref,
    other_cot_ref,
    *out_refs
):
    layers, hd, rank, tokens, cols = sizes
    rows = tokens // layers
    part = hd // 2
    section, member = here_ref[0], here_ref[1]
    core = lax.rem(member, 2)
    side = len(out_refs)
    across = layers // side
    mine = pl.ds(pl.multiple_of(lax.rem(member // 2, 2) * part, part), part)
    position = section * rows + lax.broadcasted_iota(jnp.int32, (rows, 1), 0)

    def token_weight(index):
        total = jnp.int32(0)
        for i in range(tenant_ref.shape[0]):
            total = total + jnp.where(tenant_ref[i] == tenant_ref[index], valid_ref[i], 0)
        kept = jnp.where(position < valid_ref[index], 1.0, 0.0).astype(jnp.float32)
        return kept / jnp.full((rows, 1), total, jnp.int32).astype(jnp.float32)

    own_weight = token_weight(member)
    other_weight = token_weight(member + 1 - 2 * core)
    for step, out_ref in enumerate(out_refs):
        line = lax.rem(section // across + step, side)
        own = lax.div(line, side // 2) == core
        for k in range(across):
            column = (lax.rem(line, side // 2) * across + k) * 2 + core
            at = pl.ds(pl.multiple_of(column * cols, cols), cols)
            out_ref[k, :part, :] = (wv_ref[mine, at].astype(jnp.float32) * gain_ref[:, at]).astype(
                jnp.bfloat16
            )
            out_ref[k, part:hd, :] = wo_ref[mine, at]
            x = jnp.where(
                own, x_ref[:, at].astype(jnp.float32), other_x_ref[:, at].astype(jnp.float32)
            )
            seeded = jnp.where(
                own,
                cot_ref[:, at].astype(jnp.float32) * own_weight,
                other_cot_ref[:, at].astype(jnp.float32) * other_weight,
            )
            out_ref[k, hd:, :] = jnp.concatenate([x, seeded], axis=0).astype(jnp.bfloat16)


def pick_kernel(side, across, here_ref, tenant_ref, slot_ref, parts_ref, *refs):
    lines, out_ref, turned = refs[:side], refs[side], refs[side + 1 :]
    for j in range(out_ref.shape[0]):
        out_ref[j] = parts_ref[slot_ref[tenant_ref[j]]]
    place = lax.rem(here_ref[0], across)
    for step, turned_ref in enumerate(turned):
        at = lax.rem(place + step, across)
        for k in range(side):
            turned_ref[k] = lines[k][at]


def finish_kernel(sizes, owned_ref, gain_ref, gvd_ref, gvu_ref, god_ref, gou_ref):
    layers, hd, rank, tokens, cols = sizes
    tail = jnp.zeros((rank, 2 * hd), jnp.float32)
    for c in range(layers):
        at = pl.ds(c * cols, cols)
        gvd_ref[:, at] = (owned_ref[c, :, :cols].astype(jnp.float32) * gain_ref[:, at]).astype(
            jnp.bfloat16
        )
        gou_ref[:, at] = owned_ref[c, :, cols : 2 * cols]
        tail = tail + owned_ref[c, :, 2 * cols :].astype(jnp.float32)
    gvu_ref[...] = tail[:, :hd].astype(jnp.bfloat16)
    god_ref[...] = tail[:, hd:].astype(jnp.bfloat16)


def turned_index(l, layers):
    return l % (layers // 2) * 2 + l // (layers // 2)


def gram_kernel(sizes, side, across, here_ref, *refs):
    layers, hd, rank, tokens, cols = sizes
    own_refs, other_refs, refs = refs[:across], refs[across : across + 2], refs[across + 2 :]
    pairs = across // 2
    q_ref, u_ref, v_ref, x_ref, s_ref, keep_ref, give_ref, x_wide, s_wide, w_wide = refs
    rows = tokens // layers
    part = hd // 2
    section, core = here_ref[0], lax.rem(here_ref[1], 2)
    plane = lax.rem(here_ref[1] // 2, 2)
    line, place = section // across, lax.rem(section, across)
    mine = pl.ds(pl.multiple_of(plane * part, part), part)
    theirs = pl.ds(pl.multiple_of((1 - plane) * part, part), part)
    for step in range(layers):
        dx, dy = step // side, step % side
        l = lax.rem(line + side - dy, side) * across + lax.rem(place + across - dx, across)
        slot = step % 2
        for kind in range(2):
            at = pl.ds(kind * part, part)
            w_wide[slot, kind, mine, :] = own_refs[dx][dy, at, :].astype(jnp.float32)
            w_wide[slot, kind, theirs, :] = other_refs[dx // pairs][
                dx % pairs * side + dy, at, :
            ].astype(jnp.float32)
        q_l = q_ref[turned_index(l, layers)]
        small = q_l[:, 2 * cols : 2 * cols + 2 * hd]
        delta_v = mm_tn(small[:, :hd], q_l[:, :cols])
        delta_u = mm_tn(small[:, hd:], q_l[:, cols : 2 * cols])
        at = pl.ds(pl.multiple_of(l * hd, hd), hd)
        v_ref[at, :] = (w_wide[slot, 0] + adapter_scale * delta_v).astype(jnp.bfloat16)
        u_ref[at, :] = (w_wide[slot, 1] + adapter_scale * delta_u).astype(jnp.bfloat16)
        both = own_refs[dx][dy, hd:, :].astype(jnp.float32)
        at = pl.ds(pl.multiple_of(l * rows, rows), rows)
        x_wide[at, :] = both[:rows]
        s_wide[at, :] = both[rows:]
    x_ref[...] = x_wide[...].astype(jnp.bfloat16)
    s_ref[...] = s_wide[...].astype(jnp.bfloat16)
    width = layers * hd
    base = 3 * tokens
    below = layer_mask(block, block, hd, lambda r, c: r < c)
    lane = 2 * hd
    half_count = width // lane // 2

    def put(own_core, start, column, value):
        value = value.astype(jnp.bfloat16)
        for at in range(0, value.shape[1], lane):
            index = (column + at) // lane
            out_ref = keep_ref if index // half_count == own_core else give_ref
            out_ref[index % half_count, pl.ds(start, value.shape[0]), :] = value[:, at : at + lane]

    def products(own_core):
        for bj in range(width // block):
            column = bj * block
            at_col = pl.ds(column, block)
            u_col, v_col = u_ref[at_col, :], v_ref[at_col, :]
            put(own_core, 0, column, mm_nt(x_ref[...], v_col))
            x_u = mm_nt(x_ref[...], u_col)
            if column + block == width:
                wide = x_wide[...]
                wide = wide * wide
                folded = wide[:, :lane]
                for at in range(lane, cols, lane):
                    folded = folded + wide[:, at : at + lane]
                x_u = jnp.concatenate([x_u[:, : block - hd], folded[:, :hd] + folded[:, hd:]], axis=1)
            put(own_core, tokens, column, x_u)
            put(own_core, 2 * tokens, column, mm_nt(s_ref[...], u_col))
            for bi in range(width // block):
                height = min(block, width - hd - bi * block)
                rows_at = pl.ds(bi * block, height)
                rows_u = u_ref[rows_at, :]
                if bi < bj:
                    part = mm_nt(rows_u, v_col)
                elif bi > bj:
                    part = mm_nt(rows_u, u_col)
                else:
                    part = jnp.where(below[:height], mm_nt(rows_u, v_col), mm_nt(rows_u, u_col))
                put(own_core, base + bi * block, column, part)

    for own_core in range(2):
        pl.when(core == own_core)(functools.partial(products, own_core))


def half(pair, l):
    hd = pair.shape[1] // 2
    return pair[:, hd:] if l % 2 else pair[:, :hd]


def solve_kernel(
    sizes,
    features,
    here_ref,
    own_ref,
    other_ref,
    x_ref,
    s_ref,
    u_ref,
    v_ref,
    q_ref,
    out_ref,
    c_ref,
    d_ref,
    ec_ref,
    a_ref,
    bp_ref,
    inv_ref,
    k_ref,
    sems,
):
    layers, hd, rank, tokens, cols = sizes
    width = layers * hd
    base = 3 * tokens
    half_count = own_ref.shape[0]
    core = lax.rem(here_ref[1], 2)
    copies = [
        pltpu.make_async_copy(
            source, k_ref.at[pl.ds(place * half_count, half_count)], sems.at[index]
        )
        for index, (source, place) in enumerate(((own_ref, core), (other_ref, 1 - core)))
    ]
    for copy in copies:
        copy.start()
    c_ref[...] = jnp.zeros_like(c_ref)
    d_ref[...] = jnp.zeros_like(d_ref)
    ec_ref[...] = jnp.zeros_like(ec_ref)

    def upto(l):
        return 2 * hd * ((l + 1) // 2)

    def across_row(l, start, stop):
        rows_l = pl.ds(base + l * hd, hd)
        return jnp.concatenate(
            [k_ref[index, rows_l, :] for index in range(start // (2 * hd), stop // (2 * hd))],
            axis=1,
        )

    for copy in copies:
        copy.wait()
    folded = k_ref[width // (2 * hd) - 1, tokens : 2 * tokens, :].astype(jnp.float32)[:, hd:]
    square = jnp.sum(folded, axis=1, keepdims=True)
    for l in range(layers):
        pair = l // 2
        a = half(k_ref[pair, :tokens, :], l).astype(jnp.float32)
        if l:
            w = upto(l)
            known = c_ref[:, :w]
            top = min(w, width - hd)
            a = a + half(mm(known[:, :top], k_ref[pair, base : base + top, :]), l)
        inverse = lax.rsqrt(jnp.maximum(square, 0.0) / features + norm_eps)
        c = (inverse * a).astype(jnp.bfloat16)
        c_ref[:, l * hd : (l + 1) * hd] = c
        a_ref[l] = a
        inv_ref[l] = inverse
        if l == layers - 1:
            break
        b = half(k_ref[pair, tokens : 2 * tokens, :], l).astype(jnp.float32)
        if l:
            b = b + mm_nt(known, across_row(l, 0, w))
        wide = c.astype(jnp.float32)
        after = b + half(mm(c, k_ref[pair, pl.ds(base + l * hd, hd), :]), l)
        square = square + jnp.sum(wide * (b + after), axis=1, keepdims=True)
        bp_ref[l] = after

    pull = jnp.zeros((tokens, 1), jnp.float32)
    for l in range(layers - 1, -1, -1):
        pair = l // 2
        p = half(k_ref[pair, 2 * tokens : 3 * tokens, :], l).astype(jnp.float32)
        if l < layers - 1:
            w = upto(l)
            top = width - hd
            p = p - pull * bp_ref[l]
            p = p + mm_nt(d_ref[:, w:], across_row(l, w, width))
            if w < top:
                p = p - half(mm(ec_ref[:, w:top], k_ref[pair, base + w : base + top, :]), l)
        inverse = inv_ref[l]
        d_ref[:, l * hd : (l + 1) * hd] = (inverse * p).astype(jnp.bfloat16)
        c = c_ref[:, l * hd : (l + 1) * hd].astype(jnp.float32)
        ec_ref[:, l * hd : (l + 1) * hd] = (pull * c).astype(jnp.bfloat16)
        correction = jnp.sum(p * a_ref[l], axis=1, keepdims=True) / features
        pull = pull + inverse * inverse * inverse * correction

    below = layer_mask(block, block, hd, lambda r, c: r > c)
    upto_diag = layer_mask(block, block, hd, lambda r, c: r >= c)
    blocks = width // block
    for bl in range(blocks):
        mine = pl.ds(bl * block, block)
        c_t = c_ref[:, mine].T
        d_t = d_ref[:, mine].T
        ec_t = ec_ref[:, mine].T
        y = mm(d_t, x_ref[...])
        z = mm(c_t, s_ref[...]) - mm(ec_t, x_ref[...])
        for bk in range(blocks):
            other = pl.ds(bk * block, block)
            u_k = u_ref[other, :]
            if bk <= bl:
                m = mm(d_t, c_ref[:, other])
                if bk == bl:
                    m = jnp.where(below, m, 0.0)
                y = y + mm(m.astype(jnp.bfloat16), u_k)
            if bk >= bl:
                m = mm(c_t, d_ref[:, other])
                if bk == bl:
                    m = jnp.where(upto_diag, 0.0, m)
                z = z + mm(m.astype(jnp.bfloat16), v_ref[other, :])
            if bk < bl:
                m = mm(ec_t, c_ref[:, other])
            elif bk > bl:
                m = mm(c_t, ec_ref[:, other])
            else:
                m = jnp.where(upto_diag, mm(ec_t, c_ref[:, other]), mm(c_t, ec_ref[:, other]))
            z = z - mm(m.astype(jnp.bfloat16), u_k)
        y = y.astype(jnp.bfloat16)
        z = z.astype(jnp.bfloat16)
        for j in range(block // hd):
            l = bl * (block // hd) + j
            y_l, z_l = y[j * hd : (j + 1) * hd], z[j * hd : (j + 1) * hd]
            at = turned_index(l, layers)
            small = q_ref[at, :, 2 * cols : 2 * cols + 2 * hd]
            out_ref[at, :, :cols] = (adapter_scale * mm(small[:, :hd], y_l)).astype(jnp.bfloat16)
            out_ref[at, :, cols : 2 * cols] = (adapter_scale * mm(small[:, hd:], z_l)).astype(
                jnp.bfloat16
            )
            tail = jnp.concatenate(
                [mm_nt(q_ref[at, :, :cols], y_l), mm_nt(q_ref[at, :, cols : 2 * cols], z_l)], axis=1
            )
            out_ref[at, :, 2 * cols :] = (adapter_scale * tail).astype(jnp.bfloat16)


def params(limit=vmem_bytes):
    return pltpu.CompilerParams(vmem_limit_bytes=limit)


def in_vmem(count):
    return [pl.BlockSpec(memory_space=pltpu.VMEM)] * count


def in_smem(count):
    return [pl.BlockSpec(memory_space=pltpu.SMEM)] * count


def store(sizes, members, arrays):
    layers, hd, rank, tokens, cols = sizes
    return pl.pallas_call(
        functools.partial(store_kernel, sizes),
        out_shape=jax.ShapeDtypeStruct((members, rank, 2 * cols + 2 * hd), jnp.bfloat16),
        in_specs=in_vmem(len(arrays)),
        out_specs=in_vmem(1)[0],
        compiler_params=params(whole_vmem_bytes),
    )(*arrays)


def spread_lines(sizes, side, scalars, arrays):
    layers, hd, rank, tokens, cols = sizes
    line = jax.ShapeDtypeStruct((layers // side, hd + 2 * (tokens // layers), cols), jnp.bfloat16)
    return pl.pallas_call(
        functools.partial(lines_kernel, sizes),
        out_shape=(line,) * side,
        in_specs=in_smem(len(scalars)) + in_vmem(len(arrays)),
        out_specs=tuple(in_vmem(side)),
        compiler_params=params(),
    )(*scalars, *arrays)


def pick_rows(scalars, parts, lines):
    side = len(lines)
    across = lines[0].shape[0]
    turned = jax.ShapeDtypeStruct((side,) + lines[0].shape[1:], jnp.bfloat16)
    return pl.pallas_call(
        functools.partial(pick_kernel, side, across),
        out_shape=(jax.ShapeDtypeStruct(parts.shape, parts.dtype),) + (turned,) * across,
        in_specs=in_smem(len(scalars)) + in_vmem(1 + side),
        out_specs=tuple(in_vmem(1 + across)),
        compiler_params=params(),
    )(*scalars, parts, *lines)


def relay_kernel(*refs):
    pass


def relay(value, after):
    return pl.pallas_call(
        relay_kernel,
        out_shape=jax.ShapeDtypeStruct(value.shape, value.dtype),
        in_specs=[pl.BlockSpec(memory_space=pl.ANY)] * (1 + len(after)),
        out_specs=pl.BlockSpec(memory_space=pl.ANY),
        input_output_aliases={0: 0},
    )(value, *after)


def finish(sizes, owned, gain):
    layers, hd, rank, tokens, cols = sizes
    wide = jax.ShapeDtypeStruct((rank, layers * cols), jnp.bfloat16)
    narrow = jax.ShapeDtypeStruct((rank, hd), jnp.bfloat16)
    return pl.pallas_call(
        functools.partial(finish_kernel, sizes),
        out_shape=(wide, narrow, narrow, wide),
        in_specs=in_vmem(2),
        out_specs=tuple(in_vmem(4)),
        compiler_params=params(),
    )(owned, gain)


def gram(sizes, side, here, own, other, q):
    layers, hd, rank, tokens, cols = sizes
    width = layers * hd
    share = jax.ShapeDtypeStruct(
        (width // (4 * hd), 3 * tokens + width - hd, 2 * hd), jnp.bfloat16
    )
    return pl.pallas_call(
        functools.partial(gram_kernel, sizes, side, len(own)),
        out_shape=(
            jax.ShapeDtypeStruct((width, cols), jnp.bfloat16),
            jax.ShapeDtypeStruct((width, cols), jnp.bfloat16),
            jax.ShapeDtypeStruct((tokens, cols), jnp.bfloat16),
            jax.ShapeDtypeStruct((tokens, cols), jnp.bfloat16),
            share,
            share,
        ),
        in_specs=in_smem(1) + in_vmem(len(own) + len(other) + 1),
        out_specs=tuple(in_vmem(6)),
        scratch_shapes=[
            pltpu.VMEM((tokens, cols), jnp.float32),
            pltpu.VMEM((tokens, cols), jnp.float32),
            pltpu.VMEM((2, 2, hd, cols), jnp.float32),
        ],
        compiler_params=params(),
    )(here, *own, *other, q)


def solve(sizes, features, here, own, other, x, s, u, v, q):
    layers, hd, rank, tokens, cols = sizes
    width = layers * hd
    return pl.pallas_call(
        functools.partial(solve_kernel, sizes, features),
        out_shape=jax.ShapeDtypeStruct(q.shape, jnp.bfloat16),
        in_specs=in_smem(1) + [pl.BlockSpec(memory_space=pl.ANY)] * 2 + in_vmem(5),
        out_specs=in_vmem(1)[0],
        scratch_shapes=[
            pltpu.VMEM((tokens, width), jnp.bfloat16),
            pltpu.VMEM((tokens, width), jnp.bfloat16),
            pltpu.VMEM((tokens, width), jnp.bfloat16),
            pltpu.VMEM((layers, tokens, hd), jnp.float32),
            pltpu.VMEM((layers, tokens, hd), jnp.float32),
            pltpu.VMEM((layers, tokens, 1), jnp.float32),
            pltpu.VMEM((2 * own.shape[0],) + own.shape[1:], jnp.bfloat16),
            pltpu.SemaphoreType.DMA((2,)),
        ],
        compiler_params=params(),
    )(here, own, other, x, s, u, v, q)


def swap(value, axis):
    return lax.all_to_all(value, axis, split_axis=0, concat_axis=0, tiled=True)


def pick(chooser, parts):
    flat = parts.reshape(parts.shape[0], -1)
    return mm(chooser, flat).astype(jnp.bfloat16).reshape((chooser.shape[0],) + parts.shape[1:])


def body(
    inputs,
    cotangent,
    norm_gain,
    w_value,
    w_out,
    value_down,
    value_up_factor,
    out_down,
    output_up_factor,
    block_tenant,
    valid_tokens,
    tenant_slot,
):
    section, sections = lax.axis_index(pipe), lax.axis_size(pipe)
    member, members = lax.axis_index(dp), lax.axis_size(dp)
    rows, features = inputs.shape[1], inputs.shape[2]
    hd, rank = w_value.shape[1], value_down.shape[2]
    cols = features // sections
    tokens = rows * sections
    sizes = (sections, hd, rank, tokens, cols)
    side = lax.axis_size("a") * lax.axis_size("b")
    across = lax.axis_size("x")
    planes = lax.axis_size("z")
    here = jnp.stack([section, member]).astype(jnp.int32)
    gain = norm_gain
    both_cores = [(0, 1), (1, 0)]

    stored = store(
        sizes,
        members,
        (value_down[0, 0], output_up_factor[0, 0], gain, value_up_factor[0, 0], out_down[0, 0]),
    )
    lines = spread_lines(
        sizes,
        side,
        (here, block_tenant, valid_tokens),
        (
            w_value[0],
            w_out[0],
            gain,
            inputs[0],
            cotangent[0],
            lax.ppermute(inputs[0], "core", both_cores),
            lax.ppermute(cotangent[0], "core", both_cores),
        ),
    )
    lines = [lines[0]] + [
        lax.ppermute(lines[step], ("a", "b"), [(i, (i + step) % side) for i in range(side)])
        for step in range(1, side)
    ]
    adapters, *turned = pick_rows((here, block_tenant, tenant_slot), swap(stored, dp), lines)
    turned = [turned[0]] + [
        lax.ppermute(turned[step], "x", [(i, (i + step) % across) for i in range(across)])
        for step in range(1, across)
    ]
    adapters = swap(relay(swap(adapters, "z"), turned[1:]), ("b", "x", "a"))
    pairs = across // 2
    other = [
        lax.ppermute(
            jnp.concatenate([part[:, :hd] for part in turned[at : at + pairs]], axis=0),
            "z",
            [(i, (i + turn) % planes) for i in range(planes)],
        )
        for at, turn in ((0, 1), (pairs, -1))
    ]

    u, v, x, s, kept, given = gram(sizes, side, here, turned, other, adapters)
    theirs = lax.ppermute(given, "core", both_cores)
    summed = (kept.astype(jnp.float32) + theirs.astype(jnp.float32)).astype(jnp.bfloat16)
    shares = swap(summed.reshape(sections // 2, -1, summed.shape[-1]), ("b", "x"))
    share = jnp.sum(shares.astype(jnp.float32), axis=0).astype(jnp.bfloat16)
    own = swap(jnp.broadcast_to(share[None], shares.shape), ("b", "x")).reshape(summed.shape)
    other = lax.ppermute(own, "core", both_cores)

    grads = solve(sizes, features, here, own, other, x, s, u, v, adapters)

    ids = jnp.arange(members, dtype=jnp.int32)
    tenant_hot = block_tenant[:, None] == ids[None, :]
    slot_of = jnp.sum(jnp.where(tenant_hot, tenant_slot[None, :], 0), axis=1)
    slot_hot = (ids[:, None] == slot_of[None, :]).astype(jnp.bfloat16)
    by_member = swap(swap(grads, ("b", "x", "a")), "z")
    owned = swap(pick(slot_hot, by_member), dp)
    return tuple(part[None, None] for part in finish(sizes, owned, gain))


def solution(mesh):
    sections, members = mesh.devices.shape
    finer = jax.sharding.Mesh(
        mesh.devices.reshape(2, 2, sections // 4, members // 2, 2), pipe + dp
    )
    return jax.shard_map(
        body,
        mesh=finer,
        in_specs=(
            P(pipe, dp, None),
            P(pipe, dp, None),
            P(pipe, None),
            P(pipe, None, None),
            P(pipe, None, None),
            P(pipe, dp, None, None),
            P(pipe, dp, None, None),
            P(pipe, dp, None, None),
            P(pipe, dp, None, None),
            P(),
            P(),
            P(),
        ),
        out_specs=(
            P(pipe, dp, None, None),
            P(pipe, dp, None, None),
            P(pipe, dp, None, None),
            P(pipe, dp, None, None),
        ),
        check_vma=False,
    )
```

```python
import functools

import jax
import jax.numpy as jnp
from jax import lax
from jax.experimental import pallas as pl
from jax.experimental.pallas import tpu as pltpu
from jax.sharding import PartitionSpec as P

adapter_scale = 2.0
norm_eps = 1e-05
block = 256
vmem_bytes = 20 * 1024 * 1024
whole_vmem_bytes = 56 * 1024 * 1024
pipe = ("a", "b", "x")
dp = ("z", "core")


def mm(left, right):
    return lax.dot_general(
        left, right, (((1,), (0,)), ((), ())), preferred_element_type=jnp.float32
    )


def mm_nt(left, right):
    return lax.dot_general(
        left, right, (((1,), (1,)), ((), ())), preferred_element_type=jnp.float32
    )


def mm_tn(left, right):
    return lax.dot_general(
        left, right, (((0,), (0,)), ((), ())), preferred_element_type=jnp.float32
    )


def layer_mask(rows, columns, hd, compare):
    row_layer = lax.broadcasted_iota(jnp.int32, (rows, columns), 0) // hd
    column_layer = lax.broadcasted_iota(jnp.int32, (rows, columns), 1) // hd
    return compare(row_layer, column_layer)


def pack_kernel(
    sizes, here_ref, wv_ref, wo_ref, gain_ref, vd_ref, ou_ref, vu_ref, od_ref, stored_ref, *out_refs
):
    layers, hd, rank, tokens, cols = sizes
    small = jnp.concatenate([vu_ref[...], od_ref[...]], axis=1)
    for k in range(stored_ref.shape[0]):
        at = pl.ds(k * cols, cols)
        stored_ref[k, :, :cols] = (vd_ref[:, at].astype(jnp.float32) * gain_ref[:, at]).astype(
            jnp.bfloat16
        )
        stored_ref[k, :, cols : 2 * cols] = ou_ref[:, at]
        stored_ref[k, :, 2 * cols :] = small
    part = hd // 2
    section, member = here_ref[0], here_ref[1]
    core = lax.rem(member, 2)
    side = len(out_refs)
    across = layers // side
    mine = pl.ds(pl.multiple_of(lax.rem(member // 2, 2) * part, part), part)
    for step, out_ref in enumerate(out_refs):
        line = lax.rem(section // across + step, side)
        for k in range(across):
            column = (lax.rem(line, side // 2) * across + k) * 2 + core
            at = pl.ds(pl.multiple_of(column * cols, cols), cols)
            out_ref[k, :part, :] = (wv_ref[mine, at].astype(jnp.float32) * gain_ref[:, at]).astype(
                jnp.bfloat16
            )
            out_ref[k, part:, :] = wo_ref[mine, at]


def join_kernel(
    sizes,
    here_ref,
    tenant_ref,
    valid_ref,
    parts_ref,
    x_ref,
    cot_ref,
    other_x_ref,
    other_cot_ref,
    *refs
):
    out_ref = refs[-1]
    layers, hd, rank, tokens, cols = sizes
    rows = tokens // layers
    section, member = here_ref[0], here_ref[1]
    core = lax.rem(member, 2)
    position = section * rows + lax.broadcasted_iota(jnp.int32, (rows, 1), 0)
    width = 2 * cols + 2 * hd

    def token_weight(index):
        total = jnp.int32(0)
        for i in range(tenant_ref.shape[0]):
            total = total + jnp.where(tenant_ref[i] == tenant_ref[index], valid_ref[i], 0)
        kept = jnp.where(position < valid_ref[index], 1.0, 0.0).astype(jnp.float32)
        return kept / jnp.full((rows, 1), total, jnp.int32).astype(jnp.float32)

    own_weight = token_weight(member)
    other_weight = token_weight(member + 1 - 2 * core)
    for k in range(layers // 2):
        at = pl.ds(pl.multiple_of((2 * k + core) * cols, cols), cols)
        own_x = x_ref[:, at].astype(jnp.float32)
        other_x = other_x_ref[:, at].astype(jnp.float32)
        own_seed = cot_ref[:, at].astype(jnp.float32) * own_weight
        other_seed = other_cot_ref[:, at].astype(jnp.float32) * other_weight
        for a in range(2):
            own = core == a
            out_ref[2 * k + a, :, :width] = parts_ref[2 * k + a]
            out_ref[2 * k + a, :, width:] = jnp.concatenate(
                [jnp.where(own, own_x, other_x), jnp.where(own, own_seed, other_seed)], axis=0
            ).astype(jnp.bfloat16)


def pick_kernel(side, across, here_ref, tenant_ref, slot_ref, parts_ref, *refs):
    lines, out_ref, turned = refs[:side], refs[side], refs[side + 1 :]
    for j in range(out_ref.shape[0]):
        out_ref[j] = parts_ref[slot_ref[tenant_ref[j]]]
    place = lax.rem(here_ref[0], across)
    for step, turned_ref in enumerate(turned):
        at = lax.rem(place + step, across)
        for k in range(side):
            turned_ref[k] = lines[k][at]


def finish_kernel(sizes, owned_ref, gain_ref, gvd_ref, gvu_ref, god_ref, gou_ref):
    layers, hd, rank, tokens, cols = sizes
    tail = jnp.zeros((rank, 2 * hd), jnp.float32)
    for c in range(layers):
        at = pl.ds(c * cols, cols)
        gvd_ref[:, at] = (owned_ref[c, :, :cols].astype(jnp.float32) * gain_ref[:, at]).astype(
            jnp.bfloat16
        )
        gou_ref[:, at] = owned_ref[c, :, cols : 2 * cols]
        tail = tail + owned_ref[c, :, 2 * cols :].astype(jnp.float32)
    gvu_ref[...] = tail[:, :hd].astype(jnp.bfloat16)
    god_ref[...] = tail[:, hd:].astype(jnp.bfloat16)


def turned_index(l, layers):
    return l % (layers // 2) * 2 + l // (layers // 2)


def gram_kernel(sizes, side, across, here_ref, *refs):
    layers, hd, rank, tokens, cols = sizes
    own_refs, other_refs, refs = refs[:across], refs[across : across + 2], refs[across + 2 :]
    pairs = across // 2
    q_ref, u_ref, v_ref, xs_ref, keep_ref, give_ref, x_wide, s_wide, w_wide = refs
    rows = tokens // layers
    part = hd // 2
    section, core = here_ref[0], lax.rem(here_ref[1], 2)
    plane = lax.rem(here_ref[1] // 2, 2)
    line, place = section // across, lax.rem(section, across)
    mine = pl.ds(pl.multiple_of(plane * part, part), part)
    theirs = pl.ds(pl.multiple_of((1 - plane) * part, part), part)
    for step in range(layers):
        dx, dy = step // side, step % side
        l = lax.rem(line + side - dy, side) * across + lax.rem(place + across - dx, across)
        slot = step % 2
        for kind in range(2):
            at = pl.ds(kind * part, part)
            w_wide[slot, kind, mine, :] = own_refs[dx][dy, at, :].astype(jnp.float32)
            w_wide[slot, kind, theirs, :] = other_refs[dx // pairs][
                dx % pairs * side + dy, at, :
            ].astype(jnp.float32)
        q_l = q_ref[turned_index(l, layers)]
        small = q_l[:, 2 * cols : 2 * cols + 2 * hd]
        delta_v = mm_tn(small[:, :hd], q_l[:, :cols])
        delta_u = mm_tn(small[:, hd:], q_l[:, cols : 2 * cols])
        at = pl.ds(pl.multiple_of(l * hd, hd), hd)
        v_ref[at, :] = (w_wide[slot, 0] + adapter_scale * delta_v).astype(jnp.bfloat16)
        u_ref[at, :] = (w_wide[slot, 1] + adapter_scale * delta_u).astype(jnp.bfloat16)
        both = q_l[:, 2 * cols + 2 * hd :].astype(jnp.float32)
        at = pl.ds(pl.multiple_of(l * rows, rows), rows)
        x_wide[at, :] = both[:rows]
        s_wide[at, :] = both[rows:]
    xs_ref[:tokens, :] = x_wide[...].astype(jnp.bfloat16)
    xs_ref[tokens:, :] = s_wide[...].astype(jnp.bfloat16)
    width = layers * hd
    base = 3 * tokens
    below = layer_mask(block, block, hd, lambda r, c: r < c)
    lane = 2 * hd
    half_count = width // lane // 2

    def put(own_core, start, column, value):
        value = value.astype(jnp.bfloat16)
        for at in range(0, value.shape[1], lane):
            index = (column + at) // lane
            out_ref = keep_ref if index // half_count == own_core else give_ref
            out_ref[index % half_count, pl.ds(start, value.shape[0]), :] = value[:, at : at + lane]

    def products(own_core):
        for bj in range(width // block):
            column = bj * block
            at_col = pl.ds(column, block)
            u_col, v_col = u_ref[at_col, :], v_ref[at_col, :]
            x_rows, s_rows = xs_ref[:tokens, :], xs_ref[tokens:, :]
            put(own_core, 0, column, mm_nt(x_rows, v_col))
            x_u = mm_nt(x_rows, u_col)
            if column + block == width:
                wide = x_wide[...]
                wide = wide * wide
                folded = wide[:, :lane]
                for at in range(lane, cols, lane):
                    folded = folded + wide[:, at : at + lane]
                x_u = jnp.concatenate([x_u[:, : block - hd], folded[:, :hd] + folded[:, hd:]], axis=1)
            put(own_core, tokens, column, x_u)
            put(own_core, 2 * tokens, column, mm_nt(s_rows, u_col))
            for bi in range(width // block):
                height = min(block, width - hd - bi * block)
                rows_at = pl.ds(bi * block, height)
                rows_u = u_ref[rows_at, :]
                if bi < bj:
                    part = mm_nt(rows_u, v_col)
                elif bi > bj:
                    part = mm_nt(rows_u, u_col)
                else:
                    part = jnp.where(below[:height], mm_nt(rows_u, v_col), mm_nt(rows_u, u_col))
                put(own_core, base + bi * block, column, part)

    for own_core in range(2):
        pl.when(core == own_core)(functools.partial(products, own_core))


def half(pair, l):
    hd = pair.shape[1] // 2
    return pair[:, hd:] if l % 2 else pair[:, :hd]


def solve_kernel(
    sizes,
    features,
    here_ref,
    own_ref,
    other_ref,
    xs_ref,
    u_ref,
    v_ref,
    q_ref,
    out_ref,
    c_ref,
    d_ref,
    ec_ref,
    a_ref,
    bp_ref,
    inv_ref,
    k_ref,
    sems,
):
    layers, hd, rank, tokens, cols = sizes
    width = layers * hd
    base = 3 * tokens
    half_count = own_ref.shape[0]
    core = lax.rem(here_ref[1], 2)
    for index in range(half_count):
        for source, place in ((own_ref, core), (other_ref, 1 - core)):
            to = place * half_count + index
            pltpu.make_async_copy(source.at[index], k_ref.at[to], sems.at[to]).start()

    def arrive(index):
        pltpu.make_async_copy(own_ref.at[0], k_ref.at[index], sems.at[index]).wait()

    c_ref[...] = jnp.zeros_like(c_ref)
    d_ref[...] = jnp.zeros_like(d_ref)
    ec_ref[...] = jnp.zeros_like(ec_ref)

    def upto(l):
        return 2 * hd * ((l + 1) // 2)

    def across_row(l, start, stop):
        rows_l = pl.ds(base + l * hd, hd)
        return jnp.concatenate(
            [k_ref[index, rows_l, :] for index in range(start // (2 * hd), stop // (2 * hd))],
            axis=1,
        )

    last = width // (2 * hd) - 1
    arrive(last)
    folded = k_ref[last, tokens : 2 * tokens, :].astype(jnp.float32)[:, hd:]
    square = jnp.sum(folded, axis=1, keepdims=True)
    for l in range(layers):
        pair = l // 2
        if l % 2 == 0 and pair < last:
            arrive(pair)
        a = half(k_ref[pair, :tokens, :], l).astype(jnp.float32)
        if l:
            w = upto(l)
            known = c_ref[:, :w]
            top = min(w, width - hd)
            a = a + half(mm(known[:, :top], k_ref[pair, base : base + top, :]), l)
        inverse = lax.rsqrt(jnp.maximum(square, 0.0) / features + norm_eps)
        c = (inverse * a).astype(jnp.bfloat16)
        c_ref[:, l * hd : (l + 1) * hd] = c
        a_ref[l] = a
        inv_ref[l] = inverse
        if l == layers - 1:
            break
        b = half(k_ref[pair, tokens : 2 * tokens, :], l).astype(jnp.float32)
        if l:
            b = b + mm_nt(known, across_row(l, 0, w))
        wide = c.astype(jnp.float32)
        after = b + half(mm(c, k_ref[pair, pl.ds(base + l * hd, hd), :]), l)
        square = square + jnp.sum(wide * (b + after), axis=1, keepdims=True)
        bp_ref[l] = after

    pull = jnp.zeros((tokens, 1), jnp.float32)
    for l in range(layers - 1, -1, -1):
        pair = l // 2
        p = half(k_ref[pair, 2 * tokens : 3 * tokens, :], l).astype(jnp.float32)
        if l < layers - 1:
            w = upto(l)
            top = width - hd
            p = p - pull * bp_ref[l]
            p = p + mm_nt(d_ref[:, w:], across_row(l, w, width))
            if w < top:
                p = p - half(mm(ec_ref[:, w:top], k_ref[pair, base + w : base + top, :]), l)
        inverse = inv_ref[l]
        d_ref[:, l * hd : (l + 1) * hd] = (inverse * p).astype(jnp.bfloat16)
        c = c_ref[:, l * hd : (l + 1) * hd].astype(jnp.float32)
        ec_ref[:, l * hd : (l + 1) * hd] = (pull * c).astype(jnp.bfloat16)
        correction = jnp.sum(p * a_ref[l], axis=1, keepdims=True) / features
        pull = pull + inverse * inverse * inverse * correction

    below = layer_mask(block, block, hd, lambda r, c: r > c)
    upto_diag = layer_mask(block, block, hd, lambda r, c: r >= c)
    group = block // hd
    diagonal = lax.broadcasted_iota(jnp.int32, (group * rank, block), 0) // rank == (
        lax.broadcasted_iota(jnp.int32, (group * rank, block), 1) // hd
    )

    def side_by_side(parts):
        return parts[0] if len(parts) == 1 else jnp.concatenate(parts, axis=1)

    def spread_diagonal(parts):
        tall = jnp.concatenate(parts, axis=0)
        return jnp.where(diagonal, side_by_side([tall] * group), jnp.zeros((), jnp.bfloat16))

    for start in range(0, width, block):
        stop = start + block
        mine = pl.ds(start, block)
        c_t = c_ref[:, mine].T
        d_t = d_ref[:, mine].T
        ec_t = ec_ref[:, mine].T

        m = [jnp.where(below, mm(d_t, c_ref[:, mine]), 0.0).astype(jnp.bfloat16)]
        if start:
            m = [mm(d_t, c_ref[:, :start]).astype(jnp.bfloat16)] + m
        y = mm(d_t, xs_ref[:tokens, :]) + mm(side_by_side(m), u_ref[:stop, :])

        m = [jnp.where(upto_diag, 0.0, mm(c_t, d_ref[:, mine])).astype(jnp.bfloat16)]
        if stop < width:
            m = m + [mm(c_t, d_ref[:, stop:]).astype(jnp.bfloat16)]
        z = mm(side_by_side([-ec_t, c_t]), xs_ref[...]) + mm(side_by_side(m), v_ref[start:, :])
        m = [
            jnp.where(upto_diag, mm(ec_t, c_ref[:, mine]), mm(c_t, ec_ref[:, mine])).astype(
                jnp.bfloat16
            )
        ]
        if start:
            m = [mm(ec_t, c_ref[:, :start]).astype(jnp.bfloat16)] + m
        if stop < width:
            m = m + [mm(c_t, ec_ref[:, stop:]).astype(jnp.bfloat16)]
        z = z - mm(side_by_side(m), u_ref[...])

        y = y.astype(jnp.bfloat16)
        z = z.astype(jnp.bfloat16)
        places = [turned_index(l, layers) for l in range(start // hd, stop // hd)]
        smalls = [q_ref[at, :, 2 * cols : 2 * cols + 2 * hd] for at in places]
        up = adapter_scale * mm(spread_diagonal([small[:, :hd] for small in smalls]), y)
        down = adapter_scale * mm(spread_diagonal([small[:, hd:] for small in smalls]), z)
        tail_y = mm_nt(jnp.concatenate([q_ref[at, :, :cols] for at in places], axis=0), y)
        tail_z = mm_nt(jnp.concatenate([q_ref[at, :, cols : 2 * cols] for at in places], axis=0), z)
        for j, at in enumerate(places):
            rows_j = slice(j * rank, (j + 1) * rank)
            out_ref[at, :, :cols] = up[rows_j].astype(jnp.bfloat16)
            out_ref[at, :, cols : 2 * cols] = down[rows_j].astype(jnp.bfloat16)
            tail = jnp.concatenate(
                [tail_y[rows_j, j * hd : (j + 1) * hd], tail_z[rows_j, j * hd : (j + 1) * hd]],
                axis=1,
            )
            out_ref[at, :, 2 * cols :] = (adapter_scale * tail).astype(jnp.bfloat16)


def params(limit=vmem_bytes):
    return pltpu.CompilerParams(vmem_limit_bytes=limit)


def in_vmem(count):
    return [pl.BlockSpec(memory_space=pltpu.VMEM)] * count


def in_smem(count):
    return [pl.BlockSpec(memory_space=pltpu.SMEM)] * count


def pack(sizes, side, members, here, arrays):
    layers, hd, rank, tokens, cols = sizes
    line = jax.ShapeDtypeStruct((layers // side, hd, cols), jnp.bfloat16)
    stored = jax.ShapeDtypeStruct((members, rank, 2 * cols + 2 * hd), jnp.bfloat16)
    return pl.pallas_call(
        functools.partial(pack_kernel, sizes),
        out_shape=(stored,) + (line,) * side,
        in_specs=in_smem(1) + in_vmem(len(arrays)),
        out_specs=tuple(in_vmem(1 + side)),
        compiler_params=params(whole_vmem_bytes),
    )(here, *arrays)


def pick_rows(scalars, parts, lines):
    side = len(lines)
    across = lines[0].shape[0]
    turned = jax.ShapeDtypeStruct((side,) + lines[0].shape[1:], jnp.bfloat16)
    return pl.pallas_call(
        functools.partial(pick_kernel, side, across),
        out_shape=(jax.ShapeDtypeStruct(parts.shape, parts.dtype),) + (turned,) * across,
        in_specs=in_smem(len(scalars)) + in_vmem(1 + side),
        out_specs=tuple(in_vmem(1 + across)),
        compiler_params=params(),
    )(*scalars, parts, *lines)


def join(sizes, scalars, parts, arrays, after):
    layers, hd, rank, tokens, cols = sizes
    return pl.pallas_call(
        functools.partial(join_kernel, sizes),
        out_shape=jax.ShapeDtypeStruct(parts.shape[:2] + (3 * cols + 2 * hd,), jnp.bfloat16),
        in_specs=in_smem(len(scalars))
        + in_vmem(1 + len(arrays))
        + [pl.BlockSpec(memory_space=pl.ANY)] * len(after),
        out_specs=in_vmem(1)[0],
        compiler_params=params(),
    )(*scalars, parts, *arrays, *after)


def finish(sizes, owned, gain):
    layers, hd, rank, tokens, cols = sizes
    wide = jax.ShapeDtypeStruct((rank, layers * cols), jnp.bfloat16)
    narrow = jax.ShapeDtypeStruct((rank, hd), jnp.bfloat16)
    return pl.pallas_call(
        functools.partial(finish_kernel, sizes),
        out_shape=(wide, narrow, narrow, wide),
        in_specs=in_vmem(2),
        out_specs=tuple(in_vmem(4)),
        compiler_params=params(),
    )(owned, gain)


def gram(sizes, side, here, own, other, q):
    layers, hd, rank, tokens, cols = sizes
    width = layers * hd
    share = jax.ShapeDtypeStruct(
        (width // (4 * hd), 3 * tokens + width - hd, 2 * hd), jnp.bfloat16
    )
    return pl.pallas_call(
        functools.partial(gram_kernel, sizes, side, len(own)),
        out_shape=(
            jax.ShapeDtypeStruct((width, cols), jnp.bfloat16),
            jax.ShapeDtypeStruct((width, cols), jnp.bfloat16),
            jax.ShapeDtypeStruct((2 * tokens, cols), jnp.bfloat16),
            share,
            share,
        ),
        in_specs=in_smem(1) + in_vmem(len(own) + len(other) + 1),
        out_specs=tuple(in_vmem(5)),
        scratch_shapes=[
            pltpu.VMEM((tokens, cols), jnp.float32),
            pltpu.VMEM((tokens, cols), jnp.float32),
            pltpu.VMEM((2, 2, hd, cols), jnp.float32),
        ],
        compiler_params=params(),
    )(here, *own, *other, q)


def solve(sizes, features, here, own, other, xs, u, v, q):
    layers, hd, rank, tokens, cols = sizes
    width = layers * hd
    return pl.pallas_call(
        functools.partial(solve_kernel, sizes, features),
        out_shape=jax.ShapeDtypeStruct(q.shape[:2] + (2 * cols + 2 * hd,), jnp.bfloat16),
        in_specs=in_smem(1) + [pl.BlockSpec(memory_space=pl.ANY)] * 2 + in_vmem(4),
        out_specs=in_vmem(1)[0],
        scratch_shapes=[
            pltpu.VMEM((tokens, width), jnp.bfloat16),
            pltpu.VMEM((tokens, width), jnp.bfloat16),
            pltpu.VMEM((tokens, width), jnp.bfloat16),
            pltpu.VMEM((layers, tokens, hd), jnp.float32),
            pltpu.VMEM((layers, tokens, hd), jnp.float32),
            pltpu.VMEM((layers, tokens, 1), jnp.float32),
            pltpu.VMEM((2 * own.shape[0],) + own.shape[1:], jnp.bfloat16),
            pltpu.SemaphoreType.DMA((2 * own.shape[0],)),
        ],
        compiler_params=params(),
    )(here, own, other, xs, u, v, q)


def swap(value, axis):
    return lax.all_to_all(value, axis, split_axis=0, concat_axis=0, tiled=True)


def pick(chooser, parts):
    flat = parts.reshape(parts.shape[0], -1)
    return mm(chooser, flat).astype(jnp.bfloat16).reshape((chooser.shape[0],) + parts.shape[1:])


def body(
    inputs,
    cotangent,
    norm_gain,
    w_value,
    w_out,
    value_down,
    value_up_factor,
    out_down,
    output_up_factor,
    block_tenant,
    valid_tokens,
    tenant_slot,
):
    section, sections = lax.axis_index(pipe), lax.axis_size(pipe)
    member, members = lax.axis_index(dp), lax.axis_size(dp)
    rows, features = inputs.shape[1], inputs.shape[2]
    hd, rank = w_value.shape[1], value_down.shape[2]
    cols = features // sections
    tokens = rows * sections
    sizes = (sections, hd, rank, tokens, cols)
    side = lax.axis_size("a") * lax.axis_size("b")
    across = lax.axis_size("x")
    planes = lax.axis_size("z")
    here = jnp.stack([section, member]).astype(jnp.int32)
    gain = norm_gain
    both_cores = [(0, 1), (1, 0)]

    stored, *lines = pack(
        sizes,
        side,
        members,
        here,
        (
            w_value[0],
            w_out[0],
            gain,
            value_down[0, 0],
            output_up_factor[0, 0],
            value_up_factor[0, 0],
            out_down[0, 0],
        ),
    )
    lines = [lines[0]] + [
        lax.ppermute(lines[step], ("a", "b"), [(i, (i + step) % side) for i in range(side)])
        for step in range(1, side)
    ]
    adapters, *turned = pick_rows((here, block_tenant, tenant_slot), swap(stored, dp), lines)
    turned = [turned[0]] + [
        lax.ppermute(turned[step], "x", [(i, (i + step) % across) for i in range(across)])
        for step in range(1, across)
    ]
    joined = join(
        sizes,
        (here, block_tenant, valid_tokens),
        swap(adapters, "z"),
        (
            inputs[0],
            cotangent[0],
            lax.ppermute(inputs[0], "core", both_cores),
            lax.ppermute(cotangent[0], "core", both_cores),
        ),
        turned[1:],
    )
    adapters = swap(joined, ("b", "x", "a"))
    pairs = across // 2
    other = [
        lax.ppermute(
            jnp.concatenate(turned[at : at + pairs], axis=0),
            "z",
            [(i, (i + turn) % planes) for i in range(planes)],
        )
        for at, turn in ((0, 1), (pairs, -1))
    ]

    u, v, rows_xs, kept, given = gram(sizes, side, here, turned, other, adapters)
    theirs = lax.ppermute(given, "core", both_cores)
    summed = (kept.astype(jnp.float32) + theirs.astype(jnp.float32)).astype(jnp.bfloat16)
    shares = swap(summed.reshape(sections // 2, -1, summed.shape[-1]), ("b", "x"))
    share = jnp.sum(shares.astype(jnp.float32), axis=0).astype(jnp.bfloat16)
    own = swap(jnp.broadcast_to(share[None], shares.shape), ("b", "x")).reshape(summed.shape)
    other = lax.ppermute(own, "core", both_cores)

    grads = solve(sizes, features, here, own, other, rows_xs, u, v, adapters)

    ids = jnp.arange(members, dtype=jnp.int32)
    tenant_hot = block_tenant[:, None] == ids[None, :]
    slot_of = jnp.sum(jnp.where(tenant_hot, tenant_slot[None, :], 0), axis=1)
    slot_hot = (ids[:, None] == slot_of[None, :]).astype(jnp.bfloat16)
    by_member = swap(swap(grads, ("b", "x", "a")), "z")
    owned = swap(pick(slot_hot, by_member), dp)
    return tuple(part[None, None] for part in finish(sizes, owned, gain))


def solution(mesh):
    sections, members = mesh.devices.shape
    finer = jax.sharding.Mesh(
        mesh.devices.reshape(2, 2, sections // 4, members // 2, 2), pipe + dp
    )
    return jax.shard_map(
        body,
        mesh=finer,
        in_specs=(
            P(pipe, dp, None),
            P(pipe, dp, None),
            P(pipe, None),
            P(pipe, None, None),
            P(pipe, None, None),
            P(pipe, dp, None, None),
            P(pipe, dp, None, None),
            P(pipe, dp, None, None),
            P(pipe, dp, None, None),
            P(),
            P(),
            P(),
        ),
        out_specs=(
            P(pipe, dp, None, None),
            P(pipe, dp, None, None),
            P(pipe, dp, None, None),
            P(pipe, dp, None, None),
        ),
        check_vma=False,
    )
```

```python
import functools

import jax
import jax.numpy as jnp
from jax import lax
from jax.experimental import pallas as pl
from jax.experimental.pallas import tpu as pltpu
from jax.sharding import PartitionSpec as P

adapter_scale = 2.0
norm_eps = 1e-05
block = 256
vmem_bytes = 20 * 1024 * 1024
whole_vmem_bytes = 56 * 1024 * 1024
merge_cost_bytes = 4 * 1024 * 1024
pipe = ("a", "b", "x")
dp = ("z", "core")


def mm(left, right):
    return lax.dot_general(
        left, right, (((1,), (0,)), ((), ())), preferred_element_type=jnp.float32
    )


def mm_nt(left, right):
    return lax.dot_general(
        left, right, (((1,), (1,)), ((), ())), preferred_element_type=jnp.float32
    )


def mm_tn(left, right):
    return lax.dot_general(
        left, right, (((0,), (0,)), ((), ())), preferred_element_type=jnp.float32
    )


def layer_mask(rows, columns, hd, compare):
    row_layer = lax.broadcasted_iota(jnp.int32, (rows, columns), 0) // hd
    column_layer = lax.broadcasted_iota(jnp.int32, (rows, columns), 1) // hd
    return compare(row_layer, column_layer)


def pack_kernel(
    sizes, here_ref, wv_ref, wo_ref, gain_ref, vd_ref, ou_ref, vu_ref, od_ref, stored_ref, *out_refs
):
    layers, hd, rank, tokens, cols = sizes
    small = jnp.concatenate([vu_ref[...], od_ref[...]], axis=1)
    for k in range(stored_ref.shape[0]):
        at = pl.ds(k * cols, cols)
        stored_ref[k, :, :cols] = (vd_ref[:, at].astype(jnp.float32) * gain_ref[:, at]).astype(
            jnp.bfloat16
        )
        stored_ref[k, :, cols : 2 * cols] = ou_ref[:, at]
        stored_ref[k, :, 2 * cols :] = small
    part = hd // 2
    section, member = here_ref[0], here_ref[1]
    core = lax.rem(member, 2)
    side = len(out_refs)
    across = layers // side
    mine = pl.ds(pl.multiple_of(lax.rem(member // 2, 2) * part, part), part)
    for step, out_ref in enumerate(out_refs):
        line = lax.rem(section // across + step, side)
        for k in range(across):
            column = (lax.rem(line, side // 2) * across + k) * 2 + core
            at = pl.ds(pl.multiple_of(column * cols, cols), cols)
            out_ref[k, :part, :] = (wv_ref[mine, at].astype(jnp.float32) * gain_ref[:, at]).astype(
                jnp.bfloat16
            )
            out_ref[k, part:, :] = wo_ref[mine, at]


def join_kernel(
    sizes,
    here_ref,
    tenant_ref,
    valid_ref,
    parts_ref,
    x_ref,
    cot_ref,
    other_x_ref,
    other_cot_ref,
    *refs
):
    out_ref = refs[-1]
    layers, hd, rank, tokens, cols = sizes
    rows = tokens // layers
    section, member = here_ref[0], here_ref[1]
    core = lax.rem(member, 2)
    position = section * rows + lax.broadcasted_iota(jnp.int32, (rows, 1), 0)
    width = 2 * cols + 2 * hd

    def token_weight(index):
        total = jnp.int32(0)
        for i in range(tenant_ref.shape[0]):
            total = total + jnp.where(tenant_ref[i] == tenant_ref[index], valid_ref[i], 0)
        kept = jnp.where(position < valid_ref[index], 1.0, 0.0).astype(jnp.float32)
        return kept / jnp.full((rows, 1), total, jnp.int32).astype(jnp.float32)

    own_weight = token_weight(member)
    other_weight = token_weight(member + 1 - 2 * core)
    for k in range(layers // 2):
        at = pl.ds(pl.multiple_of((2 * k + core) * cols, cols), cols)
        own_x = x_ref[:, at].astype(jnp.float32)
        other_x = other_x_ref[:, at].astype(jnp.float32)
        own_seed = cot_ref[:, at].astype(jnp.float32) * own_weight
        other_seed = other_cot_ref[:, at].astype(jnp.float32) * other_weight
        for a in range(2):
            own = core == a
            out_ref[2 * k + a, :, :width] = parts_ref[2 * k + a]
            out_ref[2 * k + a, :, width:] = jnp.concatenate(
                [jnp.where(own, own_x, other_x), jnp.where(own, own_seed, other_seed)], axis=0
            ).astype(jnp.bfloat16)


def pick_kernel(side, across, here_ref, tenant_ref, slot_ref, parts_ref, *refs):
    lines, out_ref, turned, sems = refs[:side], refs[side], refs[side + 1 : -1], refs[-1]
    place = lax.rem(here_ref[0], across)
    copies = [
        pltpu.make_async_copy(
            lines[0].at[lax.rem(place + step, across)], turned_ref.at[0], sems.at[step]
        )
        for step, turned_ref in enumerate(turned)
    ]
    for copy in copies:
        copy.start()
    for j in range(out_ref.shape[0]):
        out_ref[j] = parts_ref[slot_ref[tenant_ref[j]]]
    for step, turned_ref in enumerate(turned):
        at = lax.rem(place + step, across)
        for k in range(1, side):
            turned_ref[k] = lines[k][at]
    for copy in copies:
        copy.wait()


def finish_kernel(sizes, owned_ref, gain_ref, gvd_ref, gvu_ref, god_ref, gou_ref):
    layers, hd, rank, tokens, cols = sizes
    tail = jnp.zeros((rank, 2 * hd), jnp.float32)
    for c in range(layers):
        at = pl.ds(c * cols, cols)
        gvd_ref[:, at] = (owned_ref[c, :, :cols].astype(jnp.float32) * gain_ref[:, at]).astype(
            jnp.bfloat16
        )
        gou_ref[:, at] = owned_ref[c, :, cols : 2 * cols]
        tail = tail + owned_ref[c, :, 2 * cols :].astype(jnp.float32)
    gvu_ref[...] = tail[:, :hd].astype(jnp.bfloat16)
    god_ref[...] = tail[:, hd:].astype(jnp.bfloat16)


def turned_index(l, layers):
    return l % (layers // 2) * 2 + l // (layers // 2)


def merge_kernel(sizes, side, across, here_ref, *refs):
    layers, hd, rank, tokens, cols = sizes
    own_refs, other_refs, (u_ref, v_ref) = refs[:across], refs[across:-2], refs[-2:]
    pairs = across // 2
    part = hd // 2
    plane = lax.rem(here_ref[1] // 2, 2)
    line, place = here_ref[0] // across, lax.rem(here_ref[0], across)
    for step in range(layers):
        dx, dy = step // side, step % side
        l = lax.rem(line + side - dy, side) * across + lax.rem(place + across - dx, across)
        own, other = own_refs[dx][dy], other_refs[dx // pairs][dx % pairs * side + dy]
        mine = pl.ds(pl.multiple_of(l * hd + plane * part, part), part)
        theirs = pl.ds(pl.multiple_of(l * hd + (1 - plane) * part, part), part)
        v_ref[mine, :] = own[:part]
        u_ref[mine, :] = own[part:]
        v_ref[theirs, :] = other[:part]
        u_ref[theirs, :] = other[part:]


def gram_kernel(
    sizes,
    here_ref,
    wo_ref,
    wv_ref,
    q_ref,
    u_ref,
    v_ref,
    xs_ref,
    keep_ref,
    give_ref,
    x_wide,
    s_wide,
    sems,
):
    layers, hd, rank, tokens, cols = sizes
    rows = tokens // layers
    core = lax.rem(here_ref[1], 2)
    copies = [
        pltpu.make_async_copy(wo_ref, u_ref, sems.at[0]),
        pltpu.make_async_copy(wv_ref, v_ref, sems.at[1]),
    ]
    for copy in copies:
        copy.start()
    for l in range(layers):
        both = q_ref[turned_index(l, layers), :, 2 * cols + 2 * hd :].astype(jnp.float32)
        at = pl.ds(l * rows, rows)
        x_wide[at, :] = both[:rows]
        s_wide[at, :] = both[rows:]
    for copy in copies:
        copy.wait()
    for l in range(layers):
        q_l = q_ref[turned_index(l, layers)]
        small = q_l[:, 2 * cols : 2 * cols + 2 * hd]
        delta_v = mm_tn(small[:, :hd], q_l[:, :cols])
        delta_u = mm_tn(small[:, hd:], q_l[:, cols : 2 * cols])
        at = pl.ds(l * hd, hd)
        v_ref[at, :] = (v_ref[at, :].astype(jnp.float32) + adapter_scale * delta_v).astype(
            jnp.bfloat16
        )
        u_ref[at, :] = (u_ref[at, :].astype(jnp.float32) + adapter_scale * delta_u).astype(
            jnp.bfloat16
        )
    xs_ref[:tokens, :] = x_wide[...].astype(jnp.bfloat16)
    xs_ref[tokens:, :] = s_wide[...].astype(jnp.bfloat16)
    width = layers * hd
    base = 3 * tokens
    below = layer_mask(block, block, hd, lambda r, c: r < c)
    lane = 2 * hd
    half_count = width // lane // 2

    def put(own_core, start, column, value):
        value = value.astype(jnp.bfloat16)
        for at in range(0, value.shape[1], lane):
            index = (column + at) // lane
            out_ref = keep_ref if index // half_count == own_core else give_ref
            out_ref[index % half_count, pl.ds(start, value.shape[0]), :] = value[:, at : at + lane]

    def products(own_core):
        for bj in range(width // block):
            column = bj * block
            at_col = pl.ds(column, block)
            u_col, v_col = u_ref[at_col, :], v_ref[at_col, :]
            x_rows, s_rows = xs_ref[:tokens, :], xs_ref[tokens:, :]
            put(own_core, 0, column, mm_nt(x_rows, v_col))
            x_u = mm_nt(x_rows, u_col)
            if column + block == width:
                wide = x_wide[...]
                wide = wide * wide
                folded = wide[:, :lane]
                for at in range(lane, cols, lane):
                    folded = folded + wide[:, at : at + lane]
                x_u = jnp.concatenate([x_u[:, : block - hd], folded[:, :hd] + folded[:, hd:]], axis=1)
            put(own_core, tokens, column, x_u)
            put(own_core, 2 * tokens, column, mm_nt(s_rows, u_col))
            for bi in range(width // block):
                height = min(block, width - hd - bi * block)
                rows_at = pl.ds(bi * block, height)
                rows_u = u_ref[rows_at, :]
                if bi < bj:
                    part = mm_nt(rows_u, v_col)
                elif bi > bj:
                    part = mm_nt(rows_u, u_col)
                else:
                    part = jnp.where(below[:height], mm_nt(rows_u, v_col), mm_nt(rows_u, u_col))
                put(own_core, base + bi * block, column, part)

    for own_core in range(2):
        pl.when(core == own_core)(functools.partial(products, own_core))


def half(pair, l):
    hd = pair.shape[1] // 2
    return pair[:, hd:] if l % 2 else pair[:, :hd]


def solve_kernel(
    sizes,
    features,
    here_ref,
    own_ref,
    other_ref,
    xs_ref,
    u_ref,
    v_ref,
    q_ref,
    out_ref,
    c_ref,
    d_ref,
    ec_ref,
    a_ref,
    bp_ref,
    inv_ref,
    k_ref,
    sems,
):
    layers, hd, rank, tokens, cols = sizes
    width = layers * hd
    base = 3 * tokens
    half_count = own_ref.shape[0]
    core = lax.rem(here_ref[1], 2)
    for index in range(half_count):
        for source, place in ((own_ref, core), (other_ref, 1 - core)):
            to = place * half_count + index
            pltpu.make_async_copy(source.at[index], k_ref.at[to], sems.at[to]).start()

    def arrive(index):
        pltpu.make_async_copy(own_ref.at[0], k_ref.at[index], sems.at[index]).wait()

    c_ref[...] = jnp.zeros_like(c_ref)
    d_ref[...] = jnp.zeros_like(d_ref)
    ec_ref[...] = jnp.zeros_like(ec_ref)

    def upto(l):
        return 2 * hd * ((l + 1) // 2)

    def across_row(l, start, stop):
        rows_l = pl.ds(base + l * hd, hd)
        return jnp.concatenate(
            [k_ref[index, rows_l, :] for index in range(start // (2 * hd), stop // (2 * hd))],
            axis=1,
        )

    last = width // (2 * hd) - 1
    arrive(last)
    folded = k_ref[last, tokens : 2 * tokens, :].astype(jnp.float32)[:, hd:]
    square = jnp.sum(folded, axis=1, keepdims=True)
    for l in range(layers):
        pair = l // 2
        if l % 2 == 0 and pair < last:
            arrive(pair)
        a = half(k_ref[pair, :tokens, :], l).astype(jnp.float32)
        if l:
            w = upto(l)
            known = c_ref[:, :w]
            top = min(w, width - hd)
            a = a + half(mm(known[:, :top], k_ref[pair, base : base + top, :]), l)
        inverse = lax.rsqrt(jnp.maximum(square, 0.0) / features + norm_eps)
        c = (inverse * a).astype(jnp.bfloat16)
        c_ref[:, l * hd : (l + 1) * hd] = c
        a_ref[l] = a
        inv_ref[l] = inverse
        if l == layers - 1:
            break
        b = half(k_ref[pair, tokens : 2 * tokens, :], l).astype(jnp.float32)
        if l:
            b = b + mm_nt(known, across_row(l, 0, w))
        wide = c.astype(jnp.float32)
        after = b + half(mm(c, k_ref[pair, pl.ds(base + l * hd, hd), :]), l)
        square = square + jnp.sum(wide * (b + after), axis=1, keepdims=True)
        bp_ref[l] = after

    below = layer_mask(block, block, hd, lambda r, c: r > c)
    upto_diag = layer_mask(block, block, hd, lambda r, c: r >= c)
    group = block // hd
    diagonal = lax.broadcasted_iota(jnp.int32, (group * rank, block), 0) // rank == (
        lax.broadcasted_iota(jnp.int32, (group * rank, block), 1) // hd
    )

    def side_by_side(parts):
        return parts[0] if len(parts) == 1 else jnp.concatenate(parts, axis=1)

    def spread_diagonal(parts):
        tall = jnp.concatenate(parts, axis=0)
        return jnp.where(diagonal, side_by_side([tall] * group), jnp.zeros((), jnp.bfloat16))

    def weight_gradients(start):
        stop = start + block
        mine = pl.ds(start, block)
        c_t = c_ref[:, mine].T
        d_t = d_ref[:, mine].T
        ec_t = ec_ref[:, mine].T

        m = [jnp.where(below, mm(d_t, c_ref[:, mine]), 0.0).astype(jnp.bfloat16)]
        if start:
            m = [mm(d_t, c_ref[:, :start]).astype(jnp.bfloat16)] + m
        yield
        y = mm(d_t, xs_ref[:tokens, :]) + mm(side_by_side(m), u_ref[:stop, :])
        yield
        m = [jnp.where(upto_diag, 0.0, mm(c_t, d_ref[:, mine])).astype(jnp.bfloat16)]
        if stop < width:
            m = m + [mm(c_t, d_ref[:, stop:]).astype(jnp.bfloat16)]
        yield
        z = mm(side_by_side([-ec_t, c_t]), xs_ref[...]) + mm(side_by_side(m), v_ref[start:, :])
        yield
        m = [
            jnp.where(upto_diag, mm(ec_t, c_ref[:, mine]), mm(c_t, ec_ref[:, mine])).astype(
                jnp.bfloat16
            )
        ]
        if start:
            m = [mm(ec_t, c_ref[:, :start]).astype(jnp.bfloat16)] + m
        if stop < width:
            m = m + [mm(c_t, ec_ref[:, stop:]).astype(jnp.bfloat16)]
        yield
        z = z - mm(side_by_side(m), u_ref[...])
        yield
        y = y.astype(jnp.bfloat16)
        z = z.astype(jnp.bfloat16)
        places = [turned_index(l, layers) for l in range(start // hd, stop // hd)]
        smalls = [q_ref[at, :, 2 * cols : 2 * cols + 2 * hd] for at in places]
        up = adapter_scale * mm(spread_diagonal([small[:, :hd] for small in smalls]), y)
        down = adapter_scale * mm(spread_diagonal([small[:, hd:] for small in smalls]), z)
        tail_y = mm_nt(jnp.concatenate([q_ref[at, :, :cols] for at in places], axis=0), y)
        tail_z = mm_nt(jnp.concatenate([q_ref[at, :, cols : 2 * cols] for at in places], axis=0), z)
        for j, at in enumerate(places):
            rows_j = slice(j * rank, (j + 1) * rank)
            out_ref[at, :, :cols] = up[rows_j].astype(jnp.bfloat16)
            out_ref[at, :, cols : 2 * cols] = down[rows_j].astype(jnp.bfloat16)
            tail = jnp.concatenate(
                [tail_y[rows_j, j * hd : (j + 1) * hd], tail_z[rows_j, j * hd : (j + 1) * hd]],
                axis=1,
            )
            out_ref[at, :, 2 * cols :] = (adapter_scale * tail).astype(jnp.bfloat16)

    pull = jnp.zeros((tokens, 1), jnp.float32)
    pending = iter(())
    for l in range(layers - 1, -1, -1):
        pair = l // 2
        p = half(k_ref[pair, 2 * tokens : 3 * tokens, :], l).astype(jnp.float32)
        if l < layers - 1:
            w = upto(l)
            top = width - hd
            p = p - pull * bp_ref[l]
            p = p + mm_nt(d_ref[:, w:], across_row(l, w, width))
            if w < top:
                p = p - half(mm(ec_ref[:, w:top], k_ref[pair, base + w : base + top, :]), l)
        next(pending, None)
        inverse = inv_ref[l]
        d_ref[:, l * hd : (l + 1) * hd] = (inverse * p).astype(jnp.bfloat16)
        c = c_ref[:, l * hd : (l + 1) * hd].astype(jnp.float32)
        ec_ref[:, l * hd : (l + 1) * hd] = (pull * c).astype(jnp.bfloat16)
        correction = jnp.sum(p * a_ref[l], axis=1, keepdims=True) / features
        pull = pull + inverse * inverse * inverse * correction
        next(pending, None)
        if l * hd % block == 0:
            for _ in pending:
                pass
            pending = weight_gradients(l * hd)
    for _ in pending:
        pass


def params(limit=vmem_bytes):
    return pltpu.CompilerParams(vmem_limit_bytes=limit)


def in_vmem(count):
    return [pl.BlockSpec(memory_space=pltpu.VMEM)] * count


def in_smem(count):
    return [pl.BlockSpec(memory_space=pltpu.SMEM)] * count


def pack(sizes, side, members, here, arrays):
    layers, hd, rank, tokens, cols = sizes
    line = jax.ShapeDtypeStruct((layers // side, hd, cols), jnp.bfloat16)
    stored = jax.ShapeDtypeStruct((members, rank, 2 * cols + 2 * hd), jnp.bfloat16)
    return pl.pallas_call(
        functools.partial(pack_kernel, sizes),
        out_shape=(stored,) + (line,) * side,
        in_specs=in_smem(1) + in_vmem(len(arrays)),
        out_specs=tuple(in_vmem(1 + side)),
        compiler_params=params(whole_vmem_bytes),
    )(here, *arrays)


def pick_rows(scalars, parts, lines):
    side = len(lines)
    across = lines[0].shape[0]
    turned = jax.ShapeDtypeStruct((side,) + lines[0].shape[1:], jnp.bfloat16)
    return pl.pallas_call(
        functools.partial(pick_kernel, side, across),
        out_shape=(jax.ShapeDtypeStruct(parts.shape, parts.dtype),) + (turned,) * across,
        in_specs=in_smem(len(scalars))
        + in_vmem(1)
        + [pl.BlockSpec(memory_space=pl.ANY)]
        + in_vmem(side - 1),
        out_specs=tuple(in_vmem(1 + across)),
        scratch_shapes=[pltpu.SemaphoreType.DMA((across,))],
        compiler_params=params(),
    )(*scalars, parts, *lines)


def join(sizes, scalars, parts, arrays, after):
    layers, hd, rank, tokens, cols = sizes
    return pl.pallas_call(
        functools.partial(join_kernel, sizes),
        out_shape=jax.ShapeDtypeStruct(parts.shape[:2] + (3 * cols + 2 * hd,), jnp.bfloat16),
        in_specs=in_smem(len(scalars))
        + in_vmem(1 + len(arrays))
        + [pl.BlockSpec(memory_space=pl.ANY)] * len(after),
        out_specs=in_vmem(1)[0],
        compiler_params=params(),
    )(*scalars, parts, *arrays, *after)


def finish(sizes, owned, gain):
    layers, hd, rank, tokens, cols = sizes
    wide = jax.ShapeDtypeStruct((rank, layers * cols), jnp.bfloat16)
    narrow = jax.ShapeDtypeStruct((rank, hd), jnp.bfloat16)
    return pl.pallas_call(
        functools.partial(finish_kernel, sizes),
        out_shape=(wide, narrow, narrow, wide),
        in_specs=in_vmem(2),
        out_specs=tuple(in_vmem(4)),
        compiler_params=params(),
    )(owned, gain)


def merge(sizes, side, here, own, other):
    layers, hd, rank, tokens, cols = sizes
    table = jax.ShapeDtypeStruct((layers * hd, cols), jnp.bfloat16)
    return pl.pallas_call(
        functools.partial(merge_kernel, sizes, side, len(own)),
        out_shape=(table, table),
        in_specs=in_smem(1) + in_vmem(len(own) + len(other)),
        out_specs=tuple(in_vmem(2)),
        compiler_params=params(),
        cost_estimate=pl.CostEstimate(
            flops=0, bytes_accessed=merge_cost_bytes, transcendentals=0
        ),
    )(here, *own, *other)


def gram(sizes, here, w_out, w_value, q):
    layers, hd, rank, tokens, cols = sizes
    width = layers * hd
    share = jax.ShapeDtypeStruct(
        (width // (4 * hd), 3 * tokens + width - hd, 2 * hd), jnp.bfloat16
    )
    table = jax.ShapeDtypeStruct((width, cols), jnp.bfloat16)
    return pl.pallas_call(
        functools.partial(gram_kernel, sizes),
        out_shape=(
            table,
            table,
            jax.ShapeDtypeStruct((2 * tokens, cols), jnp.bfloat16),
            share,
            share,
        ),
        in_specs=in_smem(1) + [pl.BlockSpec(memory_space=pl.ANY)] * 2 + in_vmem(1),
        out_specs=tuple(in_vmem(5)),
        scratch_shapes=[
            pltpu.VMEM((tokens, cols), jnp.float32),
            pltpu.VMEM((tokens, cols), jnp.float32),
            pltpu.SemaphoreType.DMA((2,)),
        ],
        compiler_params=params(),
    )(here, w_out, w_value, q)


def solve(sizes, features, here, own, other, xs, u, v, q):
    layers, hd, rank, tokens, cols = sizes
    width = layers * hd
    return pl.pallas_call(
        functools.partial(solve_kernel, sizes, features),
        out_shape=jax.ShapeDtypeStruct(q.shape[:2] + (2 * cols + 2 * hd,), jnp.bfloat16),
        in_specs=in_smem(1) + [pl.BlockSpec(memory_space=pl.ANY)] * 2 + in_vmem(4),
        out_specs=in_vmem(1)[0],
        scratch_shapes=[
            pltpu.VMEM((tokens, width), jnp.bfloat16),
            pltpu.VMEM((tokens, width), jnp.bfloat16),
            pltpu.VMEM((tokens, width), jnp.bfloat16),
            pltpu.VMEM((layers, tokens, hd), jnp.float32),
            pltpu.VMEM((layers, tokens, hd), jnp.float32),
            pltpu.VMEM((layers, tokens, 1), jnp.float32),
            pltpu.VMEM((2 * own.shape[0],) + own.shape[1:], jnp.bfloat16),
            pltpu.SemaphoreType.DMA((2 * own.shape[0],)),
        ],
        compiler_params=params(),
    )(here, own, other, xs, u, v, q)


def swap(value, axis):
    return lax.all_to_all(value, axis, split_axis=0, concat_axis=0, tiled=True)


def pick(chooser, parts):
    flat = parts.reshape(parts.shape[0], -1)
    return mm(chooser, flat).astype(jnp.bfloat16).reshape((chooser.shape[0],) + parts.shape[1:])


def body(
    inputs,
    cotangent,
    norm_gain,
    w_value,
    w_out,
    value_down,
    value_up_factor,
    out_down,
    output_up_factor,
    block_tenant,
    valid_tokens,
    tenant_slot,
):
    section, sections = lax.axis_index(pipe), lax.axis_size(pipe)
    member, members = lax.axis_index(dp), lax.axis_size(dp)
    rows, features = inputs.shape[1], inputs.shape[2]
    hd, rank = w_value.shape[1], value_down.shape[2]
    cols = features // sections
    tokens = rows * sections
    sizes = (sections, hd, rank, tokens, cols)
    side = lax.axis_size("a") * lax.axis_size("b")
    across = lax.axis_size("x")
    planes = lax.axis_size("z")
    here = jnp.stack([section, member]).astype(jnp.int32)
    gain = norm_gain
    both_cores = [(0, 1), (1, 0)]

    stored, *lines = pack(
        sizes,
        side,
        members,
        here,
        (
            w_value[0],
            w_out[0],
            gain,
            value_down[0, 0],
            output_up_factor[0, 0],
            value_up_factor[0, 0],
            out_down[0, 0],
        ),
    )
    lines = [lines[0]] + [
        lax.ppermute(lines[step], ("a", "b"), [(i, (i + step) % side) for i in range(side)])
        for step in range(1, side)
    ]
    adapters, *turned = pick_rows((here, block_tenant, tenant_slot), swap(stored, dp), lines)
    turned = [turned[0]] + [
        lax.ppermute(turned[step], "x", [(i, (i + step) % across) for i in range(across)])
        for step in range(1, across)
    ]
    joined = join(
        sizes,
        (here, block_tenant, valid_tokens),
        swap(adapters, "z"),
        (
            inputs[0],
            cotangent[0],
            lax.ppermute(inputs[0], "core", both_cores),
            lax.ppermute(cotangent[0], "core", both_cores),
        ),
        turned[1:],
    )
    adapters = swap(joined, ("b", "x", "a"))
    pairs = across // 2
    other = [
        lax.ppermute(
            jnp.concatenate(turned[at : at + pairs], axis=0),
            "z",
            [(i, (i + turn) % planes) for i in range(planes)],
        )
        for at, turn in ((0, 1), (pairs, -1))
    ]

    u, v, rows_xs, kept, given = gram(
        sizes, here, *merge(sizes, side, here, turned, other), adapters
    )
    theirs = lax.ppermute(given, "core", both_cores)
    summed = (kept.astype(jnp.float32) + theirs.astype(jnp.float32)).astype(jnp.bfloat16)
    shares = swap(summed.reshape(sections // 2, -1, summed.shape[-1]), ("b", "x"))
    share = jnp.sum(shares.astype(jnp.float32), axis=0).astype(jnp.bfloat16)
    own = swap(jnp.broadcast_to(share[None], shares.shape), ("b", "x")).reshape(summed.shape)
    other = lax.ppermute(own, "core", both_cores)

    grads = solve(sizes, features, here, own, other, rows_xs, u, v, adapters)

    ids = jnp.arange(members, dtype=jnp.int32)
    tenant_hot = block_tenant[:, None] == ids[None, :]
    slot_of = jnp.sum(jnp.where(tenant_hot, tenant_slot[None, :], 0), axis=1)
    slot_hot = (ids[:, None] == slot_of[None, :]).astype(jnp.bfloat16)
    by_member = swap(swap(grads, ("b", "x", "a")), "z")
    owned = swap(pick(slot_hot, by_member), dp)
    return tuple(part[None, None] for part in finish(sizes, owned, gain))


def solution(mesh):
    sections, members = mesh.devices.shape
    finer = jax.sharding.Mesh(
        mesh.devices.reshape(2, 2, sections // 4, members // 2, 2), pipe + dp
    )
    return jax.shard_map(
        body,
        mesh=finer,
        in_specs=(
            P(pipe, dp, None),
            P(pipe, dp, None),
            P(pipe, None),
            P(pipe, None, None),
            P(pipe, None, None),
            P(pipe, dp, None, None),
            P(pipe, dp, None, None),
            P(pipe, dp, None, None),
            P(pipe, dp, None, None),
            P(),
            P(),
            P(),
        ),
        out_specs=(
            P(pipe, dp, None, None),
            P(pipe, dp, None, None),
            P(pipe, dp, None, None),
            P(pipe, dp, None, None),
        ),
        check_vma=False,
    )
```

```python
import functools

import jax
import jax.numpy as jnp
from jax import lax
from jax.experimental import pallas as pl
from jax.experimental.pallas import tpu as pltpu
from jax.sharding import PartitionSpec as P

adapter_scale = 2.0
norm_eps = 1e-05
block = 256
vmem_bytes = 20 * 1024 * 1024
whole_vmem_bytes = 56 * 1024 * 1024
merge_cost_bytes = 40 * 1024 * 1024
pipe = ("a", "b", "x")
dp = ("z", "core")


def mm(left, right):
    return lax.dot_general(
        left, right, (((1,), (0,)), ((), ())), preferred_element_type=jnp.float32
    )


def mm_nt(left, right):
    return lax.dot_general(
        left, right, (((1,), (1,)), ((), ())), preferred_element_type=jnp.float32
    )


def mm_tn(left, right):
    return lax.dot_general(
        left, right, (((0,), (0,)), ((), ())), preferred_element_type=jnp.float32
    )


def layer_mask(rows, columns, hd, compare):
    row_layer = lax.broadcasted_iota(jnp.int32, (rows, columns), 0) // hd
    column_layer = lax.broadcasted_iota(jnp.int32, (rows, columns), 1) // hd
    return compare(row_layer, column_layer)


def pack_kernel(
    sizes, here_ref, wv_ref, wo_ref, gain_ref, vd_ref, ou_ref, vu_ref, od_ref, stored_ref, *out_refs
):
    layers, hd, rank, tokens, cols = sizes
    small = jnp.concatenate([vu_ref[...], od_ref[...]], axis=1)
    for k in range(stored_ref.shape[0]):
        at = pl.ds(k * cols, cols)
        stored_ref[k, :, :cols] = (vd_ref[:, at].astype(jnp.float32) * gain_ref[:, at]).astype(
            jnp.bfloat16
        )
        stored_ref[k, :, cols : 2 * cols] = ou_ref[:, at]
        stored_ref[k, :, 2 * cols :] = small
    part = hd // 2
    section, member = here_ref[0], here_ref[1]
    core = lax.rem(member, 2)
    side = len(out_refs)
    across = layers // side
    mine = pl.ds(pl.multiple_of(lax.rem(member // 2, 2) * part, part), part)
    for step, out_ref in enumerate(out_refs):
        line = lax.rem(section // across + step, side)
        for k in range(across):
            column = (lax.rem(line, side // 2) * across + k) * 2 + core
            at = pl.ds(pl.multiple_of(column * cols, cols), cols)
            out_ref[k, :part, :] = (wv_ref[mine, at].astype(jnp.float32) * gain_ref[:, at]).astype(
                jnp.bfloat16
            )
            out_ref[k, part:, :] = wo_ref[mine, at]


def join_kernel(
    sizes,
    here_ref,
    tenant_ref,
    valid_ref,
    parts_ref,
    x_ref,
    cot_ref,
    other_x_ref,
    other_cot_ref,
    *refs
):
    out_ref = refs[-1]
    layers, hd, rank, tokens, cols = sizes
    rows = tokens // layers
    section, member = here_ref[0], here_ref[1]
    core = lax.rem(member, 2)
    position = section * rows + lax.broadcasted_iota(jnp.int32, (rows, 1), 0)
    width = 2 * cols + 2 * hd

    def token_weight(index):
        total = jnp.int32(0)
        for i in range(tenant_ref.shape[0]):
            total = total + jnp.where(tenant_ref[i] == tenant_ref[index], valid_ref[i], 0)
        kept = jnp.where(position < valid_ref[index], 1.0, 0.0).astype(jnp.float32)
        return kept / jnp.full((rows, 1), total, jnp.int32).astype(jnp.float32)

    own_weight = token_weight(member)
    other_weight = token_weight(member + 1 - 2 * core)
    for k in range(layers // 2):
        at = pl.ds(pl.multiple_of((2 * k + core) * cols, cols), cols)
        own_x = x_ref[:, at].astype(jnp.float32)
        other_x = other_x_ref[:, at].astype(jnp.float32)
        own_seed = cot_ref[:, at].astype(jnp.float32) * own_weight
        other_seed = other_cot_ref[:, at].astype(jnp.float32) * other_weight
        for a in range(2):
            own = core == a
            out_ref[2 * k + a, :, :width] = parts_ref[2 * k + a]
            out_ref[2 * k + a, :, width:] = jnp.concatenate(
                [jnp.where(own, own_x, other_x), jnp.where(own, own_seed, other_seed)], axis=0
            ).astype(jnp.bfloat16)


def pick_kernel(side, across, here_ref, tenant_ref, slot_ref, parts_ref, *refs):
    lines, out_ref, turned, sems = refs[:side], refs[side], refs[side + 1 : -1], refs[-1]
    place = lax.rem(here_ref[0], across)
    copies = [
        pltpu.make_async_copy(
            lines[0].at[lax.rem(place + step, across)], turned_ref.at[0], sems.at[step]
        )
        for step, turned_ref in enumerate(turned)
    ]
    for copy in copies:
        copy.start()
    for j in range(out_ref.shape[0]):
        out_ref[j] = parts_ref[slot_ref[tenant_ref[j]]]
    for step, turned_ref in enumerate(turned):
        at = lax.rem(place + step, across)
        for k in range(1, side):
            turned_ref[k] = lines[k][at]
    for copy in copies:
        copy.wait()


def finish_kernel(sizes, owned_ref, gain_ref, gvd_ref, gvu_ref, god_ref, gou_ref):
    layers, hd, rank, tokens, cols = sizes
    tail = jnp.zeros((rank, 2 * hd), jnp.float32)
    for c in range(layers):
        at = pl.ds(c * cols, cols)
        gvd_ref[:, at] = (owned_ref[c, :, :cols].astype(jnp.float32) * gain_ref[:, at]).astype(
            jnp.bfloat16
        )
        gou_ref[:, at] = owned_ref[c, :, cols : 2 * cols]
        tail = tail + owned_ref[c, :, 2 * cols :].astype(jnp.float32)
    gvu_ref[...] = tail[:, :hd].astype(jnp.bfloat16)
    god_ref[...] = tail[:, hd:].astype(jnp.bfloat16)


def turned_index(l, layers):
    return l % (layers // 2) * 2 + l // (layers // 2)


def merge_kernel(sizes, side, across, here_ref, *refs):
    layers, hd, rank, tokens, cols = sizes
    own_refs, other_refs, both_ref = refs[:across], refs[across:-1], refs[-1]
    pairs = across // 2
    part = hd // 2
    plane = lax.rem(here_ref[1] // 2, 2)
    line, place = here_ref[0] // across, lax.rem(here_ref[0], across)
    for step in range(layers):
        dx, dy = step // side, step % side
        l = lax.rem(line + side - dy, side) * across + lax.rem(place + across - dx, across)
        own, other = own_refs[dx][dy], other_refs[dx // pairs][dx % pairs * side + dy]
        mine = pl.ds(pl.multiple_of(l * hd + plane * part, part), part)
        theirs = pl.ds(pl.multiple_of(l * hd + (1 - plane) * part, part), part)
        both_ref[0, mine, :] = own[:part]
        both_ref[1, mine, :] = own[part:]
        both_ref[0, theirs, :] = other[:part]
        both_ref[1, theirs, :] = other[part:]


def gram_kernel(
    sizes,
    here_ref,
    both_ref,
    q_ref,
    u_ref,
    v_ref,
    xs_ref,
    give_ref,
    x_wide,
    s_wide,
    sems,
):
    layers, hd, rank, tokens, cols = sizes
    rows = tokens // layers
    core = lax.rem(here_ref[1], 2)
    copies = [
        pltpu.make_async_copy(both_ref.at[0], v_ref, sems.at[0]),
        pltpu.make_async_copy(both_ref.at[1], u_ref, sems.at[1]),
    ]
    for copy in copies:
        copy.start()
    for l in range(layers):
        both = q_ref[turned_index(l, layers), :, 2 * cols + 2 * hd :].astype(jnp.float32)
        at = pl.ds(l * rows, rows)
        x_wide[at, :] = both[:rows]
        s_wide[at, :] = both[rows:]
    for copy in copies:
        copy.wait()
    for l in range(layers):
        q_l = q_ref[turned_index(l, layers)]
        small = q_l[:, 2 * cols : 2 * cols + 2 * hd]
        delta_v = mm_tn(small[:, :hd], q_l[:, :cols])
        delta_u = mm_tn(small[:, hd:], q_l[:, cols : 2 * cols])
        at = pl.ds(l * hd, hd)
        v_ref[at, :] = (v_ref[at, :].astype(jnp.float32) + adapter_scale * delta_v).astype(
            jnp.bfloat16
        )
        u_ref[at, :] = (u_ref[at, :].astype(jnp.float32) + adapter_scale * delta_u).astype(
            jnp.bfloat16
        )
    xs_ref[:tokens, :] = x_wide[...].astype(jnp.bfloat16)
    xs_ref[tokens:, :] = s_wide[...].astype(jnp.bfloat16)
    for own_core in range(2):
        pl.when(core == own_core)(
            functools.partial(
                half_products, sizes, 1 - own_core, u_ref, v_ref, xs_ref, give_ref
            )
        )


def keep_kernel(sizes, here_ref, u_ref, v_ref, xs_ref, keep_ref):
    core = lax.rem(here_ref[1], 2)
    for own_core in range(2):
        pl.when(core == own_core)(
            functools.partial(half_products, sizes, own_core, u_ref, v_ref, xs_ref, keep_ref)
        )


def half_products(sizes, which, u_ref, v_ref, xs_ref, out_ref):
    layers, hd, rank, tokens, cols = sizes
    width = layers * hd
    base = 3 * tokens
    below = layer_mask(block, block, hd, lambda r, c: r < c)
    lane = 2 * hd
    count = width // block // 2

    def put(start, column, value):
        value = value.astype(jnp.bfloat16)
        for at in range(0, value.shape[1], lane):
            index = (column - which * count * block + at) // lane
            out_ref[index, pl.ds(start, value.shape[0]), :] = value[:, at : at + lane]

    x_rows, s_rows = xs_ref[:tokens, :], xs_ref[tokens:, :]
    for bj in range(which * count, which * count + count):
        column = bj * block
        at_col = pl.ds(column, block)
        u_col, v_col = u_ref[at_col, :], v_ref[at_col, :]
        put(0, column, mm_nt(x_rows, v_col))
        x_u = mm_nt(x_rows, u_col)
        if column + block == width:
            wide = x_rows.astype(jnp.float32)
            wide = wide * wide
            folded = wide[:, :lane]
            for at in range(lane, cols, lane):
                folded = folded + wide[:, at : at + lane]
            x_u = jnp.concatenate([x_u[:, : block - hd], folded[:, :hd] + folded[:, hd:]], axis=1)
        put(tokens, column, x_u)
        put(2 * tokens, column, mm_nt(s_rows, u_col))
        for bi in range(width // block):
            height = min(block, width - hd - bi * block)
            rows_at = pl.ds(bi * block, height)
            rows_u = u_ref[rows_at, :]
            if bi < bj:
                part = mm_nt(rows_u, v_col)
            elif bi > bj:
                part = mm_nt(rows_u, u_col)
            else:
                part = jnp.where(below[:height], mm_nt(rows_u, v_col), mm_nt(rows_u, u_col))
            put(base + bi * block, column, part)


def half(pair, l):
    hd = pair.shape[1] // 2
    return pair[:, hd:] if l % 2 else pair[:, :hd]


def solve_kernel(
    sizes,
    features,
    here_ref,
    own_ref,
    other_ref,
    xs_ref,
    u_ref,
    v_ref,
    q_ref,
    out_ref,
    c_ref,
    d_ref,
    ec_ref,
    a_ref,
    bp_ref,
    inv_ref,
    k_ref,
    sems,
):
    layers, hd, rank, tokens, cols = sizes
    width = layers * hd
    base = 3 * tokens
    half_count = own_ref.shape[0]
    core = lax.rem(here_ref[1], 2)
    for index in range(half_count):
        for source, place in ((own_ref, core), (other_ref, 1 - core)):
            to = place * half_count + index
            pltpu.make_async_copy(source.at[index], k_ref.at[to], sems.at[to]).start()

    def arrive(index):
        pltpu.make_async_copy(own_ref.at[0], k_ref.at[index], sems.at[index]).wait()

    c_ref[...] = jnp.zeros_like(c_ref)
    d_ref[...] = jnp.zeros_like(d_ref)
    ec_ref[...] = jnp.zeros_like(ec_ref)

    def upto(l):
        return 2 * hd * ((l + 1) // 2)

    def across_row(l, start, stop):
        rows_l = pl.ds(base + l * hd, hd)
        return jnp.concatenate(
            [k_ref[index, rows_l, :] for index in range(start // (2 * hd), stop // (2 * hd))],
            axis=1,
        )

    last = width // (2 * hd) - 1
    arrive(last)
    folded = k_ref[last, tokens : 2 * tokens, :].astype(jnp.float32)[:, hd:]
    square = jnp.sum(folded, axis=1, keepdims=True)
    for l in range(layers):
        pair = l // 2
        if l % 2 == 0 and pair < last:
            arrive(pair)
        a = half(k_ref[pair, :tokens, :], l).astype(jnp.float32)
        if l:
            w = upto(l)
            known = c_ref[:, :w]
            top = min(w, width - hd)
            a = a + half(mm(known[:, :top], k_ref[pair, base : base + top, :]), l)
        inverse = lax.rsqrt(jnp.maximum(square, 0.0) / features + norm_eps)
        c = (inverse * a).astype(jnp.bfloat16)
        c_ref[:, l * hd : (l + 1) * hd] = c
        a_ref[l] = a
        inv_ref[l] = inverse
        if l == layers - 1:
            break
        b = half(k_ref[pair, tokens : 2 * tokens, :], l).astype(jnp.float32)
        if l:
            b = b + mm_nt(known, across_row(l, 0, w))
        wide = c.astype(jnp.float32)
        after = b + half(mm(c, k_ref[pair, pl.ds(base + l * hd, hd), :]), l)
        square = square + jnp.sum(wide * (b + after), axis=1, keepdims=True)
        bp_ref[l] = after

    below = layer_mask(block, block, hd, lambda r, c: r > c)
    upto_diag = layer_mask(block, block, hd, lambda r, c: r >= c)
    group = block // hd
    diagonal = lax.broadcasted_iota(jnp.int32, (group * rank, block), 0) // rank == (
        lax.broadcasted_iota(jnp.int32, (group * rank, block), 1) // hd
    )

    def side_by_side(parts):
        return parts[0] if len(parts) == 1 else jnp.concatenate(parts, axis=1)

    def spread_diagonal(parts):
        tall = jnp.concatenate(parts, axis=0)
        return jnp.where(diagonal, side_by_side([tall] * group), jnp.zeros((), jnp.bfloat16))

    def weight_gradients(start):
        stop = start + block
        mine = pl.ds(start, block)
        c_t = c_ref[:, mine].T
        d_t = d_ref[:, mine].T
        ec_t = ec_ref[:, mine].T

        m = [jnp.where(below, mm(d_t, c_ref[:, mine]), 0.0).astype(jnp.bfloat16)]
        if start:
            m = [mm(d_t, c_ref[:, :start]).astype(jnp.bfloat16)] + m
        yield
        y = mm(d_t, xs_ref[:tokens, :]) + mm(side_by_side(m), u_ref[:stop, :])
        yield
        m = [jnp.where(upto_diag, 0.0, mm(c_t, d_ref[:, mine])).astype(jnp.bfloat16)]
        if stop < width:
            m = m + [mm(c_t, d_ref[:, stop:]).astype(jnp.bfloat16)]
        yield
        z = mm(side_by_side([-ec_t, c_t]), xs_ref[...]) + mm(side_by_side(m), v_ref[start:, :])
        yield
        m = [
            jnp.where(upto_diag, mm(ec_t, c_ref[:, mine]), mm(c_t, ec_ref[:, mine])).astype(
                jnp.bfloat16
            )
        ]
        if start:
            m = [mm(ec_t, c_ref[:, :start]).astype(jnp.bfloat16)] + m
        if stop < width:
            m = m + [mm(c_t, ec_ref[:, stop:]).astype(jnp.bfloat16)]
        yield
        z = z - mm(side_by_side(m), u_ref[...])
        yield
        y = y.astype(jnp.bfloat16)
        z = z.astype(jnp.bfloat16)
        places = [turned_index(l, layers) for l in range(start // hd, stop // hd)]
        smalls = [q_ref[at, :, 2 * cols : 2 * cols + 2 * hd] for at in places]
        up = adapter_scale * mm(spread_diagonal([small[:, :hd] for small in smalls]), y)
        down = adapter_scale * mm(spread_diagonal([small[:, hd:] for small in smalls]), z)
        tail_y = mm_nt(jnp.concatenate([q_ref[at, :, :cols] for at in places], axis=0), y)
        tail_z = mm_nt(jnp.concatenate([q_ref[at, :, cols : 2 * cols] for at in places], axis=0), z)
        for j, at in enumerate(places):
            rows_j = slice(j * rank, (j + 1) * rank)
            out_ref[at, :, :cols] = up[rows_j].astype(jnp.bfloat16)
            out_ref[at, :, cols : 2 * cols] = down[rows_j].astype(jnp.bfloat16)
            tail = jnp.concatenate(
                [tail_y[rows_j, j * hd : (j + 1) * hd], tail_z[rows_j, j * hd : (j + 1) * hd]],
                axis=1,
            )
            out_ref[at, :, 2 * cols :] = (adapter_scale * tail).astype(jnp.bfloat16)

    pull = jnp.zeros((tokens, 1), jnp.float32)
    pending = iter(())
    for l in range(layers - 1, -1, -1):
        pair = l // 2
        p = half(k_ref[pair, 2 * tokens : 3 * tokens, :], l).astype(jnp.float32)
        if l < layers - 1:
            w = upto(l)
            top = width - hd
            p = p - pull * bp_ref[l]
            p = p + mm_nt(d_ref[:, w:], across_row(l, w, width))
            if w < top:
                p = p - half(mm(ec_ref[:, w:top], k_ref[pair, base + w : base + top, :]), l)
        next(pending, None)
        inverse = inv_ref[l]
        d_ref[:, l * hd : (l + 1) * hd] = (inverse * p).astype(jnp.bfloat16)
        c = c_ref[:, l * hd : (l + 1) * hd].astype(jnp.float32)
        ec_ref[:, l * hd : (l + 1) * hd] = (pull * c).astype(jnp.bfloat16)
        correction = jnp.sum(p * a_ref[l], axis=1, keepdims=True) / features
        pull = pull + inverse * inverse * inverse * correction
        next(pending, None)
        if l * hd % block == 0:
            for _ in pending:
                pass
            pending = weight_gradients(l * hd)
    for _ in pending:
        pass


def params(limit=vmem_bytes):
    return pltpu.CompilerParams(vmem_limit_bytes=limit)


def in_vmem(count):
    return [pl.BlockSpec(memory_space=pltpu.VMEM)] * count


def in_smem(count):
    return [pl.BlockSpec(memory_space=pltpu.SMEM)] * count


def pack(sizes, side, members, here, arrays):
    layers, hd, rank, tokens, cols = sizes
    line = jax.ShapeDtypeStruct((layers // side, hd, cols), jnp.bfloat16)
    stored = jax.ShapeDtypeStruct((members, rank, 2 * cols + 2 * hd), jnp.bfloat16)
    return pl.pallas_call(
        functools.partial(pack_kernel, sizes),
        out_shape=(stored,) + (line,) * side,
        in_specs=in_smem(1) + in_vmem(len(arrays)),
        out_specs=tuple(in_vmem(1 + side)),
        compiler_params=params(whole_vmem_bytes),
    )(here, *arrays)


def pick_rows(scalars, parts, lines):
    side = len(lines)
    across = lines[0].shape[0]
    turned = jax.ShapeDtypeStruct((side,) + lines[0].shape[1:], jnp.bfloat16)
    return pl.pallas_call(
        functools.partial(pick_kernel, side, across),
        out_shape=(jax.ShapeDtypeStruct(parts.shape, parts.dtype),) + (turned,) * across,
        in_specs=in_smem(len(scalars))
        + in_vmem(1)
        + [pl.BlockSpec(memory_space=pl.ANY)]
        + in_vmem(side - 1),
        out_specs=tuple(in_vmem(1 + across)),
        scratch_shapes=[pltpu.SemaphoreType.DMA((across,))],
        compiler_params=params(),
    )(*scalars, parts, *lines)


def join(sizes, scalars, parts, arrays, after):
    layers, hd, rank, tokens, cols = sizes
    return pl.pallas_call(
        functools.partial(join_kernel, sizes),
        out_shape=jax.ShapeDtypeStruct(parts.shape[:2] + (3 * cols + 2 * hd,), jnp.bfloat16),
        in_specs=in_smem(len(scalars))
        + in_vmem(1 + len(arrays))
        + [pl.BlockSpec(memory_space=pl.ANY)] * len(after),
        out_specs=in_vmem(1)[0],
        compiler_params=params(),
    )(*scalars, parts, *arrays, *after)


def finish(sizes, owned, gain):
    layers, hd, rank, tokens, cols = sizes
    wide = jax.ShapeDtypeStruct((rank, layers * cols), jnp.bfloat16)
    narrow = jax.ShapeDtypeStruct((rank, hd), jnp.bfloat16)
    return pl.pallas_call(
        functools.partial(finish_kernel, sizes),
        out_shape=(wide, narrow, narrow, wide),
        in_specs=in_vmem(2),
        out_specs=tuple(in_vmem(4)),
        compiler_params=params(),
    )(owned, gain)


def merge(sizes, side, here, own, other):
    layers, hd, rank, tokens, cols = sizes
    return pl.pallas_call(
        functools.partial(merge_kernel, sizes, side, len(own)),
        out_shape=jax.ShapeDtypeStruct((2, layers * hd, cols), jnp.bfloat16),
        in_specs=in_smem(1) + in_vmem(len(own) + len(other)),
        out_specs=in_vmem(1)[0],
        compiler_params=params(),
        cost_estimate=pl.CostEstimate(
            flops=0, bytes_accessed=merge_cost_bytes, transcendentals=0
        ),
    )(here, *own, *other)


def gram(sizes, here, both, q):
    layers, hd, rank, tokens, cols = sizes
    width = layers * hd
    share = jax.ShapeDtypeStruct(
        (width // (4 * hd), 3 * tokens + width - hd, 2 * hd), jnp.bfloat16
    )
    table = jax.ShapeDtypeStruct((width, cols), jnp.bfloat16)
    return pl.pallas_call(
        functools.partial(gram_kernel, sizes),
        out_shape=(
            table,
            table,
            jax.ShapeDtypeStruct((2 * tokens, cols), jnp.bfloat16),
            share,
        ),
        in_specs=in_smem(1) + [pl.BlockSpec(memory_space=pl.ANY)] + in_vmem(1),
        out_specs=tuple(in_vmem(4)),
        scratch_shapes=[
            pltpu.VMEM((tokens, cols), jnp.float32),
            pltpu.VMEM((tokens, cols), jnp.float32),
            pltpu.SemaphoreType.DMA((2,)),
        ],
        compiler_params=params(),
    )(here, both, q)


def keep(sizes, here, u, v, xs, shape):
    return pl.pallas_call(
        functools.partial(keep_kernel, sizes),
        out_shape=jax.ShapeDtypeStruct(shape, jnp.bfloat16),
        in_specs=in_smem(1) + in_vmem(3),
        out_specs=in_vmem(1)[0],
        compiler_params=params(),
        cost_estimate=pl.CostEstimate(flops=1 << 31, bytes_accessed=1 << 22, transcendentals=0),
    )(here, u, v, xs)


def solve(sizes, features, here, own, other, xs, u, v, q):
    layers, hd, rank, tokens, cols = sizes
    width = layers * hd
    return pl.pallas_call(
        functools.partial(solve_kernel, sizes, features),
        out_shape=jax.ShapeDtypeStruct(q.shape[:2] + (2 * cols + 2 * hd,), jnp.bfloat16),
        in_specs=in_smem(1) + [pl.BlockSpec(memory_space=pl.ANY)] * 2 + in_vmem(4),
        out_specs=in_vmem(1)[0],
        scratch_shapes=[
            pltpu.VMEM((tokens, width), jnp.bfloat16),
            pltpu.VMEM((tokens, width), jnp.bfloat16),
            pltpu.VMEM((tokens, width), jnp.bfloat16),
            pltpu.VMEM((layers, tokens, hd), jnp.float32),
            pltpu.VMEM((layers, tokens, hd), jnp.float32),
            pltpu.VMEM((layers, tokens, 1), jnp.float32),
            pltpu.VMEM((2 * own.shape[0],) + own.shape[1:], jnp.bfloat16),
            pltpu.SemaphoreType.DMA((2 * own.shape[0],)),
        ],
        compiler_params=params(),
    )(here, own, other, xs, u, v, q)


def swap(value, axis):
    return lax.all_to_all(value, axis, split_axis=0, concat_axis=0, tiled=True)


def pick(chooser, parts):
    flat = parts.reshape(parts.shape[0], -1)
    return mm(chooser, flat).astype(jnp.bfloat16).reshape((chooser.shape[0],) + parts.shape[1:])


def body(
    inputs,
    cotangent,
    norm_gain,
    w_value,
    w_out,
    value_down,
    value_up_factor,
    out_down,
    output_up_factor,
    block_tenant,
    valid_tokens,
    tenant_slot,
):
    section, sections = lax.axis_index(pipe), lax.axis_size(pipe)
    member, members = lax.axis_index(dp), lax.axis_size(dp)
    rows, features = inputs.shape[1], inputs.shape[2]
    hd, rank = w_value.shape[1], value_down.shape[2]
    cols = features // sections
    tokens = rows * sections
    sizes = (sections, hd, rank, tokens, cols)
    side = lax.axis_size("a") * lax.axis_size("b")
    across = lax.axis_size("x")
    planes = lax.axis_size("z")
    here = jnp.stack([section, member]).astype(jnp.int32)
    gain = norm_gain
    both_cores = [(0, 1), (1, 0)]

    stored, *lines = pack(
        sizes,
        side,
        members,
        here,
        (
            w_value[0],
            w_out[0],
            gain,
            value_down[0, 0],
            output_up_factor[0, 0],
            value_up_factor[0, 0],
            out_down[0, 0],
        ),
    )
    lines = [lines[0]] + [
        lax.ppermute(lines[step], ("a", "b"), [(i, (i + step) % side) for i in range(side)])
        for step in range(1, side)
    ]
    adapters, *turned = pick_rows((here, block_tenant, tenant_slot), swap(stored, dp), lines)
    turned = [turned[0]] + [
        lax.ppermute(turned[step], "x", [(i, (i + step) % across) for i in range(across)])
        for step in range(1, across)
    ]
    joined = join(
        sizes,
        (here, block_tenant, valid_tokens),
        swap(adapters, "z"),
        (
            inputs[0],
            cotangent[0],
            lax.ppermute(inputs[0], "core", both_cores),
            lax.ppermute(cotangent[0], "core", both_cores),
        ),
        turned[1:],
    )
    adapters = swap(joined, ("b", "x", "a"))
    pairs = across // 2
    other = [
        lax.ppermute(
            jnp.concatenate(turned[at : at + pairs], axis=0),
            "z",
            [(i, (i + turn) % planes) for i in range(planes)],
        )
        for at, turn in ((0, 1), (pairs, -1))
    ]

    u, v, rows_xs, given = gram(
        sizes, here, merge(sizes, side, here, turned, other), adapters
    )
    theirs = lax.ppermute(given, "core", both_cores)
    kept = keep(sizes, here, u, v, rows_xs, given.shape)
    summed = (kept.astype(jnp.float32) + theirs.astype(jnp.float32)).astype(jnp.bfloat16)
    shares = swap(summed.reshape(sections // 2, -1, summed.shape[-1]), ("b", "x"))
    share = jnp.sum(shares.astype(jnp.float32), axis=0).astype(jnp.bfloat16)
    own = swap(jnp.broadcast_to(share[None], shares.shape), ("b", "x")).reshape(summed.shape)
    other = lax.ppermute(own, "core", both_cores)

    grads = solve(sizes, features, here, own, other, rows_xs, u, v, adapters)

    ids = jnp.arange(members, dtype=jnp.int32)
    tenant_hot = block_tenant[:, None] == ids[None, :]
    slot_of = jnp.sum(jnp.where(tenant_hot, tenant_slot[None, :], 0), axis=1)
    slot_hot = (ids[:, None] == slot_of[None, :]).astype(jnp.bfloat16)
    by_member = swap(swap(grads, ("b", "x", "a")), "z")
    owned = swap(pick(slot_hot, by_member), dp)
    return tuple(part[None, None] for part in finish(sizes, owned, gain))


def solution(mesh):
    sections, members = mesh.devices.shape
    finer = jax.sharding.Mesh(
        mesh.devices.reshape(2, 2, sections // 4, members // 2, 2), pipe + dp
    )
    return jax.shard_map(
        body,
        mesh=finer,
        in_specs=(
            P(pipe, dp, None),
            P(pipe, dp, None),
            P(pipe, None),
            P(pipe, None, None),
            P(pipe, None, None),
            P(pipe, dp, None, None),
            P(pipe, dp, None, None),
            P(pipe, dp, None, None),
            P(pipe, dp, None, None),
            P(),
            P(),
            P(),
        ),
        out_specs=(
            P(pipe, dp, None, None),
            P(pipe, dp, None, None),
            P(pipe, dp, None, None),
            P(pipe, dp, None, None),
        ),
        check_vma=False,
    )
```

```python
import functools

import jax
import jax.numpy as jnp
from jax import lax
from jax.experimental import pallas as pl
from jax.experimental.pallas import tpu as pltpu
from jax.sharding import PartitionSpec as P

adapter_scale = 2.0
norm_eps = 1e-05
block = 256
vmem_bytes = 20 * 1024 * 1024
whole_vmem_bytes = 56 * 1024 * 1024
merge_cost_bytes = 40 * 1024 * 1024
pipe = ("a", "b", "x")
dp = ("z", "core")


def mm(left, right):
    return lax.dot_general(
        left, right, (((1,), (0,)), ((), ())), preferred_element_type=jnp.float32
    )


def mm_nt(left, right):
    return lax.dot_general(
        left, right, (((1,), (1,)), ((), ())), preferred_element_type=jnp.float32
    )


def mm_tn(left, right):
    return lax.dot_general(
        left, right, (((0,), (0,)), ((), ())), preferred_element_type=jnp.float32
    )


def layer_mask(rows, columns, hd, compare):
    row_layer = lax.broadcasted_iota(jnp.int32, (rows, columns), 0) // hd
    column_layer = lax.broadcasted_iota(jnp.int32, (rows, columns), 1) // hd
    return compare(row_layer, column_layer)


def pack_kernel(
    sizes, here_ref, wv_ref, wo_ref, gain_ref, vd_ref, ou_ref, vu_ref, od_ref, stored_ref, *out_refs
):
    layers, hd, rank, tokens, cols = sizes
    small = jnp.concatenate([vu_ref[...], od_ref[...]], axis=1)
    for k in range(stored_ref.shape[0]):
        at = pl.ds(k * cols, cols)
        stored_ref[k, :, :cols] = (vd_ref[:, at].astype(jnp.float32) * gain_ref[:, at]).astype(
            jnp.bfloat16
        )
        stored_ref[k, :, cols : 2 * cols] = ou_ref[:, at]
        stored_ref[k, :, 2 * cols :] = small
    part = hd // 2
    section, member = (here_ref[0] // layers), lax.rem(here_ref[0], layers)
    core = lax.rem(member, 2)
    side = len(out_refs)
    across = layers // side
    mine = pl.ds(pl.multiple_of(lax.rem(member // 2, 2) * part, part), part)
    for step, out_ref in enumerate(out_refs):
        line = lax.rem(section // across + step, side)
        for k in range(across):
            column = (lax.rem(line, side // 2) * across + k) * 2 + core
            at = pl.ds(pl.multiple_of(column * cols, cols), cols)
            out_ref[k, :part, :] = (wv_ref[mine, at].astype(jnp.float32) * gain_ref[:, at]).astype(
                jnp.bfloat16
            )
            out_ref[k, part:, :] = wo_ref[mine, at]


def join_kernel(
    sizes,
    here_ref,
    tenant_ref,
    valid_ref,
    parts_ref,
    x_ref,
    cot_ref,
    other_x_ref,
    other_cot_ref,
    *refs
):
    out_ref = refs[-1]
    layers, hd, rank, tokens, cols = sizes
    rows = tokens // layers
    section, member = (here_ref[0] // layers), lax.rem(here_ref[0], layers)
    core = lax.rem(member, 2)
    position = section * rows + lax.broadcasted_iota(jnp.int32, (rows, 1), 0)
    width = 2 * cols + 2 * hd

    def token_weight(index):
        total = jnp.int32(0)
        for i in range(tenant_ref.shape[0]):
            total = total + jnp.where(tenant_ref[i] == tenant_ref[index], valid_ref[i], 0)
        kept = jnp.where(position < valid_ref[index], 1.0, 0.0).astype(jnp.float32)
        return kept / jnp.full((rows, 1), total, jnp.int32).astype(jnp.float32)

    own_weight = token_weight(member)
    other_weight = token_weight(member + 1 - 2 * core)
    for k in range(layers // 2):
        at = pl.ds(pl.multiple_of((2 * k + core) * cols, cols), cols)
        own_x = x_ref[:, at].astype(jnp.float32)
        other_x = other_x_ref[:, at].astype(jnp.float32)
        own_seed = cot_ref[:, at].astype(jnp.float32) * own_weight
        other_seed = other_cot_ref[:, at].astype(jnp.float32) * other_weight
        for a in range(2):
            own = core == a
            out_ref[2 * k + a, :, :width] = parts_ref[2 * k + a]
            out_ref[2 * k + a, :, width:] = jnp.concatenate(
                [jnp.where(own, own_x, other_x), jnp.where(own, own_seed, other_seed)], axis=0
            ).astype(jnp.bfloat16)


def pick_kernel(side, across, here_ref, tenant_ref, slot_ref, parts_ref, *refs):
    lines, out_ref, turned, sems = refs[:side], refs[side], refs[side + 1 : -1], refs[-1]
    layers = side * across
    place = lax.rem(here_ref[0] // layers, across)
    copies = [
        pltpu.make_async_copy(
            lines[0].at[lax.rem(place + step, across)], turned_ref.at[0], sems.at[step]
        )
        for step, turned_ref in enumerate(turned)
    ]
    for copy in copies:
        copy.start()
    for j in range(out_ref.shape[0]):
        out_ref[j] = parts_ref[slot_ref[tenant_ref[j]]]
    for step, turned_ref in enumerate(turned):
        at = lax.rem(place + step, across)
        for k in range(1, side):
            turned_ref[k] = lines[k][at]
    for copy in copies:
        copy.wait()


def finish_kernel(sizes, owned_ref, gain_ref, gvd_ref, gvu_ref, god_ref, gou_ref):
    layers, hd, rank, tokens, cols = sizes
    tail = jnp.zeros((rank, 2 * hd), jnp.float32)
    for c in range(layers):
        at = pl.ds(c * cols, cols)
        gvd_ref[:, at] = (owned_ref[c, :, :cols].astype(jnp.float32) * gain_ref[:, at]).astype(
            jnp.bfloat16
        )
        gou_ref[:, at] = owned_ref[c, :, cols : 2 * cols]
        tail = tail + owned_ref[c, :, 2 * cols :].astype(jnp.float32)
    gvu_ref[...] = tail[:, :hd].astype(jnp.bfloat16)
    god_ref[...] = tail[:, hd:].astype(jnp.bfloat16)


def turned_index(l, layers):
    return l % (layers // 2) * 2 + l // (layers // 2)


def merge_kernel(sizes, side, across, here_ref, *refs):
    layers, hd, rank, tokens, cols = sizes
    own_refs, other_refs, both_ref = refs[:across], refs[across:-1], refs[-1]
    pairs = across // 2
    part = hd // 2
    plane = lax.rem(lax.rem(here_ref[0], layers) // 2, 2)
    line, place = (here_ref[0] // layers) // across, lax.rem((here_ref[0] // layers), across)
    for step in range(layers):
        dx, dy = step // side, step % side
        l = lax.rem(line + side - dy, side) * across + lax.rem(place + across - dx, across)
        own, other = own_refs[dx][dy], other_refs[dx // pairs][dx % pairs * side + dy]
        mine = pl.ds(pl.multiple_of(l * hd + plane * part, part), part)
        theirs = pl.ds(pl.multiple_of(l * hd + (1 - plane) * part, part), part)
        both_ref[0, mine, :] = own[:part]
        both_ref[1, mine, :] = own[part:]
        both_ref[0, theirs, :] = other[:part]
        both_ref[1, theirs, :] = other[part:]


def gram_kernel(
    sizes,
    here_ref,
    both_ref,
    q_ref,
    u_ref,
    v_ref,
    xs_ref,
    give_ref,
    x_wide,
    s_wide,
    sems,
):
    layers, hd, rank, tokens, cols = sizes
    rows = tokens // layers
    core = lax.rem(lax.rem(here_ref[0], layers), 2)
    copies = [
        pltpu.make_async_copy(both_ref.at[0], v_ref, sems.at[0]),
        pltpu.make_async_copy(both_ref.at[1], u_ref, sems.at[1]),
    ]
    for copy in copies:
        copy.start()
    for l in range(layers):
        both = q_ref[turned_index(l, layers), :, 2 * cols + 2 * hd :].astype(jnp.float32)
        at = pl.ds(l * rows, rows)
        x_wide[at, :] = both[:rows]
        s_wide[at, :] = both[rows:]
    for copy in copies:
        copy.wait()
    for l in range(layers):
        q_l = q_ref[turned_index(l, layers)]
        small = q_l[:, 2 * cols : 2 * cols + 2 * hd]
        delta_v = mm_tn(small[:, :hd], q_l[:, :cols])
        delta_u = mm_tn(small[:, hd:], q_l[:, cols : 2 * cols])
        at = pl.ds(l * hd, hd)
        v_ref[at, :] = (v_ref[at, :].astype(jnp.float32) + adapter_scale * delta_v).astype(
            jnp.bfloat16
        )
        u_ref[at, :] = (u_ref[at, :].astype(jnp.float32) + adapter_scale * delta_u).astype(
            jnp.bfloat16
        )
    xs_ref[:tokens, :] = x_wide[...].astype(jnp.bfloat16)
    xs_ref[tokens:, :] = s_wide[...].astype(jnp.bfloat16)
    for own_core in range(2):
        pl.when(core == own_core)(
            functools.partial(
                half_products, sizes, 1 - own_core, u_ref, v_ref, xs_ref, give_ref
            )
        )


def keep_kernel(sizes, here_ref, u_ref, v_ref, xs_ref, keep_ref):
    layers = sizes[0]
    core = lax.rem(lax.rem(here_ref[0], layers), 2)
    for own_core in range(2):
        pl.when(core == own_core)(
            functools.partial(half_products, sizes, own_core, u_ref, v_ref, xs_ref, keep_ref)
        )


def half_products(sizes, which, u_ref, v_ref, xs_ref, out_ref):
    layers, hd, rank, tokens, cols = sizes
    width = layers * hd
    base = 3 * tokens
    below = layer_mask(block, block, hd, lambda r, c: r < c)
    lane = 2 * hd
    count = width // block // 2

    def put(start, column, value):
        value = value.astype(jnp.bfloat16)
        for at in range(0, value.shape[1], lane):
            index = (column - which * count * block + at) // lane
            out_ref[index, pl.ds(start, value.shape[0]), :] = value[:, at : at + lane]

    x_rows, s_rows = xs_ref[:tokens, :], xs_ref[tokens:, :]
    for bj in range(which * count, which * count + count):
        column = bj * block
        at_col = pl.ds(column, block)
        u_col, v_col = u_ref[at_col, :], v_ref[at_col, :]
        put(0, column, mm_nt(x_rows, v_col))
        x_u = mm_nt(x_rows, u_col)
        if column + block == width:
            wide = x_rows.astype(jnp.float32)
            wide = wide * wide
            folded = wide[:, :lane]
            for at in range(lane, cols, lane):
                folded = folded + wide[:, at : at + lane]
            x_u = jnp.concatenate([x_u[:, : block - hd], folded[:, :hd] + folded[:, hd:]], axis=1)
        put(tokens, column, x_u)
        put(2 * tokens, column, mm_nt(s_rows, u_col))
        for bi in range(width // block):
            height = min(block, width - hd - bi * block)
            rows_at = pl.ds(bi * block, height)
            rows_u = u_ref[rows_at, :]
            if bi < bj:
                part = mm_nt(rows_u, v_col)
            elif bi > bj:
                part = mm_nt(rows_u, u_col)
            else:
                part = jnp.where(below[:height], mm_nt(rows_u, v_col), mm_nt(rows_u, u_col))
            put(base + bi * block, column, part)


def half(pair, l):
    hd = pair.shape[1] // 2
    return pair[:, hd:] if l % 2 else pair[:, :hd]


def solve_kernel(
    sizes,
    features,
    here_ref,
    own_ref,
    other_ref,
    xs_ref,
    u_ref,
    v_ref,
    q_ref,
    out_ref,
    c_ref,
    d_ref,
    ec_ref,
    a_ref,
    bp_ref,
    inv_ref,
    k_ref,
    sems,
):
    layers, hd, rank, tokens, cols = sizes
    width = layers * hd
    base = 3 * tokens
    half_count = own_ref.shape[0]
    core = lax.rem(lax.rem(here_ref[0], layers), 2)
    for index in range(half_count):
        for source, place in ((own_ref, core), (other_ref, 1 - core)):
            to = place * half_count + index
            pltpu.make_async_copy(source.at[index], k_ref.at[to], sems.at[to]).start()

    def arrive(index):
        pltpu.make_async_copy(own_ref.at[0], k_ref.at[index], sems.at[index]).wait()

    c_ref[...] = jnp.zeros_like(c_ref)
    d_ref[...] = jnp.zeros_like(d_ref)
    ec_ref[...] = jnp.zeros_like(ec_ref)

    def upto(l):
        return 2 * hd * ((l + 1) // 2)

    def across_row(l, start, stop):
        rows_l = pl.ds(base + l * hd, hd)
        return jnp.concatenate(
            [k_ref[index, rows_l, :] for index in range(start // (2 * hd), stop // (2 * hd))],
            axis=1,
        )

    last = width // (2 * hd) - 1
    arrive(last)
    folded = k_ref[last, tokens : 2 * tokens, :].astype(jnp.float32)[:, hd:]
    square = jnp.sum(folded, axis=1, keepdims=True)
    for l in range(layers):
        pair = l // 2
        if l % 2 == 0 and pair < last:
            arrive(pair)
        a = half(k_ref[pair, :tokens, :], l).astype(jnp.float32)
        if l:
            w = upto(l)
            known = c_ref[:, :w]
            top = min(w, width - hd)
            a = a + half(mm(known[:, :top], k_ref[pair, base : base + top, :]), l)
        inverse = lax.rsqrt(jnp.maximum(square, 0.0) / features + norm_eps)
        c = (inverse * a).astype(jnp.bfloat16)
        c_ref[:, l * hd : (l + 1) * hd] = c
        a_ref[l] = a
        inv_ref[l] = inverse
        if l == layers - 1:
            break
        b = half(k_ref[pair, tokens : 2 * tokens, :], l).astype(jnp.float32)
        if l:
            b = b + mm_nt(known, across_row(l, 0, w))
        wide = c.astype(jnp.float32)
        after = b + half(mm(c, k_ref[pair, pl.ds(base + l * hd, hd), :]), l)
        square = square + jnp.sum(wide * (b + after), axis=1, keepdims=True)
        bp_ref[l] = after

    below = layer_mask(block, block, hd, lambda r, c: r > c)
    upto_diag = layer_mask(block, block, hd, lambda r, c: r >= c)
    group = block // hd
    diagonal = lax.broadcasted_iota(jnp.int32, (group * rank, block), 0) // rank == (
        lax.broadcasted_iota(jnp.int32, (group * rank, block), 1) // hd
    )

    def side_by_side(parts):
        return parts[0] if len(parts) == 1 else jnp.concatenate(parts, axis=1)

    def spread_diagonal(parts):
        tall = jnp.concatenate(parts, axis=0)
        return jnp.where(diagonal, side_by_side([tall] * group), jnp.zeros((), jnp.bfloat16))

    def weight_gradients(start):
        stop = start + block
        mine = pl.ds(start, block)
        c_t = c_ref[:, mine].T
        d_t = d_ref[:, mine].T
        ec_t = ec_ref[:, mine].T

        m = [jnp.where(below, mm(d_t, c_ref[:, mine]), 0.0).astype(jnp.bfloat16)]
        if start:
            m = [mm(d_t, c_ref[:, :start]).astype(jnp.bfloat16)] + m
        yield
        y = mm(d_t, xs_ref[:tokens, :]) + mm(side_by_side(m), u_ref[:stop, :])
        yield
        m = [jnp.where(upto_diag, 0.0, mm(c_t, d_ref[:, mine])).astype(jnp.bfloat16)]
        if stop < width:
            m = m + [mm(c_t, d_ref[:, stop:]).astype(jnp.bfloat16)]
        yield
        z = mm(side_by_side([-ec_t, c_t]), xs_ref[...]) + mm(side_by_side(m), v_ref[start:, :])
        yield
        m = [
            jnp.where(upto_diag, mm(ec_t, c_ref[:, mine]), mm(c_t, ec_ref[:, mine])).astype(
                jnp.bfloat16
            )
        ]
        if start:
            m = [mm(ec_t, c_ref[:, :start]).astype(jnp.bfloat16)] + m
        if stop < width:
            m = m + [mm(c_t, ec_ref[:, stop:]).astype(jnp.bfloat16)]
        yield
        z = z - mm(side_by_side(m), u_ref[...])
        yield
        y = y.astype(jnp.bfloat16)
        z = z.astype(jnp.bfloat16)
        places = [turned_index(l, layers) for l in range(start // hd, stop // hd)]
        smalls = [q_ref[at, :, 2 * cols : 2 * cols + 2 * hd] for at in places]
        up = adapter_scale * mm(spread_diagonal([small[:, :hd] for small in smalls]), y)
        down = adapter_scale * mm(spread_diagonal([small[:, hd:] for small in smalls]), z)
        tail_y = mm_nt(jnp.concatenate([q_ref[at, :, :cols] for at in places], axis=0), y)
        tail_z = mm_nt(jnp.concatenate([q_ref[at, :, cols : 2 * cols] for at in places], axis=0), z)
        for j, at in enumerate(places):
            rows_j = slice(j * rank, (j + 1) * rank)
            out_ref[at, :, :cols] = up[rows_j].astype(jnp.bfloat16)
            out_ref[at, :, cols : 2 * cols] = down[rows_j].astype(jnp.bfloat16)
            tail = jnp.concatenate(
                [tail_y[rows_j, j * hd : (j + 1) * hd], tail_z[rows_j, j * hd : (j + 1) * hd]],
                axis=1,
            )
            out_ref[at, :, 2 * cols :] = (adapter_scale * tail).astype(jnp.bfloat16)

    pull = jnp.zeros((tokens, 1), jnp.float32)
    pending = iter(())
    for l in range(layers - 1, -1, -1):
        pair = l // 2
        p = half(k_ref[pair, 2 * tokens : 3 * tokens, :], l).astype(jnp.float32)
        if l < layers - 1:
            w = upto(l)
            top = width - hd
            p = p - pull * bp_ref[l]
            p = p + mm_nt(d_ref[:, w:], across_row(l, w, width))
            if w < top:
                p = p - half(mm(ec_ref[:, w:top], k_ref[pair, base + w : base + top, :]), l)
        next(pending, None)
        inverse = inv_ref[l]
        d_ref[:, l * hd : (l + 1) * hd] = (inverse * p).astype(jnp.bfloat16)
        c = c_ref[:, l * hd : (l + 1) * hd].astype(jnp.float32)
        ec_ref[:, l * hd : (l + 1) * hd] = (pull * c).astype(jnp.bfloat16)
        correction = jnp.sum(p * a_ref[l], axis=1, keepdims=True) / features
        pull = pull + inverse * inverse * inverse * correction
        next(pending, None)
        if l * hd % block == 0:
            for _ in pending:
                pass
            pending = weight_gradients(l * hd)
    for _ in pending:
        pass


def params(limit=vmem_bytes):
    return pltpu.CompilerParams(vmem_limit_bytes=limit)


def in_vmem(count):
    return [pl.BlockSpec(memory_space=pltpu.VMEM)] * count


def in_smem(count):
    return [pl.BlockSpec(memory_space=pltpu.SMEM)] * count


def pack(sizes, side, members, here, arrays):
    layers, hd, rank, tokens, cols = sizes
    line = jax.ShapeDtypeStruct((layers // side, hd, cols), jnp.bfloat16)
    stored = jax.ShapeDtypeStruct((members, rank, 2 * cols + 2 * hd), jnp.bfloat16)
    return pl.pallas_call(
        functools.partial(pack_kernel, sizes),
        out_shape=(stored,) + (line,) * side,
        in_specs=in_smem(1) + in_vmem(len(arrays)),
        out_specs=tuple(in_vmem(1 + side)),
        compiler_params=params(whole_vmem_bytes),
    )(here, *arrays)


def pick_rows(scalars, parts, lines):
    side = len(lines)
    across = lines[0].shape[0]
    turned = jax.ShapeDtypeStruct((side,) + lines[0].shape[1:], jnp.bfloat16)
    return pl.pallas_call(
        functools.partial(pick_kernel, side, across),
        out_shape=(jax.ShapeDtypeStruct(parts.shape, parts.dtype),) + (turned,) * across,
        in_specs=in_smem(len(scalars))
        + in_vmem(1)
        + [pl.BlockSpec(memory_space=pl.ANY)]
        + in_vmem(side - 1),
        out_specs=tuple(in_vmem(1 + across)),
        scratch_shapes=[pltpu.SemaphoreType.DMA((across,))],
        compiler_params=params(),
    )(*scalars, parts, *lines)


def join(sizes, scalars, parts, arrays, after):
    layers, hd, rank, tokens, cols = sizes
    return pl.pallas_call(
        functools.partial(join_kernel, sizes),
        out_shape=jax.ShapeDtypeStruct(parts.shape[:2] + (3 * cols + 2 * hd,), jnp.bfloat16),
        in_specs=in_smem(len(scalars))
        + in_vmem(1 + len(arrays))
        + [pl.BlockSpec(memory_space=pl.ANY)] * len(after),
        out_specs=in_vmem(1)[0],
        compiler_params=params(),
    )(*scalars, parts, *arrays, *after)


def finish(sizes, owned, gain):
    layers, hd, rank, tokens, cols = sizes
    wide = jax.ShapeDtypeStruct((rank, layers * cols), jnp.bfloat16)
    narrow = jax.ShapeDtypeStruct((rank, hd), jnp.bfloat16)
    return pl.pallas_call(
        functools.partial(finish_kernel, sizes),
        out_shape=(wide, narrow, narrow, wide),
        in_specs=in_vmem(2),
        out_specs=tuple(in_vmem(4)),
        compiler_params=params(),
    )(owned, gain)


def merge(sizes, side, here, own, other):
    layers, hd, rank, tokens, cols = sizes
    return pl.pallas_call(
        functools.partial(merge_kernel, sizes, side, len(own)),
        out_shape=jax.ShapeDtypeStruct((2, layers * hd, cols), jnp.bfloat16),
        in_specs=in_smem(1) + in_vmem(len(own) + len(other)),
        out_specs=in_vmem(1)[0],
        compiler_params=params(),
        cost_estimate=pl.CostEstimate(
            flops=0, bytes_accessed=merge_cost_bytes, transcendentals=0
        ),
    )(here, *own, *other)


def gram(sizes, here, both, q):
    layers, hd, rank, tokens, cols = sizes
    width = layers * hd
    share = jax.ShapeDtypeStruct(
        (width // (4 * hd), 3 * tokens + width - hd, 2 * hd), jnp.bfloat16
    )
    table = jax.ShapeDtypeStruct((width, cols), jnp.bfloat16)
    return pl.pallas_call(
        functools.partial(gram_kernel, sizes),
        out_shape=(
            table,
            table,
            jax.ShapeDtypeStruct((2 * tokens, cols), jnp.bfloat16),
            share,
        ),
        in_specs=in_smem(1) + [pl.BlockSpec(memory_space=pl.ANY)] + in_vmem(1),
        out_specs=tuple(in_vmem(4)),
        scratch_shapes=[
            pltpu.VMEM((tokens, cols), jnp.float32),
            pltpu.VMEM((tokens, cols), jnp.float32),
            pltpu.SemaphoreType.DMA((2,)),
        ],
        compiler_params=params(),
    )(here, both, q)


def keep(sizes, here, u, v, xs, shape):
    return pl.pallas_call(
        functools.partial(keep_kernel, sizes),
        out_shape=jax.ShapeDtypeStruct(shape, jnp.bfloat16),
        in_specs=in_smem(1) + in_vmem(3),
        out_specs=in_vmem(1)[0],
        compiler_params=params(),
        cost_estimate=pl.CostEstimate(flops=1 << 31, bytes_accessed=1 << 22, transcendentals=0),
    )(here, u, v, xs)


def solve(sizes, features, here, own, other, xs, u, v, q):
    layers, hd, rank, tokens, cols = sizes
    width = layers * hd
    return pl.pallas_call(
        functools.partial(solve_kernel, sizes, features),
        out_shape=jax.ShapeDtypeStruct(q.shape[:2] + (2 * cols + 2 * hd,), jnp.bfloat16),
        in_specs=in_smem(1) + [pl.BlockSpec(memory_space=pl.ANY)] * 2 + in_vmem(4),
        out_specs=in_vmem(1)[0],
        scratch_shapes=[
            pltpu.VMEM((tokens, width), jnp.bfloat16),
            pltpu.VMEM((tokens, width), jnp.bfloat16),
            pltpu.VMEM((tokens, width), jnp.bfloat16),
            pltpu.VMEM((layers, tokens, hd), jnp.float32),
            pltpu.VMEM((layers, tokens, hd), jnp.float32),
            pltpu.VMEM((layers, tokens, 1), jnp.float32),
            pltpu.VMEM((2 * own.shape[0],) + own.shape[1:], jnp.bfloat16),
            pltpu.SemaphoreType.DMA((2 * own.shape[0],)),
        ],
        compiler_params=params(),
    )(here, own, other, xs, u, v, q)


def swap(value, axis):
    return lax.all_to_all(value, axis, split_axis=0, concat_axis=0, tiled=True)


def pick(chooser, parts):
    flat = parts.reshape(parts.shape[0], -1)
    return mm(chooser, flat).astype(jnp.bfloat16).reshape((chooser.shape[0],) + parts.shape[1:])


def body(
    inputs,
    cotangent,
    norm_gain,
    w_value,
    w_out,
    value_down,
    value_up_factor,
    out_down,
    output_up_factor,
    block_tenant,
    valid_tokens,
    tenant_slot,
):
    sections, members = lax.axis_size(pipe), lax.axis_size(dp)
    rows, features = inputs.shape[1], inputs.shape[2]
    hd, rank = w_value.shape[1], value_down.shape[2]
    cols = features // sections
    tokens = rows * sections
    sizes = (sections, hd, rank, tokens, cols)
    side = lax.axis_size("a") * lax.axis_size("b")
    across = lax.axis_size("x")
    planes = lax.axis_size("z")
    here = lax.axis_index(pipe + dp).astype(jnp.int32)[None]
    gain = norm_gain
    both_cores = [(0, 1), (1, 0)]

    stored, *lines = pack(
        sizes,
        side,
        members,
        here,
        (
            w_value[0],
            w_out[0],
            gain,
            value_down[0, 0],
            output_up_factor[0, 0],
            value_up_factor[0, 0],
            out_down[0, 0],
        ),
    )
    lines = [lines[0]] + [
        lax.ppermute(lines[step], ("a", "b"), [(i, (i + step) % side) for i in range(side)])
        for step in range(1, side)
    ]
    adapters, *turned = pick_rows((here, block_tenant, tenant_slot), swap(stored, dp), lines)
    turned = [turned[0]] + [
        lax.ppermute(turned[step], "x", [(i, (i + step) % across) for i in range(across)])
        for step in range(1, across)
    ]
    joined = join(
        sizes,
        (here, block_tenant, valid_tokens),
        swap(adapters, "z"),
        (
            inputs[0],
            cotangent[0],
            lax.ppermute(inputs[0], "core", both_cores),
            lax.ppermute(cotangent[0], "core", both_cores),
        ),
        turned[1:],
    )
    adapters = swap(joined, ("b", "x", "a"))
    pairs = across // 2
    other = [
        lax.ppermute(
            jnp.concatenate(turned[at : at + pairs], axis=0),
            "z",
            [(i, (i + turn) % planes) for i in range(planes)],
        )
        for at, turn in ((0, 1), (pairs, -1))
    ]

    u, v, rows_xs, given = gram(
        sizes, here, merge(sizes, side, here, turned, other), adapters
    )
    theirs = lax.ppermute(given, "core", both_cores)
    kept = keep(sizes, here, u, v, rows_xs, given.shape)
    summed = (kept.astype(jnp.float32) + theirs.astype(jnp.float32)).astype(jnp.bfloat16)
    shares = swap(summed.reshape(sections // 2, -1, summed.shape[-1]), ("b", "x"))
    share = jnp.sum(shares.astype(jnp.float32), axis=0).astype(jnp.bfloat16)
    own = swap(jnp.broadcast_to(share[None], shares.shape), ("b", "x")).reshape(summed.shape)
    other = lax.ppermute(own, "core", both_cores)

    grads = solve(sizes, features, here, own, other, rows_xs, u, v, adapters)

    ids = jnp.arange(members, dtype=jnp.int32)
    tenant_hot = block_tenant[:, None] == ids[None, :]
    slot_of = jnp.sum(jnp.where(tenant_hot, tenant_slot[None, :], 0), axis=1)
    slot_hot = (ids[:, None] == slot_of[None, :]).astype(jnp.bfloat16)
    by_member = swap(swap(grads, ("b", "x", "a")), "z")
    owned = swap(pick(slot_hot, by_member), dp)
    return tuple(part[None, None] for part in finish(sizes, owned, gain))


def solution(mesh):
    sections, members = mesh.devices.shape
    finer = jax.sharding.Mesh(
        mesh.devices.reshape(2, 2, sections // 4, members // 2, 2), pipe + dp
    )
    return jax.shard_map(
        body,
        mesh=finer,
        in_specs=(
            P(pipe, dp, None),
            P(pipe, dp, None),
            P(pipe, None),
            P(pipe, None, None),
            P(pipe, None, None),
            P(pipe, dp, None, None),
            P(pipe, dp, None, None),
            P(pipe, dp, None, None),
            P(pipe, dp, None, None),
            P(),
            P(),
            P(),
        ),
        out_specs=(
            P(pipe, dp, None, None),
            P(pipe, dp, None, None),
            P(pipe, dp, None, None),
            P(pipe, dp, None, None),
        ),
        check_vma=False,
    )
```

```python
import functools

import jax
import jax.numpy as jnp
from jax import lax
from jax.experimental import pallas as pl
from jax.experimental.pallas import tpu as pltpu
from jax.sharding import PartitionSpec as P

adapter_scale = 2.0
norm_eps = 1e-05
block = 256
vmem_bytes = 12 * 1024 * 1024
solve_vmem_bytes = 20 * 1024 * 1024
whole_vmem_bytes = 56 * 1024 * 1024
merge_cost_bytes = 40 * 1024 * 1024
pipe = ("a", "b", "x")
dp = ("z", "core")


def mm(left, right):
    return lax.dot_general(
        left, right, (((1,), (0,)), ((), ())), preferred_element_type=jnp.float32
    )


def mm_nt(left, right):
    return lax.dot_general(
        left, right, (((1,), (1,)), ((), ())), preferred_element_type=jnp.float32
    )


def mm_tn(left, right):
    return lax.dot_general(
        left, right, (((0,), (0,)), ((), ())), preferred_element_type=jnp.float32
    )


def layer_mask(rows, columns, hd, compare):
    row_layer = lax.broadcasted_iota(jnp.int32, (rows, columns), 0) // hd
    column_layer = lax.broadcasted_iota(jnp.int32, (rows, columns), 1) // hd
    return compare(row_layer, column_layer)


def pack_kernel(
    sizes, here_ref, wv_ref, wo_ref, gain_ref, vd_ref, ou_ref, vu_ref, od_ref, stored_ref, *out_refs
):
    layers, hd, rank, tokens, cols = sizes
    small = jnp.concatenate([vu_ref[...], od_ref[...]], axis=1)
    for k in range(stored_ref.shape[0]):
        at = pl.ds(k * cols, cols)
        stored_ref[k, :, :cols] = (vd_ref[:, at].astype(jnp.float32) * gain_ref[:, at]).astype(
            jnp.bfloat16
        )
        stored_ref[k, :, cols : 2 * cols] = ou_ref[:, at]
        stored_ref[k, :, 2 * cols :] = small
    part = hd // 2
    section, member = (here_ref[0] // layers), lax.rem(here_ref[0], layers)
    core = lax.rem(member, 2)
    side = len(out_refs)
    across = layers // side
    mine = pl.ds(pl.multiple_of(lax.rem(member // 2, 2) * part, part), part)
    for step, out_ref in enumerate(out_refs):
        line = lax.rem(section // across + step, side)
        for k in range(across):
            column = (lax.rem(line, side // 2) * across + k) * 2 + core
            at = pl.ds(pl.multiple_of(column * cols, cols), cols)
            out_ref[k, :part, :] = (wv_ref[mine, at].astype(jnp.float32) * gain_ref[:, at]).astype(
                jnp.bfloat16
            )
            out_ref[k, part:, :] = wo_ref[mine, at]


def join_kernel(
    sizes,
    here_ref,
    tenant_ref,
    valid_ref,
    parts_ref,
    x_ref,
    cot_ref,
    other_x_ref,
    other_cot_ref,
    *refs
):
    out_ref = refs[-1]
    layers, hd, rank, tokens, cols = sizes
    rows = tokens // layers
    section, member = (here_ref[0] // layers), lax.rem(here_ref[0], layers)
    core = lax.rem(member, 2)
    position = section * rows + lax.broadcasted_iota(jnp.int32, (rows, 1), 0)
    width = 2 * cols + 2 * hd

    def token_weight(index):
        total = jnp.int32(0)
        for i in range(tenant_ref.shape[0]):
            total = total + jnp.where(tenant_ref[i] == tenant_ref[index], valid_ref[i], 0)
        kept = jnp.where(position < valid_ref[index], 1.0, 0.0).astype(jnp.float32)
        return kept / jnp.full((rows, 1), total, jnp.int32).astype(jnp.float32)

    own_weight = token_weight(member)
    other_weight = token_weight(member + 1 - 2 * core)
    for k in range(layers // 2):
        at = pl.ds(pl.multiple_of((2 * k + core) * cols, cols), cols)
        own_x = x_ref[:, at].astype(jnp.float32)
        other_x = other_x_ref[:, at].astype(jnp.float32)
        own_seed = cot_ref[:, at].astype(jnp.float32) * own_weight
        other_seed = other_cot_ref[:, at].astype(jnp.float32) * other_weight
        for a in range(2):
            own = core == a
            out_ref[2 * k + a, :, :width] = parts_ref[2 * k + a]
            out_ref[2 * k + a, :, width:] = jnp.concatenate(
                [jnp.where(own, own_x, other_x), jnp.where(own, own_seed, other_seed)], axis=0
            ).astype(jnp.bfloat16)


def pick_kernel(side, across, here_ref, tenant_ref, slot_ref, parts_ref, *refs):
    lines, out_ref, turned, sems = refs[:side], refs[side], refs[side + 1 : -1], refs[-1]
    layers = side * across
    place = lax.rem(here_ref[0] // layers, across)
    copies = [
        pltpu.make_async_copy(
            lines[0].at[lax.rem(place + step, across)], turned_ref.at[0], sems.at[step]
        )
        for step, turned_ref in enumerate(turned)
    ]
    for copy in copies:
        copy.start()
    for j in range(out_ref.shape[0]):
        out_ref[j] = parts_ref[slot_ref[tenant_ref[j]]]
    for step, turned_ref in enumerate(turned):
        at = lax.rem(place + step, across)
        for k in range(1, side):
            turned_ref[k] = lines[k][at]
    for copy in copies:
        copy.wait()


def finish_kernel(sizes, owned_ref, gain_ref, gvd_ref, gvu_ref, god_ref, gou_ref):
    layers, hd, rank, tokens, cols = sizes
    tail = jnp.zeros((rank, 2 * hd), jnp.float32)
    for c in range(layers):
        at = pl.ds(c * cols, cols)
        gvd_ref[:, at] = (owned_ref[c, :, :cols].astype(jnp.float32) * gain_ref[:, at]).astype(
            jnp.bfloat16
        )
        gou_ref[:, at] = owned_ref[c, :, cols : 2 * cols]
        tail = tail + owned_ref[c, :, 2 * cols :].astype(jnp.float32)
    gvu_ref[...] = tail[:, :hd].astype(jnp.bfloat16)
    god_ref[...] = tail[:, hd:].astype(jnp.bfloat16)


def turned_index(l, layers):
    return l % (layers // 2) * 2 + l // (layers // 2)


def merge_kernel(sizes, side, across, here_ref, *refs):
    layers, hd, rank, tokens, cols = sizes
    own_refs, other_refs, both_ref = refs[:across], refs[across:-1], refs[-1]
    pairs = across // 2
    part = hd // 2
    plane = lax.rem(lax.rem(here_ref[0], layers) // 2, 2)
    line, place = (here_ref[0] // layers) // across, lax.rem((here_ref[0] // layers), across)
    for step in range(layers):
        dx, dy = step // side, step % side
        l = lax.rem(line + side - dy, side) * across + lax.rem(place + across - dx, across)
        own, other = own_refs[dx][dy], other_refs[dx // pairs][dx % pairs * side + dy]
        mine = pl.ds(pl.multiple_of(l * hd + plane * part, part), part)
        theirs = pl.ds(pl.multiple_of(l * hd + (1 - plane) * part, part), part)
        both_ref[0, mine, :] = own[:part]
        both_ref[1, mine, :] = own[part:]
        both_ref[0, theirs, :] = other[:part]
        both_ref[1, theirs, :] = other[part:]


def gram_kernel(
    sizes,
    here_ref,
    both_ref,
    q_ref,
    u_ref,
    v_ref,
    xs_ref,
    give_ref,
    x_wide,
    s_wide,
    sems,
):
    layers, hd, rank, tokens, cols = sizes
    rows = tokens // layers
    core = lax.rem(lax.rem(here_ref[0], layers), 2)
    copies = [
        pltpu.make_async_copy(both_ref.at[0], v_ref, sems.at[0]),
        pltpu.make_async_copy(both_ref.at[1], u_ref, sems.at[1]),
    ]
    for copy in copies:
        copy.start()
    for l in range(layers):
        both = q_ref[turned_index(l, layers), :, 2 * cols + 2 * hd :].astype(jnp.float32)
        at = pl.ds(l * rows, rows)
        x_wide[at, :] = both[:rows]
        s_wide[at, :] = both[rows:]
    for copy in copies:
        copy.wait()
    for l in range(layers):
        q_l = q_ref[turned_index(l, layers)]
        small = q_l[:, 2 * cols : 2 * cols + 2 * hd]
        delta_v = mm_tn(small[:, :hd], q_l[:, :cols])
        delta_u = mm_tn(small[:, hd:], q_l[:, cols : 2 * cols])
        at = pl.ds(l * hd, hd)
        v_ref[at, :] = (v_ref[at, :].astype(jnp.float32) + adapter_scale * delta_v).astype(
            jnp.bfloat16
        )
        u_ref[at, :] = (u_ref[at, :].astype(jnp.float32) + adapter_scale * delta_u).astype(
            jnp.bfloat16
        )
    xs_ref[:tokens, :] = x_wide[...].astype(jnp.bfloat16)
    xs_ref[tokens:, :] = s_wide[...].astype(jnp.bfloat16)
    for own_core in range(2):
        pl.when(core == own_core)(
            functools.partial(
                half_products, sizes, 1 - own_core, u_ref, v_ref, xs_ref, give_ref
            )
        )


def keep_kernel(sizes, here_ref, u_ref, v_ref, xs_ref, keep_ref):
    layers = sizes[0]
    core = lax.rem(lax.rem(here_ref[0], layers), 2)
    for own_core in range(2):
        pl.when(core == own_core)(
            functools.partial(half_products, sizes, own_core, u_ref, v_ref, xs_ref, keep_ref)
        )


def half_products(sizes, which, u_ref, v_ref, xs_ref, out_ref):
    layers, hd, rank, tokens, cols = sizes
    width = layers * hd
    base = 3 * tokens
    below = layer_mask(block, block, hd, lambda r, c: r < c)
    lane = 2 * hd
    count = width // block // 2

    def put(start, column, value):
        value = value.astype(jnp.bfloat16)
        for at in range(0, value.shape[1], lane):
            index = (column - which * count * block + at) // lane
            out_ref[index, pl.ds(start, value.shape[0]), :] = value[:, at : at + lane]

    x_rows, s_rows = xs_ref[:tokens, :], xs_ref[tokens:, :]
    for bj in range(which * count, which * count + count):
        column = bj * block
        at_col = pl.ds(column, block)
        u_col, v_col = u_ref[at_col, :], v_ref[at_col, :]
        put(0, column, mm_nt(x_rows, v_col))
        x_u = mm_nt(x_rows, u_col)
        if column + block == width:
            wide = x_rows.astype(jnp.float32)
            wide = wide * wide
            folded = wide[:, :lane]
            for at in range(lane, cols, lane):
                folded = folded + wide[:, at : at + lane]
            x_u = jnp.concatenate([x_u[:, : block - hd], folded[:, :hd] + folded[:, hd:]], axis=1)
        put(tokens, column, x_u)
        put(2 * tokens, column, mm_nt(s_rows, u_col))
        for bi in range(width // block):
            height = min(block, width - hd - bi * block)
            rows_at = pl.ds(bi * block, height)
            rows_u = u_ref[rows_at, :]
            if bi < bj:
                part = mm_nt(rows_u, v_col)
            elif bi > bj:
                part = mm_nt(rows_u, u_col)
            else:
                part = jnp.where(below[:height], mm_nt(rows_u, v_col), mm_nt(rows_u, u_col))
            put(base + bi * block, column, part)


def half(pair, l):
    hd = pair.shape[1] // 2
    return pair[:, hd:] if l % 2 else pair[:, :hd]


def solve_kernel(
    sizes,
    features,
    here_ref,
    own_ref,
    other_ref,
    xs_ref,
    u_ref,
    v_ref,
    q_ref,
    out_ref,
    c_ref,
    d_ref,
    ec_ref,
    a_ref,
    bp_ref,
    inv_ref,
    k_ref,
    sems,
):
    layers, hd, rank, tokens, cols = sizes
    width = layers * hd
    base = 3 * tokens
    half_count = own_ref.shape[0]
    core = lax.rem(lax.rem(here_ref[0], layers), 2)
    for index in range(half_count):
        for source, place in ((own_ref, core), (other_ref, 1 - core)):
            to = place * half_count + index
            pltpu.make_async_copy(source.at[index], k_ref.at[to], sems.at[to]).start()

    def arrive(index):
        pltpu.make_async_copy(own_ref.at[0], k_ref.at[index], sems.at[index]).wait()

    c_ref[...] = jnp.zeros_like(c_ref)
    d_ref[...] = jnp.zeros_like(d_ref)
    ec_ref[...] = jnp.zeros_like(ec_ref)

    def upto(l):
        return 2 * hd * ((l + 1) // 2)

    def across_row(l, start, stop):
        rows_l = pl.ds(base + l * hd, hd)
        return jnp.concatenate(
            [k_ref[index, rows_l, :] for index in range(start // (2 * hd), stop // (2 * hd))],
            axis=1,
        )

    last = width // (2 * hd) - 1
    arrive(last)
    folded = k_ref[last, tokens : 2 * tokens, :].astype(jnp.float32)[:, hd:]
    square = jnp.sum(folded, axis=1, keepdims=True)
    for l in range(layers):
        pair = l // 2
        if l % 2 == 0 and pair < last:
            arrive(pair)
        a = half(k_ref[pair, :tokens, :], l).astype(jnp.float32)
        if l:
            w = upto(l)
            known = c_ref[:, :w]
            top = min(w, width - hd)
            a = a + half(mm(known[:, :top], k_ref[pair, base : base + top, :]), l)
        inverse = lax.rsqrt(jnp.maximum(square, 0.0) / features + norm_eps)
        c = (inverse * a).astype(jnp.bfloat16)
        c_ref[:, l * hd : (l + 1) * hd] = c
        a_ref[l] = a
        inv_ref[l] = inverse
        if l == layers - 1:
            break
        b = half(k_ref[pair, tokens : 2 * tokens, :], l).astype(jnp.float32)
        if l:
            b = b + mm_nt(known, across_row(l, 0, w))
        wide = c.astype(jnp.float32)
        after = b + half(mm(c, k_ref[pair, pl.ds(base + l * hd, hd), :]), l)
        square = square + jnp.sum(wide * (b + after), axis=1, keepdims=True)
        bp_ref[l] = after

    below = layer_mask(block, block, hd, lambda r, c: r > c)
    upto_diag = layer_mask(block, block, hd, lambda r, c: r >= c)
    group = block // hd
    diagonal = lax.broadcasted_iota(jnp.int32, (group * rank, block), 0) // rank == (
        lax.broadcasted_iota(jnp.int32, (group * rank, block), 1) // hd
    )

    def side_by_side(parts):
        return parts[0] if len(parts) == 1 else jnp.concatenate(parts, axis=1)

    def spread_diagonal(parts):
        tall = jnp.concatenate(parts, axis=0)
        return jnp.where(diagonal, side_by_side([tall] * group), jnp.zeros((), jnp.bfloat16))

    def weight_gradients(start):
        stop = start + block
        mine = pl.ds(start, block)
        c_t = c_ref[:, mine].T
        d_t = d_ref[:, mine].T
        ec_t = ec_ref[:, mine].T

        m = [jnp.where(below, mm(d_t, c_ref[:, mine]), 0.0).astype(jnp.bfloat16)]
        if start:
            m = [mm(d_t, c_ref[:, :start]).astype(jnp.bfloat16)] + m
        yield
        y = mm(d_t, xs_ref[:tokens, :]) + mm(side_by_side(m), u_ref[:stop, :])
        yield
        m = [jnp.where(upto_diag, 0.0, mm(c_t, d_ref[:, mine])).astype(jnp.bfloat16)]
        if stop < width:
            m = m + [mm(c_t, d_ref[:, stop:]).astype(jnp.bfloat16)]
        yield
        z = mm(side_by_side([-ec_t, c_t]), xs_ref[...]) + mm(side_by_side(m), v_ref[start:, :])
        yield
        m = [
            jnp.where(upto_diag, mm(ec_t, c_ref[:, mine]), mm(c_t, ec_ref[:, mine])).astype(
                jnp.bfloat16
            )
        ]
        if start:
            m = [mm(ec_t, c_ref[:, :start]).astype(jnp.bfloat16)] + m
        if stop < width:
            m = m + [mm(c_t, ec_ref[:, stop:]).astype(jnp.bfloat16)]
        yield
        z = z - mm(side_by_side(m), u_ref[...])
        yield
        y = y.astype(jnp.bfloat16)
        z = z.astype(jnp.bfloat16)
        places = [turned_index(l, layers) for l in range(start // hd, stop // hd)]
        smalls = [q_ref[at, :, 2 * cols : 2 * cols + 2 * hd] for at in places]
        up = adapter_scale * mm(spread_diagonal([small[:, :hd] for small in smalls]), y)
        down = adapter_scale * mm(spread_diagonal([small[:, hd:] for small in smalls]), z)
        tail_y = mm_nt(jnp.concatenate([q_ref[at, :, :cols] for at in places], axis=0), y)
        tail_z = mm_nt(jnp.concatenate([q_ref[at, :, cols : 2 * cols] for at in places], axis=0), z)
        for j, at in enumerate(places):
            rows_j = slice(j * rank, (j + 1) * rank)
            out_ref[at, :, :cols] = up[rows_j].astype(jnp.bfloat16)
            out_ref[at, :, cols : 2 * cols] = down[rows_j].astype(jnp.bfloat16)
            tail = jnp.concatenate(
                [tail_y[rows_j, j * hd : (j + 1) * hd], tail_z[rows_j, j * hd : (j + 1) * hd]],
                axis=1,
            )
            out_ref[at, :, 2 * cols :] = (adapter_scale * tail).astype(jnp.bfloat16)

    pull = jnp.zeros((tokens, 1), jnp.float32)
    pending = iter(())
    for l in range(layers - 1, -1, -1):
        pair = l // 2
        p = half(k_ref[pair, 2 * tokens : 3 * tokens, :], l).astype(jnp.float32)
        if l < layers - 1:
            w = upto(l)
            top = width - hd
            p = p - pull * bp_ref[l]
            p = p + mm_nt(d_ref[:, w:], across_row(l, w, width))
            if w < top:
                p = p - half(mm(ec_ref[:, w:top], k_ref[pair, base + w : base + top, :]), l)
        next(pending, None)
        inverse = inv_ref[l]
        d_ref[:, l * hd : (l + 1) * hd] = (inverse * p).astype(jnp.bfloat16)
        c = c_ref[:, l * hd : (l + 1) * hd].astype(jnp.float32)
        ec_ref[:, l * hd : (l + 1) * hd] = (pull * c).astype(jnp.bfloat16)
        correction = jnp.sum(p * a_ref[l], axis=1, keepdims=True) / features
        pull = pull + inverse * inverse * inverse * correction
        next(pending, None)
        if l * hd % block == 0:
            for _ in pending:
                pass
            pending = weight_gradients(l * hd)
    for _ in pending:
        pass


def params(limit=vmem_bytes):
    return pltpu.CompilerParams(vmem_limit_bytes=limit)


def in_vmem(count):
    return [pl.BlockSpec(memory_space=pltpu.VMEM)] * count


def in_smem(count):
    return [pl.BlockSpec(memory_space=pltpu.SMEM)] * count


def pack(sizes, side, members, here, arrays):
    layers, hd, rank, tokens, cols = sizes
    line = jax.ShapeDtypeStruct((layers // side, hd, cols), jnp.bfloat16)
    stored = jax.ShapeDtypeStruct((members, rank, 2 * cols + 2 * hd), jnp.bfloat16)
    return pl.pallas_call(
        functools.partial(pack_kernel, sizes),
        out_shape=(stored,) + (line,) * side,
        in_specs=in_smem(1) + in_vmem(len(arrays)),
        out_specs=tuple(in_vmem(1 + side)),
        compiler_params=params(whole_vmem_bytes),
    )(here, *arrays)


def pick_rows(scalars, parts, lines):
    side = len(lines)
    across = lines[0].shape[0]
    turned = jax.ShapeDtypeStruct((side,) + lines[0].shape[1:], jnp.bfloat16)
    return pl.pallas_call(
        functools.partial(pick_kernel, side, across),
        out_shape=(jax.ShapeDtypeStruct(parts.shape, parts.dtype),) + (turned,) * across,
        in_specs=in_smem(len(scalars))
        + in_vmem(1)
        + [pl.BlockSpec(memory_space=pl.ANY)]
        + in_vmem(side - 1),
        out_specs=tuple(in_vmem(1 + across)),
        scratch_shapes=[pltpu.SemaphoreType.DMA((across,))],
        compiler_params=params(),
    )(*scalars, parts, *lines)


def join(sizes, scalars, parts, arrays, after):
    layers, hd, rank, tokens, cols = sizes
    return pl.pallas_call(
        functools.partial(join_kernel, sizes),
        out_shape=jax.ShapeDtypeStruct(parts.shape[:2] + (3 * cols + 2 * hd,), jnp.bfloat16),
        in_specs=in_smem(len(scalars))
        + in_vmem(1 + len(arrays))
        + [pl.BlockSpec(memory_space=pl.ANY)] * len(after),
        out_specs=in_vmem(1)[0],
        compiler_params=params(),
    )(*scalars, parts, *arrays, *after)


def finish(sizes, owned, gain):
    layers, hd, rank, tokens, cols = sizes
    wide = jax.ShapeDtypeStruct((rank, layers * cols), jnp.bfloat16)
    narrow = jax.ShapeDtypeStruct((rank, hd), jnp.bfloat16)
    return pl.pallas_call(
        functools.partial(finish_kernel, sizes),
        out_shape=(wide, narrow, narrow, wide),
        in_specs=in_vmem(2),
        out_specs=tuple(in_vmem(4)),
        compiler_params=params(),
    )(owned, gain)


def merge(sizes, side, here, own, other):
    layers, hd, rank, tokens, cols = sizes
    return pl.pallas_call(
        functools.partial(merge_kernel, sizes, side, len(own)),
        out_shape=jax.ShapeDtypeStruct((2, layers * hd, cols), jnp.bfloat16),
        in_specs=in_smem(1) + in_vmem(len(own) + len(other)),
        out_specs=in_vmem(1)[0],
        compiler_params=params(),
        cost_estimate=pl.CostEstimate(
            flops=0, bytes_accessed=merge_cost_bytes, transcendentals=0
        ),
    )(here, *own, *other)


def gram(sizes, here, both, q):
    layers, hd, rank, tokens, cols = sizes
    width = layers * hd
    share = jax.ShapeDtypeStruct(
        (width // (4 * hd), 3 * tokens + width - hd, 2 * hd), jnp.bfloat16
    )
    table = jax.ShapeDtypeStruct((width, cols), jnp.bfloat16)
    return pl.pallas_call(
        functools.partial(gram_kernel, sizes),
        out_shape=(
            table,
            table,
            jax.ShapeDtypeStruct((2 * tokens, cols), jnp.bfloat16),
            share,
        ),
        in_specs=in_smem(1) + [pl.BlockSpec(memory_space=pl.ANY)] + in_vmem(1),
        out_specs=tuple(in_vmem(4)),
        scratch_shapes=[
            pltpu.VMEM((tokens, cols), jnp.float32),
            pltpu.VMEM((tokens, cols), jnp.float32),
            pltpu.SemaphoreType.DMA((2,)),
        ],
        compiler_params=params(),
    )(here, both, q)


def keep(sizes, here, u, v, xs, shape):
    return pl.pallas_call(
        functools.partial(keep_kernel, sizes),
        out_shape=jax.ShapeDtypeStruct(shape, jnp.bfloat16),
        in_specs=in_smem(1) + in_vmem(3),
        out_specs=in_vmem(1)[0],
        compiler_params=params(),
        cost_estimate=pl.CostEstimate(flops=1 << 31, bytes_accessed=1 << 22, transcendentals=0),
    )(here, u, v, xs)


def solve(sizes, features, here, own, other, xs, u, v, q):
    layers, hd, rank, tokens, cols = sizes
    width = layers * hd
    return pl.pallas_call(
        functools.partial(solve_kernel, sizes, features),
        out_shape=jax.ShapeDtypeStruct(q.shape[:2] + (2 * cols + 2 * hd,), jnp.bfloat16),
        in_specs=in_smem(1) + [pl.BlockSpec(memory_space=pl.ANY)] * 2 + in_vmem(4),
        out_specs=in_vmem(1)[0],
        scratch_shapes=[
            pltpu.VMEM((tokens, width), jnp.bfloat16),
            pltpu.VMEM((tokens, width), jnp.bfloat16),
            pltpu.VMEM((tokens, width), jnp.bfloat16),
            pltpu.VMEM((layers, tokens, hd), jnp.float32),
            pltpu.VMEM((layers, tokens, hd), jnp.float32),
            pltpu.VMEM((layers, tokens, 1), jnp.float32),
            pltpu.VMEM((2 * own.shape[0],) + own.shape[1:], jnp.bfloat16),
            pltpu.SemaphoreType.DMA((2 * own.shape[0],)),
        ],
        compiler_params=params(solve_vmem_bytes),
    )(here, own, other, xs, u, v, q)


def swap(value, axis):
    return lax.all_to_all(value, axis, split_axis=0, concat_axis=0, tiled=True)


def pick(chooser, parts):
    flat = parts.reshape(parts.shape[0], -1)
    return mm(chooser, flat).astype(jnp.bfloat16).reshape((chooser.shape[0],) + parts.shape[1:])


def body(
    inputs,
    cotangent,
    norm_gain,
    w_value,
    w_out,
    value_down,
    value_up_factor,
    out_down,
    output_up_factor,
    block_tenant,
    valid_tokens,
    tenant_slot,
):
    sections, members = lax.axis_size(pipe), lax.axis_size(dp)
    rows, features = inputs.shape[1], inputs.shape[2]
    hd, rank = w_value.shape[1], value_down.shape[2]
    cols = features // sections
    tokens = rows * sections
    sizes = (sections, hd, rank, tokens, cols)
    side = lax.axis_size("a") * lax.axis_size("b")
    across = lax.axis_size("x")
    planes = lax.axis_size("z")
    here = lax.axis_index(pipe + dp).astype(jnp.int32)[None]
    gain = norm_gain
    both_cores = [(0, 1), (1, 0)]

    stored, *lines = pack(
        sizes,
        side,
        members,
        here,
        (
            w_value[0],
            w_out[0],
            gain,
            value_down[0, 0],
            output_up_factor[0, 0],
            value_up_factor[0, 0],
            out_down[0, 0],
        ),
    )
    lines = [lines[0]] + [
        lax.ppermute(lines[step], ("a", "b"), [(i, (i + step) % side) for i in range(side)])
        for step in range(1, side)
    ]
    adapters, *turned = pick_rows((here, block_tenant, tenant_slot), swap(stored, dp), lines)
    turned = [turned[0]] + [
        lax.ppermute(turned[step], "x", [(i, (i + step) % across) for i in range(across)])
        for step in range(1, across)
    ]
    joined = join(
        sizes,
        (here, block_tenant, valid_tokens),
        swap(adapters, "z"),
        (
            inputs[0],
            cotangent[0],
            lax.ppermute(inputs[0], "core", both_cores),
            lax.ppermute(cotangent[0], "core", both_cores),
        ),
        turned[1:],
    )
    adapters = swap(joined, ("b", "x", "a"))
    pairs = across // 2
    other = [
        lax.ppermute(
            jnp.concatenate(turned[at : at + pairs], axis=0),
            "z",
            [(i, (i + turn) % planes) for i in range(planes)],
        )
        for at, turn in ((0, 1), (pairs, -1))
    ]

    u, v, rows_xs, given = gram(
        sizes, here, merge(sizes, side, here, turned, other), adapters
    )
    theirs = lax.ppermute(given, "core", both_cores)
    kept = keep(sizes, here, u, v, rows_xs, given.shape)
    summed = (kept.astype(jnp.float32) + theirs.astype(jnp.float32)).astype(jnp.bfloat16)
    shares = swap(summed.reshape(sections // 2, -1, summed.shape[-1]), ("b", "x"))
    share = jnp.sum(shares.astype(jnp.float32), axis=0).astype(jnp.bfloat16)
    own = swap(jnp.broadcast_to(share[None], shares.shape), ("b", "x")).reshape(summed.shape)
    other = lax.ppermute(own, "core", both_cores)

    grads = solve(sizes, features, here, own, other, rows_xs, u, v, adapters)

    ids = jnp.arange(members, dtype=jnp.int32)
    tenant_hot = block_tenant[:, None] == ids[None, :]
    slot_of = jnp.sum(jnp.where(tenant_hot, tenant_slot[None, :], 0), axis=1)
    slot_hot = (ids[:, None] == slot_of[None, :]).astype(jnp.bfloat16)
    by_member = swap(swap(grads, ("b", "x", "a")), "z")
    owned = swap(pick(slot_hot, by_member), dp)
    return tuple(part[None, None] for part in finish(sizes, owned, gain))


def solution(mesh):
    sections, members = mesh.devices.shape
    finer = jax.sharding.Mesh(
        mesh.devices.reshape(2, 2, sections // 4, members // 2, 2), pipe + dp
    )
    return jax.shard_map(
        body,
        mesh=finer,
        in_specs=(
            P(pipe, dp, None),
            P(pipe, dp, None),
            P(pipe, None),
            P(pipe, None, None),
            P(pipe, None, None),
            P(pipe, dp, None, None),
            P(pipe, dp, None, None),
            P(pipe, dp, None, None),
            P(pipe, dp, None, None),
            P(),
            P(),
            P(),
        ),
        out_specs=(
            P(pipe, dp, None, None),
            P(pipe, dp, None, None),
            P(pipe, dp, None, None),
            P(pipe, dp, None, None),
        ),
        check_vma=False,
    )
```
